32 devices in a mesh: dp: 8 (over z, core), fsdp: 4 (over y, x).
Axes of the slice: x: 2, y: 2, z: 4, core: 2. Of those that a mesh axis runs over, the one named last changes fastest.
Arguments:
- hidden_in: bfloat16 [256, 2304], P(('dp', 'fsdp')), may hold values from -30 to 30
- cache_pool: bfloat16 [1152, 16, 2, 2048], P('dp', None, None, 'fsdp'), may hold values from -64 to 64
- project_in: bfloat16 [2304, 3, 2048], P('dp', None, 'fsdp'), may hold values from -0.125 to 0.125
- project_out: bfloat16 [2048, 2304], P('fsdp', 'dp'), may hold values from -0.125 to 0.125
- norm_first: bfloat16 [2304], replicated, may hold values from 0.099609375 to 1.8984375
- norm_second: bfloat16 [2304], replicated, may hold values from 0.099609375 to 1.8984375
- router: bfloat16 [2304, 8], replicated, may hold values from -0.125 to 0.125
- gate_up: bfloat16 [8, 2304, 2, 5760], P(None, 'dp', None, 'fsdp'), may hold values from -0.125 to 0.125
- expert_down: bfloat16 [8, 2304, 5760], P(None, 'dp', 'fsdp'), may hold values from -0.078125 to 0.078125
- lengths: int32 [256], replicated, may hold values from 65 to 128, as said below
- prompt_pages: int32 [32, 4], P('dp'), may hold values from 0 to 143, as said below
- own_pages: int32 [256, 4], P('dp'), may hold values from 0 to 143, as said below
- groups: int32 [256], P('dp'), may hold values from 0 to 3
- move_target: int32 [8, 4], replicated, may hold values from 0 to 7, as said below
- routes: int32 [256, 2], P(('dp', 'fsdp')), may hold values from 0 to 7, all different within a row; in each aligned block of 8 rows (0 to 7, 8 to 15, ...) at most 4 rows name the same one
Outputs:
- layer_out: bfloat16 [256, 2304], P(('dp', 'fsdp'))
The draws below stay inside these ranges and needn't reach their ends.
Inputs may be any that keep to these rules, and one draw needn't show every extreme that they name: `lengths`: every request's cache holds its shared prompt's 4 * 16 positions and at least one more; some request holds 128. `prompt_pages`: within a row, the prompt pages of all its shared prompts and the own pages of all its requests are distinct pages. `own_pages`: within a row, the prompt pages of all its shared prompts and the own pages of all its requests are distinct pages. Row s sends its request slots 32 - 4 + j, j < 4, to rows move_target[s, j]; a row's 4 destinations are distinct and differ from s, and for each j every row is the destination of exactly one row. `routes`: in the 8 rows of one device no expert is named more than 4 times.
All inputs are finite; a program needn't handle non-finite values.
Results may differ from the reference program's by a relative error of at most 0.009.
Values may be sent and summed in bfloat16 or wider, within the bound.
No kernel may reach another device: no remote copies, remote signals or barrier semaphores. Data moves between devices by JAX's collectives and lax.ppermute only.
A program may use at most 128 MiB of HBM per device.

```python
import math
import jax
import jax.numpy as jnp
import numpy as np
from jax import lax

D = 2304
HEADS = 32
HD = 64
FF = 5760
EXPERTS = 8
PAGE = 16
PREF = 4
OWNP = 4
GROUPS_ROW = 4
REQ_DEV = 8
CAP = 4
ROWS = 8
MIG = 4
REQ_ROW = 32
REQS = 256
POOL = 144
LMAX = 128


def pool_layout(key):

    def one_row(row_key):
        shuffled = jax.random.permutation(row_key, POOL).astype(jnp.int32)
        prompt_part = shuffled[:GROUPS_ROW * PREF].reshape(GROUPS_ROW, PREF)
        own_part = shuffled[GROUPS_ROW * PREF:].reshape(REQ_ROW, OWNP)
        return (prompt_part, own_part)
    row_keys = jax.random.split(jax.random.fold_in(key, 11), ROWS)
    prompt_part, own_part = jax.vmap(one_row)(row_keys)
    return (prompt_part.reshape(ROWS * GROUPS_ROW, PREF), own_part.reshape(REQS, OWNP))


def draw_prompt_pages(key, part):
    return pool_layout(key)[0]


def draw_own_pages(key, part):
    return pool_layout(key)[1]


def draw_lengths(key, part):
    span_own = OWNP * PAGE
    first_draw = jax.random.randint(jax.random.fold_in(key, 1), (REQS,), 0, span_own)
    second_draw = jax.random.randint(jax.random.fold_in(key, 2), (REQS,), 0, span_own)
    extra = first_draw * second_draw // max(span_own - 1, 1)
    longest = jax.random.randint(jax.random.fold_in(key, 3), (), 0, REQS)
    result = jnp.where(jnp.arange(REQS) == longest, LMAX, PREF * PAGE + 1 + extra)
    return result.astype(jnp.int32)


def draw_move_target(key, part):
    shuffled = jax.random.permutation(jax.random.fold_in(key, 5), ROWS).astype(jnp.int32)
    offsets = jax.random.permutation(jax.random.fold_in(key, 6), ROWS - 1)[:MIG].astype(jnp.int32) + 1
    places = jnp.arange(ROWS, dtype=jnp.int32)
    targets = shuffled[(places[:, None] + offsets[None, :]) % ROWS]
    return jnp.zeros((ROWS, MIG), jnp.int32).at[shuffled].set(targets)


def draw_hidden_in(key, part):
    row_scale = jnp.exp(jax.random.uniform(jax.random.fold_in(key, 1), (REQS, 1), jnp.float32, jnp.log(0.5), jnp.log(2.0)))
    column_scale = jnp.exp(jax.random.uniform(jax.random.fold_in(key, 2), (1, D), jnp.float32, jnp.log(0.3), jnp.log(3.0)))
    base_values = jnp.clip(jax.random.normal(jax.random.fold_in(key, 3), (REQS, D), jnp.float32), -4.0, 4.0)
    return (base_values * row_scale * column_scale).astype(jnp.bfloat16)


def draw_cache_pool(key, part):
    pages_all = POOL * ROWS
    shape = (pages_all, PAGE, 2, HEADS * HD)
    result = jnp.clip(jax.random.normal(jax.random.fold_in(key, 6), shape, jnp.float32), -6.0, 6.0)
    return result.astype(jnp.bfloat16)


def place_ends(values, key, low, largest):
    longest = values.shape.index(max(values.shape))
    spots = []
    for shift in (0, 1):
        where = [jax.random.randint(jax.random.fold_in(key, axis), (), 0, length) for axis, length in enumerate(values.shape)]
        where[longest] = (where[longest] + shift) % values.shape[longest]
        spots.append(tuple(where))
    return values.at[spots[0]].set(low).at[spots[1]].set(largest)


def steps_of(rng, shape, cuts, smallest, top_value):
    def one(dim, blocks):
        heights = jax.random.uniform(jax.random.fold_in(jax.random.fold_in(rng, 6), dim), (blocks,), jnp.float32, smallest / len(cuts), top_value / len(cuts))
        return jnp.repeat(jnp.exp(heights), shape[dim] // blocks).reshape((-1,) + (1,) * (len(shape) - dim - 1))

    factor_of = one(*cuts[0])
    for cut in cuts[1:]:
        factor_of = factor_of * one(*cut)
    return factor_of


def assign_block(rng, own, number, rows, count, top, reach, skew):
    ranking = jax.random.permutation(rng, count)
    crowded, ordinary = shares(count, rows * top, reach, skew, True), shares(count, rows * top, reach, skew, False)
    places = jnp.arange(count)

    def named(sizes, rotation):
        used = int((sizes > 0).sum())
        fixed = max(1, used // 4)
        moved = fixed + (places - fixed + rotation * (used - fixed)) % max(1, count - fixed)
        return jnp.zeros((count,), jnp.int32).at[ranking[jnp.where(places < fixed, places, moved)]].set(jnp.asarray(sizes, jnp.int32))

    sizes = jnp.where(number % 4 == 0, named(crowded, number // 4), named(ordinary, number - number // 4 - 1))
    mixed = jax.random.permutation(jax.random.fold_in(own, 3), count)
    source_of, sink = mixed[0:count // 2 * 2:2], mixed[1:count // 2 * 2:2]
    room = jnp.minimum(sizes[source_of] - 1, reach - sizes[sink]) // 2
    room = jnp.where((source_of == ranking[0]) | (sink == ranking[0]) | (sizes[sink] == 0), 0, jnp.maximum(room, 0))
    moved = jax.random.randint(jax.random.fold_in(own, 4), (count // 2,), 0, 1 << 20) % (room + 1)
    sizes = sizes.at[source_of].add(-moved).at[sink].add(moved)
    items = jnp.searchsorted(jnp.cumsum(sizes), jnp.arange(rows * top), side="right").astype(jnp.int32)
    grid = items.reshape(top, rows).T
    grid = grid[jax.random.permutation(jax.random.fold_in(own, 1), rows)]
    rotation = jax.random.randint(jax.random.fold_in(own, 2), (rows, 1), 0, top)
    return jnp.take_along_axis(grid, (jnp.arange(top)[None, :] + rotation) % top, axis=1)


def shares(count, total, limit, skew, full):
    loads = [(1 << 20) // math.isqrt(standing ** skew) + 1 for standing in range(1, count + 1)]
    largest = limit if full else min(limit, max(-(-total // count), total * loads[0] // sum(loads)))
    least = 1 if total - largest >= count - 1 else 0
    holding, rest = [largest] + [least] * (count - 1), total - largest - least * (count - 1)
    while rest > 0:
        free = [i for i in range(1, count) if holding[i] < largest] or [i for i in range(1, count) if holding[i] < limit]
        whole, remaining = sum([loads[i] for i in free]), rest
        for i in free:
            addition = min(limit - holding[i], max(1, remaining * loads[i] // whole), rest)
            holding[i] = holding[i] + addition
            rest = rest - addition
    return np.array(holding)


def gaussian(rng, extent, spread, limit, pieces=(), kind=jnp.bfloat16):
    entries = jax.random.normal(rng, extent, jnp.float32) * spread
    if len(pieces) > 0:
        entries = steps_of(rng, extent, pieces, -0.22, 0.18) * entries
    return jnp.clip(entries, min=-limit, max=limit).astype(kind)


def setup_inputs(seed: int = 0) -> dict:
    key_list = jax.random.split(jax.random.key(seed), 16)
    hidden_in = draw_hidden_in(jax.random.fold_in(key_list[15], 71), 0)
    cache_pool = draw_cache_pool(jax.random.fold_in(key_list[15], 71), 0)
    project_in = gaussian(key_list[2], (D, 3, HEADS * HD), D ** -0.5, 0.125, ((0, 8), (2, 4)))
    project_out = gaussian(key_list[3], (HEADS * HD, D), (HEADS * HD) ** -0.5, 0.125, ((0, 4), (1, 8)))
    norm_first = jnp.clip(1.0 + 0.18 * jax.random.normal(key_list[4], (D,), jnp.float32), 0.099609375, 1.8984375).astype(jnp.bfloat16)
    norm_second = jnp.clip(1.0 + 0.18 * jax.random.normal(key_list[5], (D,), jnp.float32), 0.099609375, 1.8984375).astype(jnp.bfloat16)
    router = gaussian(key_list[6], (D, EXPERTS), D ** -0.5, 0.125)
    gate_up = gaussian(key_list[7], (EXPERTS, D, 2, FF), D ** -0.5, 0.125, ((1, 8), (3, 4)))
    expert_down = gaussian(key_list[8], (EXPERTS, D, FF), FF ** -0.5, 0.078125, ((1, 8), (2, 4)))
    lengths = draw_lengths(jax.random.fold_in(key_list[15], 71), 0)
    prompt_pages = draw_prompt_pages(jax.random.fold_in(key_list[15], 71), 0)
    own_pages = draw_own_pages(jax.random.fold_in(key_list[15], 71), 0)
    groups = place_ends(jax.random.randint(key_list[12], (REQS,), 0, GROUPS_ROW), jax.random.fold_in(key_list[12], 1), 0, GROUPS_ROW - 1).astype(jnp.int32)
    move_target = draw_move_target(jax.random.fold_in(key_list[15], 71), 0)
    routes_keys = jax.random.split(jax.random.fold_in(key_list[14], 1), REQS // REQ_DEV)
    routes_turns = jax.random.permutation(jax.random.fold_in(key_list[14], 3), REQS // REQ_DEV)
    routes = jax.vmap(lambda own, number: assign_block(jax.random.fold_in(key_list[14], 2), own, number, REQ_DEV, EXPERTS, 2, CAP, 1))(routes_keys, routes_turns).reshape((REQS, 2))
    return {"hidden_in": hidden_in, "cache_pool": cache_pool, "project_in": project_in, "project_out": project_out, "norm_first": norm_first, "norm_second": norm_second, "router": router, "gate_up": gate_up, "expert_down": expert_down, "lengths": lengths, "prompt_pages": prompt_pages, "own_pages": own_pages, "groups": groups, "move_target": move_target, "routes": routes}


def rms_scale(values, scaling):
    return values * lax.rsqrt(lax.optimization_barrier(jnp.mean(values * values, axis=-1, keepdims=True)) + 1e-06) * scaling.astype(jnp.float32)

def rotate(tensor, position):
    half_dim = tensor.shape[-1] // 2
    channel = jnp.arange(half_dim, dtype=jnp.float32)
    inverse = jnp.exp(-jnp.log(10000.0) * 2.0 * channel / tensor.shape[-1])
    angles = position.astype(jnp.float32)[:, None, None] * inverse
    cosine = jnp.cos(angles)
    sine_part = jnp.sin(angles)
    first_half = tensor[..., :half_dim]
    second_half = tensor[..., half_dim:]
    return jnp.concatenate([first_half * cosine - second_half * sine_part, second_half * cosine + first_half * sine_part], axis=-1)

def attend_row(query, key_new, value_new, position, page_list, cache_pool):
    count_rows = query.shape[0]
    gathered = cache_pool[page_list].astype(jnp.float32)
    gathered = gathered.reshape(count_rows, page_list.shape[1] * PAGE, 2, HEADS, HD)
    key_rows = gathered[:, :, 0]
    value_rows = gathered[:, :, 1]
    scale_factor = HD ** (-0.5)
    query_wide = query.astype(jnp.float32)
    scores = jnp.einsum('nhd,nlhd->nhl', query_wide, key_rows, precision=lax.Precision.HIGHEST) * scale_factor
    valid_mask = jnp.arange(key_rows.shape[1], dtype=jnp.int32)[None, :] < position[:, None]
    scores = jnp.where(valid_mask[:, None, :], scores, -jnp.inf)
    own_score = lax.optimization_barrier(jnp.sum(query_wide * key_new.astype(jnp.float32), axis=-1)) * scale_factor
    highest = jnp.maximum(lax.optimization_barrier(jnp.max(scores, axis=-1)), own_score)
    weights_cache = jnp.exp(scores - highest[..., None])
    weight_own = jnp.exp(own_score - highest)
    denominator = lax.optimization_barrier(jnp.sum(weights_cache, axis=-1)) + weight_own
    probs_cache = (weights_cache / denominator[..., None]).astype(jnp.bfloat16)
    prob_own = (weight_own / denominator).astype(jnp.bfloat16)
    mixture = jnp.einsum('nhl,nlhd->nhd', probs_cache.astype(jnp.float32), value_rows, precision=lax.Precision.HIGHEST)
    mixture = mixture + prob_own.astype(jnp.float32)[..., None] * value_new.astype(jnp.float32)
    return mixture.astype(jnp.bfloat16).reshape(count_rows, HEADS * HD)

def reference(hidden_in, cache_pool, project_in, project_out, norm_first, norm_second, router, gate_up, expert_down, lengths, prompt_pages, own_pages, groups, move_target, routes):
    row_ids = jnp.arange(ROWS, dtype=jnp.int32)
    matched = (move_target[:, None, :] == row_ids[None, :, None]).astype(jnp.int32)
    source_row = lax.optimization_barrier(jnp.sum(matched * row_ids[:, None, None], axis=0))
    staying = REQ_ROW - MIG
    resident = row_ids[:, None] * REQ_ROW + jnp.arange(staying, dtype=jnp.int32)[None, :]
    arrived = source_row * REQ_ROW + staying + jnp.arange(MIG, dtype=jnp.int32)[None, :]
    anchor = jnp.concatenate([resident, arrived], axis=1).reshape(REQS).astype(jnp.int32)
    old_row = jnp.arange(REQS, dtype=jnp.int32) // REQ_ROW
    prompt_list = prompt_pages[(old_row * GROUPS_ROW + groups).astype(jnp.int32)]
    page_list = jnp.concatenate([prompt_list, own_pages], axis=1) + (old_row * POOL)[:, None]
    position = lengths[anchor]
    moved = hidden_in[anchor]
    normed_attn = rms_scale(moved.astype(jnp.float32), norm_first).astype(jnp.bfloat16)
    projected = jnp.dot(normed_attn, project_in.reshape(D, 3 * HEADS * HD), preferred_element_type=jnp.float32)
    projected = projected.reshape(REQS, 3, HEADS, HD)
    query = rotate(projected[:, 0], position).astype(jnp.bfloat16)
    key_new = rotate(projected[:, 1], position).astype(jnp.bfloat16)
    value_new = projected[:, 2].astype(jnp.bfloat16)
    pages_moved = page_list[anchor]

    def blocked(array):
        return array.reshape((ROWS, REQ_ROW) + array.shape[1:])

    def one_row(item):
        return attend_row(item[0], item[1], item[2], item[3], item[4], cache_pool)
    heads_out = lax.map(one_row, (blocked(query), blocked(key_new), blocked(value_new), blocked(position), blocked(pages_moved)))
    heads_out = heads_out.reshape(REQS, HEADS * HD)
    resid = moved.astype(jnp.float32) + jnp.dot(heads_out, project_out, preferred_element_type=jnp.float32)
    moe_in = rms_scale(resid, norm_second).astype(jnp.bfloat16)
    logits = jnp.dot(moe_in, router, preferred_element_type=jnp.float32)
    chosen = jnp.take_along_axis(logits, routes, axis=1)
    route_weights = jnp.stack([jax.nn.sigmoid(chosen[:, 0] - chosen[:, 1]), jax.nn.sigmoid(chosen[:, 1] - chosen[:, 0])], axis=1)
    down_whole = jnp.transpose(expert_down, (0, 2, 1))
    capacity_all = REQS // REQ_DEV * CAP
    request_ids = jnp.arange(REQS, dtype=jnp.int32)

    def one_expert(item):
        expert, gate_expert, down_expert = item
        matches = routes == expert
        used_rows = jnp.any(matches, axis=1)
        weight_rows = lax.optimization_barrier(jnp.sum(jnp.where(matches, route_weights, 0.0), axis=1))
        ordering = jnp.argsort(jnp.where(used_rows, request_ids, REQS + request_ids))[:capacity_all].astype(jnp.int32)
        rows_in = moe_in[ordering]
        gate_part = jnp.dot(rows_in, gate_expert[:, 0], preferred_element_type=jnp.float32)
        up_part = jnp.dot(rows_in, gate_expert[:, 1], preferred_element_type=jnp.float32)
        activation = (jax.nn.silu(gate_part) * up_part).astype(jnp.bfloat16)
        expert_y = jnp.dot(activation, down_expert, preferred_element_type=jnp.float32)
        factor = weight_rows[ordering] * used_rows[ordering].astype(jnp.float32)
        return (ordering, expert_y * factor[:, None])
    orderings, contributions = lax.map(one_expert, (jnp.arange(EXPERTS, dtype=jnp.int32), gate_up, down_whole))
    moe_total = jnp.zeros((REQS, D), jnp.float32).at[orderings.reshape(-1)].add(contributions.reshape(-1, D))
    return (resid + moe_total).astype(jnp.bfloat16)
```

```python
import functools

import jax
import jax.numpy as jnp
from jax import lax
from jax.experimental import pallas as pl
from jax.experimental.pallas import tpu as pltpu
from jax.sharding import PartitionSpec as P

HD = 64
CAP = 4
PIECES = 3
LANES = 128
BF16 = jnp.bfloat16
F32 = jnp.float32
FAR = -3.0e38


def params(mib=40):
    return pltpu.CompilerParams(vmem_limit_bytes=mib * 2**20)


def dot_nn(a, b):
    return lax.dot_general(a, b, (((1,), (0,)), ((), ())), preferred_element_type=F32)


def dot_nt(a, b):
    return lax.dot_general(a, b, (((1,), (1,)), ((), ())), preferred_element_type=F32)


def split_bf16(value, count=PIECES):
    pieces = []
    for _ in range(count):
        piece = value.astype(BF16).astype(F32)
        pieces.append(piece)
        value = value - piece
    return pieces


def full_spec(shape):
    zeros = (0,) * len(shape)
    return pl.BlockSpec(tuple(shape), lambda *_: zeros)


def pool_kernel(pool_ref, key_ref, value_ref):
    pages, page_len, _, cols = pool_ref.shape
    rows = pages * page_len
    both = pool_ref[...].reshape(2 * rows, cols)
    wide = lax.broadcasted_iota(jnp.int32, (rows, 2 * rows), 1)
    high = lax.broadcasted_iota(jnp.int32, (rows, 2 * rows), 0)
    key_ref[...] = dot_nn((wide == 2 * high).astype(BF16), both).astype(BF16)
    value_ref[...] = dot_nn((wide == 2 * high + 1).astype(BF16), both).astype(BF16)


def split_pool(cache_pool):
    pages, page_len, _, cols = cache_pool.shape
    block = next(b for b in (16, 8, 4, 2, 1) if pages % b == 0)
    out = jax.ShapeDtypeStruct((pages * page_len, cols), BF16)
    spec = pl.BlockSpec((block * page_len, cols), lambda b: (b, 0))
    return pl.pallas_call(
        pool_kernel,
        grid=(pages // block,),
        in_specs=[pl.BlockSpec((block, page_len, 2, cols), lambda b: (b, 0, 0, 0))],
        out_specs=[spec, spec],
        out_shape=[out, out],
        compiler_params=params(),
        cost_estimate=pl.CostEstimate(
            flops=8 * block * page_len * cache_pool.size,
            bytes_accessed=4 * cache_pool.size,
            transcendentals=0,
        ),
        name="pool_split",
    )(cache_pool)


def qkv_kernel(order_ref, recv_ref, norm_ref, w_ref, keep_ref, send_ref, raw_ref, normed, slots):
    width = norm_ref.shape[1]
    half, row, _ = keep_ref.shape
    cols = w_ref.shape[2]
    values = recv_ref[:, :width]
    scale = recv_ref[:, width : width + 1].astype(F32)
    for piece in range(1, PIECES):
        scale = scale + recv_ref[:, width + piece : width + piece + 1].astype(F32)
    normed[...] = (values.astype(F32) * scale * norm_ref[...]).astype(BF16)
    for slot in range(2 * half):
        rows = pl.ds(pl.multiple_of(order_ref[slot] * row, row), row)
        slots[slot * row : (slot + 1) * row] = normed[rows]
        raw_ref[slot * row : (slot + 1) * row] = recv_ref[rows, :width]
    for part in range(3):
        here = slice(part * cols, (part + 1) * cols)
        result = dot_nn(slots[...], w_ref[part]).astype(BF16).reshape(2 * half, row, cols)
        keep_ref[:, :, here] = result[:half]
        send_ref[:, :, here] = result[half:]


def project_qkv(order, recv, norm_slice, weights, half, row):
    total, _ = recv.shape
    width, cols = weights.shape[1:]
    out = jax.ShapeDtypeStruct((half, row, 3 * cols), BF16)
    raw = jax.ShapeDtypeStruct((total, width), BF16)
    return pl.pallas_call(
        qkv_kernel,
        grid_spec=pltpu.PrefetchScalarGridSpec(
            num_scalar_prefetch=1,
            grid=(1,),
            in_specs=[full_spec(recv.shape), full_spec(norm_slice.shape), full_spec(weights.shape)],
            out_specs=[full_spec(out.shape), full_spec(out.shape), full_spec(raw.shape)],
            scratch_shapes=[pltpu.VMEM((total, width), BF16), pltpu.VMEM((total, width), BF16)],
        ),
        out_shape=[out, out, raw],
        compiler_params=params(),
        cost_estimate=pl.CostEstimate(
            flops=6 * total * width * cols, bytes_accessed=6 * total * cols + 6 * width * cols, transcendentals=0
        ),
        name="qkv",
    )(order, recv, norm_slice, weights)


def attention_kernel(*refs):
    parts, (cos_ref, sin_ref, bias_ref, key_ref, value_ref, out_ref, scores, probs) = refs[:-8], refs[-8:]
    row, cols = out_ref.shape
    heads = cols // HD
    total = parts[0][...].astype(F32)
    for part in parts[1:]:
        total = total + part[...].astype(F32)
    lane = lax.broadcasted_iota(jnp.int32, (row, cols), 1)
    first_half = lane % HD < HD // 2

    def rotate(values):
        partner = jnp.where(
            first_half, pltpu.roll(values, cols - HD // 2, 1), pltpu.roll(values, HD // 2, 1)
        )
        return (values * cos_ref[...] + partner * sin_ref[...]).astype(BF16)

    query = rotate(total[:, :cols]).astype(F32)
    key_new = rotate(total[:, cols : 2 * cols]).astype(F32)
    value_new = total[:, 2 * cols :].astype(BF16).astype(F32)
    spread = jnp.concatenate(
        [jnp.where(lane // HD == h, query, 0.0).astype(BF16) for h in range(heads)], axis=0
    )
    scores[...] = dot_nt(spread, key_ref[...])
    own_parts = []
    for h in range(heads):
        here = slice(h * row, (h + 1) * row)
        mine = lane // HD == h
        own = jnp.sum(jnp.where(mine, query * key_new, 0.0), axis=1, keepdims=True) * HD**-0.5
        score = scores[here] * HD**-0.5 + bias_ref[...]
        highest = jnp.maximum(jnp.max(score, axis=1, keepdims=True), own)
        weight = jnp.exp(score - highest)
        weight_own = jnp.exp(own - highest)
        inverse = 1.0 / (jnp.sum(weight, axis=1, keepdims=True) + weight_own)
        probs[here] = (weight * inverse).astype(BF16)
        own_parts.append((weight_own * inverse).astype(BF16).astype(F32))
    mixture = dot_nn(probs[...], value_ref[...])
    result = jnp.zeros((row, cols), F32)
    for h in range(heads):
        mixed = mixture[h * row : (h + 1) * row] + own_parts[h] * value_new
        result = jnp.where(lane // HD == h, mixed, result)
    out_ref[...] = result.astype(BF16)


def attend(parts, cosine, sine, bias, keys, values):
    row, cols = cosine.shape
    stretch = keys.shape[0]
    heads = cols // HD
    operands = [*parts, cosine, sine, bias, keys, values]
    return pl.pallas_call(
        attention_kernel,
        grid=(1,),
        in_specs=[full_spec(x.shape) for x in operands],
        out_specs=full_spec((row, cols)),
        out_shape=jax.ShapeDtypeStruct((row, cols), BF16),
        scratch_shapes=[
            pltpu.VMEM((heads * row, stretch), F32),
            pltpu.VMEM((heads * row, stretch), BF16),
        ],
        compiler_params=params(),
        cost_estimate=pl.CostEstimate(
            flops=4 * heads * row * stretch * cols,
            bytes_accessed=4 * stretch * cols,
            transcendentals=heads * row * stretch,
        ),
        name="attention",
    )(*operands)


def out_kernel(*refs):
    parts, (other_ref, w_ref, out_ref) = refs[:-3], refs[-3:]
    half = len(parts) * parts[0].shape[0]
    mine = jnp.concatenate([part[...] for part in parts], axis=0)
    out_ref[:, :half] = dot_nt(w_ref[...], mine).astype(BF16)
    out_ref[:, half:] = dot_nt(w_ref[...], other_ref[...]).astype(BF16)


def project_heads(parts, other, weights):
    half = other.shape[0]
    operands = [*parts, other, weights]
    out = (weights.shape[0], 2 * half)
    return pl.pallas_call(
        out_kernel,
        grid=(1,),
        in_specs=[full_spec(x.shape) for x in operands],
        out_specs=full_spec(out),
        out_shape=jax.ShapeDtypeStruct(out, BF16),
        compiler_params=params(),
        cost_estimate=pl.CostEstimate(
            flops=2 * weights.size * out[1], bytes_accessed=4 * weights.size, transcendentals=0
        ),
        name="out_projection",
    )(*operands)


def pair_block(pairs):
    return next(b for b in (256, 128, 64, 32, 16) if pairs % b == 0)


def dispatch(parts, hid_ref, norm_ref, router_ref, pos_ref, route_ref, resid_ref, spread_ref, aux_ref, aux_at):
    width, total = hid_ref.shape
    pairs = spread_ref.shape[1]
    resid = hid_ref[...].astype(F32)
    for part in parts:
        resid = resid + part[...].astype(F32)
    resid_ref[...] = resid
    moe = (resid * norm_ref[...]).astype(BF16)
    squares = jnp.sum(resid * resid, axis=0, keepdims=True)
    logits = dot_nn(router_ref[...], moe)
    expert = lax.broadcasted_iota(jnp.int32, logits.shape, 0)
    sign = (expert == route_ref[0:1]).astype(F32) - (expert == route_ref[1:2]).astype(F32)
    gap = jnp.sum(logits * sign, axis=0, keepdims=True)
    high = lax.broadcasted_iota(jnp.int32, (LANES, total), 0)
    aux_plain = jnp.zeros((LANES, total), F32)
    aux_signed = jnp.zeros((LANES, total), F32)
    for k, piece in enumerate(split_bf16(squares)):
        aux_plain = jnp.where(high == aux_at + k, piece, aux_plain)
    for k, piece in enumerate(split_bf16(gap)):
        aux_signed = jnp.where(high == aux_at + PIECES + k, piece, aux_signed)
    aux_plain = aux_plain.astype(BF16)
    aux_signed = aux_signed.astype(BF16)
    feature = lax.broadcasted_iota(jnp.int32, (width, 2 * width), 0)
    lane = lax.broadcasted_iota(jnp.int32, (width, 2 * width), 1)
    even = (lane == 2 * feature).astype(BF16)
    odd = (lane == 2 * feature + 1).astype(BF16)
    block = pair_block(pairs)
    for start in range(0, pairs, block):
        here = slice(start, start + block)
        pair = lax.broadcasted_iota(jnp.int32, (block, total), 0) + start
        first = (pair == pos_ref[0:1]).astype(F32)
        second = (pair == pos_ref[1:2]).astype(F32)
        both = (first + second).astype(BF16)
        rows = dot_nt(both, moe).astype(BF16)
        spread_ref[0, here] = dot_nn(rows, even).astype(BF16)
        spread_ref[1, here] = dot_nn(rows, odd).astype(BF16)
        aux_ref[here] = dot_nt(both, aux_plain) + dot_nt((first - second).astype(BF16), aux_signed)


def windows(pairs, per_expert):
    return min(per_expert + 16, pairs)


def window_of(offset_ref, expert, pairs, window):
    first = offset_ref[expert]
    start = pl.multiple_of(jnp.minimum(first // 16 * 16, pairs - window), 16)
    rows = lax.broadcasted_iota(jnp.int32, (window, 1), 0) + start
    return pl.ds(start, window), (rows >= first) & (rows < offset_ref[expert + 1])


def gate_kernel(count_parts, columns, tail, window, offset_ref, order_ref, *refs):
    first = count_parts > 0
    if first:
        parts, refs = refs[:count_parts], refs[count_parts:]
        hid_ref, norm_ref, router_ref, pos_ref, route_ref, w_ref, tail_ref = refs[:7]
        keep_ref, send_ref, resid_ref, spread_ref, held, aux = refs[7:]
    else:
        spread_ref, w_ref, keep_ref, send_ref, held = refs
    expert = pl.program_id(0)
    pairs = spread_ref.shape[1]
    width = spread_ref.shape[2] // 2

    if first:
        tail_width, _, aux_at, size = tail

        @pl.when(expert == 0)
        def _():
            dispatch(
                parts, hid_ref, norm_ref, router_ref, pos_ref, route_ref, resid_ref, spread_ref, aux, aux_at % LANES
            )

    rows, valid = window_of(offset_ref, expert, pairs, window)
    left = jnp.concatenate([spread_ref[0, rows], spread_ref[1, rows]], axis=0)
    weights = w_ref[0].reshape(2 * width, w_ref.shape[3])[:, :columns]
    result = dot_nn(left, weights).astype(BF16)
    held[rows, :columns] = jnp.where(valid, result[:window], held[rows, :columns])
    held[rows, columns : 2 * columns] = jnp.where(
        valid, result[window:], held[rows, columns : 2 * columns]
    )
    if first:
        weights = tail_ref[0].reshape(2 * width, LANES)
        result = dot_nn(left, weights)
        lane = lax.broadcasted_iota(jnp.int32, (window, LANES), 1)
        gate, up = result[:window], result[window:]
        if tail_width == LANES:
            block = jnp.where(lane < size, gate, pltpu.roll(up, size, 1))
            block = jnp.where(lane < 2 * size, block, aux[rows])
        else:
            block = jnp.concatenate(
                [jnp.where(lane < size, gate, 0.0), jnp.where(lane < size, up, 0.0), aux[rows]], axis=1
            )
        here = slice(2 * columns, 2 * columns + tail_width)
        held[rows, here] = jnp.where(valid, block.astype(BF16), held[rows, here])

    @pl.when(expert == pl.num_programs(0) - 1)
    def _():
        half, block, _ = keep_ref.shape
        for slot in range(half):
            mine = pl.ds(pl.multiple_of(order_ref[slot] * block, block), block)
            other = pl.ds(pl.multiple_of(order_ref[half + slot] * block, block), block)
            keep_ref[slot] = held[mine]
            send_ref[slot] = held[other]


def tail_layout(units):
    size = units % LANES
    if 2 * size + 2 * PIECES <= LANES:
        return LANES, size, 2 * size, size
    return 3 * LANES, LANES, 2 * LANES, size


def core_kernel(aux_at, keep_ref, recv_ref, *outs):
    half, block, width = keep_ref.shape
    for slot in range(half):
        total = keep_ref[slot].astype(F32) + recv_ref[slot].astype(F32)
        if aux_at is None:
            outs[slot][...] = total.astype(BF16)
            continue
        base = aux_at // LANES * LANES
        if base:
            outs[slot][:, :base] = total[:, :base].astype(BF16)
        tile = total[:, base : base + LANES]
        lane = lax.broadcasted_iota(jnp.int32, tile.shape, 1)
        at = aux_at - base
        for start in (at, at + PIECES):
            value = tile[:, start : start + 1]
            for k in range(1, PIECES):
                value = value + tile[:, start + k : start + k + 1]
            for k, piece in enumerate(split_bf16(value)):
                tile = jnp.where(lane == start + k, piece, tile)
        outs[slot][:, base : base + LANES] = tile.astype(BF16)
        if base + LANES < width:
            outs[slot][:, base + LANES :] = total[:, base + LANES :].astype(BF16)


def core_sum(keep, recv, aux_at, name):
    half, block, width = keep.shape
    out = jax.ShapeDtypeStruct((block, width), BF16)
    return pl.pallas_call(
        functools.partial(core_kernel, aux_at),
        grid=(1,),
        in_specs=[full_spec(keep.shape)] * 2,
        out_specs=[full_spec(out.shape)] * half,
        out_shape=[out] * half,
        compiler_params=params(),
        cost_estimate=pl.CostEstimate(flops=keep.size, bytes_accessed=6 * keep.size, transcendentals=0),
        name=name,
    )(keep, recv)


def act_kernel(count_parts, columns, tail, features, *refs):
    parts, refs = refs[:count_parts], refs[count_parts:]
    total = parts[0][...].astype(F32)
    for part in parts[1:]:
        total = total + part[...].astype(F32)
    if tail is None:
        stat_ref, act_ref = refs
        inverse, weight = stat_ref[:, 0:1], stat_ref[:, 1:2]
    else:
        act_ref, stat_ref = refs
        tail_width, up_at, aux_at, size = tail
        base = 2 * columns + aux_at
        squares = total[:, base : base + 1]
        gap = total[:, base + PIECES : base + PIECES + 1]
        for k in range(1, PIECES):
            squares = squares + total[:, base + k : base + k + 1]
            gap = gap + total[:, base + PIECES + k : base + PIECES + k + 1]
        inverse = lax.rsqrt(squares / features + 1e-06)
        weight = 1.0 / (1.0 + jnp.exp(-gap * inverse))
        lane = lax.broadcasted_iota(jnp.int32, (total.shape[0], LANES), 1)
        stat_ref[...] = jnp.where(lane == 0, inverse, weight)

    def activate(gate, up):
        gate = gate * inverse
        return gate / (1.0 + jnp.exp(-gate)) * (up * inverse) * weight

    act_ref[:, :columns] = activate(total[:, :columns], total[:, columns : 2 * columns]).astype(BF16)
    if tail is not None:
        block = total[:, 2 * columns : 2 * columns + LANES]
        if tail_width == LANES:
            up = pltpu.roll(block, LANES - size, 1)
        else:
            up = total[:, 2 * columns + LANES : 2 * columns + 2 * LANES]
        last = jnp.where(lane < size, activate(block, up), 0.0)
        act_ref[:, columns:] = last.astype(BF16)


def activation(parts, stats, columns, tail, features, name):
    rows = parts[0].shape[0]
    out = jax.ShapeDtypeStruct((rows, columns + (LANES if tail else 0)), BF16)
    stat = jax.ShapeDtypeStruct((rows, LANES), F32)
    operands = [*parts] + ([] if tail else [stats])
    outs = [out, stat] if tail else [out]
    result = pl.pallas_call(
        functools.partial(act_kernel, len(parts), columns, tail, features),
        grid=(1,),
        in_specs=[full_spec(x.shape) for x in operands],
        out_specs=[full_spec(x.shape) for x in outs],
        out_shape=outs,
        compiler_params=params(),
        cost_estimate=pl.CostEstimate(
            flops=16 * rows * columns, bytes_accessed=20 * rows * columns, transcendentals=rows * columns
        ),
        name=name,
    )(*operands)
    return (result[0], result[1]) if tail else (result[0], stats)


def down_kernel(count_parts, columns, tail, window, begins, ends, requests, offset_ref, order_ref, *refs):
    parts, refs = refs[:count_parts], refs[count_parts:]
    other_ref, w_ref, refs = refs[0], refs[1], refs[2:]
    if tail:
        tail_ref, refs = refs[0], refs[1:]
    if not begins:
        before_ref, refs = refs[0], refs[1:]
    if ends:
        place_ref, resid_ref, out_ref, total_ref, held = refs
    else:
        total_ref, held = refs
    expert = pl.program_id(0)
    block = parts[0].shape[0]
    half = len(parts)
    pairs = held.shape[0]

    @pl.when(expert == 0)
    def _():
        for slot in range(half):
            mine = pl.ds(pl.multiple_of(order_ref[slot] * block, block), block)
            other = pl.ds(pl.multiple_of(order_ref[half + slot] * block, block), block)
            held[mine] = parts[slot][...]
            held[other] = other_ref[slot]
        total_ref[...] = jnp.zeros_like(total_ref) if begins else before_ref[...]

    rows, valid = window_of(offset_ref, expert, pairs, window)
    result = dot_nt(held[rows, :columns], w_ref[0][:, :columns])
    if tail:
        size = tail[3]
        result = result + dot_nt(held[rows, columns : columns + size], tail_ref[0][:, :size])
    total_ref[rows] = total_ref[rows] + jnp.where(valid, result, 0.0)

    if ends:

        @pl.when(expert == pl.num_programs(0) - 1)
        def _():
            total = out_ref.shape[0]
            pieces = [x.astype(BF16) for x in split_bf16(total_ref[...], 2)]
            resid = [x.astype(BF16) for x in split_bf16(resid_ref[...], 2)]
            step = pair_block(total) if total > 256 else total
            step = min(step, 256)
            for start in range(0, total, step):
                here = slice(start, start + step)
                pair = lax.broadcasted_iota(jnp.int32, (step, pairs), 1)
                pick = (pair == place_ref[here, 0:1]) | (pair == place_ref[here, 1:2])
                pick = pick.astype(F32).astype(BF16)
                token = lax.broadcasted_iota(jnp.int32, (step, total), 1)
                move = (token == place_ref[here, 2:3]).astype(F32).astype(BF16)
                result = dot_nn(pick, pieces[0]) + dot_nn(pick, pieces[1])
                result = result + dot_nt(move, resid[0]) + dot_nt(move, resid[1])
                out_ref[here] = result.astype(BF16)


def largest_tile(full):
    return LANES * min(4, full)


def local(
    hidden_in,
    cache_pool,
    project_in,
    project_out,
    norm_first,
    norm_second,
    router,
    gate_up,
    expert_down,
    lengths,
    prompt_pages,
    own_pages,
    groups,
    move_target,
    routes,
):
    dp = lax.axis_size("dp")
    fs = lax.axis_size("fsdp")
    half = dp // 2
    my_row = lax.axis_index("dp")
    my_column = lax.axis_index("fsdp")
    my_chip, my_core = my_row // 2, my_row % 2
    req, features = hidden_in.shape
    row = req * fs
    total = row * dp
    pairs = 2 * total
    width = project_in.shape[0]
    cols = cache_pool.shape[3]
    heads = cols // HD
    page_len = cache_pool.shape[1]
    movers = move_target.shape[1]
    staying = row - movers
    experts = router.shape[1]
    units = gate_up.shape[3]
    window = windows(pairs, CAP * dp * fs)

    chip = jnp.arange(half, dtype=jnp.int32)
    order = jnp.concatenate([(chip ^ my_chip) * 2 + my_core, (chip ^ my_chip) * 2 + 1 - my_core])

    def swap(x):
        return lax.ppermute(x, "dp", [(i, i ^ 1) for i in range(dp)])

    def over_chips(x, s):
        return lax.ppermute(x, "dp", [(i, i ^ (2 * s)) for i in range(dp)])

    def over_columns(x, s):
        return lax.ppermute(x, "fsdp", [(i, i ^ s) for i in range(fs)])

    wide = hidden_in.astype(F32)
    factor = lax.rsqrt(jnp.mean(wide * wide, axis=1, keepdims=True) + 1e-06)
    extra = []
    for _ in range(PIECES):
        piece = lax.reduce_precision(factor, 8, 7)
        extra.append(piece.astype(BF16))
        factor = factor - piece
    extra = jnp.concatenate([*extra, routes.astype(BF16)], axis=1)
    sliced = hidden_in.reshape(req, dp, width).transpose(1, 0, 2)
    room = -(width + extra.shape[1]) % LANES
    sliced = jnp.concatenate(
        [
            sliced,
            jnp.broadcast_to(extra[None], (dp, *extra.shape)),
            jnp.zeros((dp, req, room), BF16),
        ],
        axis=2,
    )
    payload = jnp.broadcast_to(sliced[:, None], (dp, fs, *sliced.shape[1:]))
    payload = payload.reshape(dp * fs, req, sliced.shape[2])
    recv = lax.all_to_all(payload, ("dp", "fsdp"), 0, 0, tiled=True).reshape(total, sliced.shape[2])

    keys, values = split_pool(cache_pool)
    group_hit = groups[:, None] == jnp.arange(prompt_pages.shape[0], dtype=jnp.int32)[None, :]
    prompt_list = jnp.sum(jnp.where(group_hit[:, :, None], prompt_pages[None], 0), axis=1)
    page_list = jnp.concatenate([prompt_list, own_pages], axis=1)
    row_lengths = lax.dynamic_slice_in_dim(lengths, my_row * row, row)
    spot = jnp.arange(cache_pool.shape[0] * page_len, dtype=jnp.int32)
    listed = page_list[:, :, None] == (spot // page_len)[None, None, :]
    left = row_lengths[:, None] - page_len * jnp.arange(page_list.shape[1], dtype=jnp.int32)[None, :]
    reach = jnp.sum(jnp.where(listed, left[:, :, None], 0), axis=1)
    bias = jnp.where((spot % page_len)[None, :] < reach, 0.0, FAR).astype(F32)
    lane = jnp.arange(cols, dtype=jnp.int32)
    channel = (lane % (HD // 2)).astype(F32)
    inverse = jnp.exp(-jnp.log(10000.0) * 2.0 * channel / HD)
    angles = row_lengths.astype(F32)[:, None] * inverse[None, :]
    cosine = jnp.cos(angles)
    sine = jnp.where((lane % HD < HD // 2)[None, :], -1.0, 1.0) * jnp.sin(angles)

    def slice_of(vector):
        return lax.dynamic_slice_in_dim(vector, my_row * width, width)

    keep, send, raw = project_qkv(
        order,
        recv,
        slice_of(norm_first).astype(F32)[None, :],
        project_in.transpose(1, 0, 2),
        half,
        row,
    )
    other = swap(send)
    sums = [(keep[s].astype(F32) + other[s].astype(F32)).astype(BF16) for s in range(half)]
    parts = [sums[0]] + [over_chips(sums[s], s) for s in range(1, half)]
    heads_out = attend(parts, cosine, sine, bias, keys, values)

    parts = [heads_out] + [over_chips(heads_out, s) for s in range(1, half)]
    other = swap(jnp.concatenate(parts, axis=0))
    projected = project_heads(parts, other, project_out.T)
    parts = [projected] + [over_columns(projected, s) for s in range(1, fs)]

    routes_all = recv[:, width + PIECES : width + PIECES + 2].astype(jnp.int32)
    expert_ids = jnp.arange(experts, dtype=jnp.int32)
    picked = (routes_all[:, :, None] == expert_ids[None, None, :]).astype(jnp.int32)
    member = picked[:, 0] + picked[:, 1]
    upto = jnp.cumsum(member, axis=0)
    counts = upto[-1]
    ends = jnp.cumsum(counts)
    offsets = jnp.concatenate([jnp.zeros((1,), jnp.int32), ends]).astype(jnp.int32)
    places = (upto - member) + offsets[None, :experts]
    place = jnp.sum(picked * places[:, None, :], axis=2)

    row_ids = jnp.arange(dp, dtype=jnp.int32)
    table = jnp.concatenate([place, routes_all], axis=1).reshape(dp, row, 4)
    to_row = (move_target[:, :, None] == row_ids[None, None, :]).astype(jnp.int32)
    moved = jnp.sum(to_row[:, :, :, None] * table[:, staying:].transpose(1, 0, 2)[None], axis=2)
    by_source = jnp.concatenate([table[:, :staying], moved], axis=1)
    here = (order[:, None] == row_ids[None, :]).astype(jnp.int32)
    by_slot = jnp.sum(here[:, :, None, None] * by_source[None], axis=1).reshape(total, 4).T
    slot_of_row = jnp.sum(here * row_ids[:, None], axis=0)
    source_slot = jnp.sum(to_row * slot_of_row[:, None, None], axis=0).T
    slot_of = jnp.concatenate([jnp.broadcast_to(slot_of_row[:, None], (dp, staying)), source_slot], axis=1)
    token = jnp.arange(total, dtype=jnp.int32)
    lies_at = slot_of.reshape(total) * row + token % row
    lies_at = jnp.where(token // req % fs == my_column, lies_at, -1)
    place_table = jnp.concatenate([place, lies_at[:, None]], axis=1)

    full = units // LANES
    step = largest_tile(full)
    chunks = [(k, min(step, full * LANES - k * step)) for k in range(-(-full * LANES // step))]
    tail = tail_layout(units)
    tail_block = units // LANES
    block = pairs // dp
    spread = jax.ShapeDtypeStruct((2, pairs, 2 * width), BF16)
    resid_shape = jax.ShapeDtypeStruct((width, total), F32)
    norm_column = slice_of(norm_second).astype(F32)[:, None]
    router_slice = lax.dynamic_slice_in_dim(router, my_row * width, width).T
    acts, stats = [], None
    pos_slot, route_slot = by_slot[:2], by_slot[2:]
    reduced = []
    for index, (number, columns) in enumerate(chunks):
        first = index == 0
        out_width = 2 * columns + (tail[0] if first else 0)
        half_out = jax.ShapeDtypeStruct((half, block, out_width), BF16)
        weight_spec = pl.BlockSpec((1, width, 2, step), lambda e, *_, k=number: (e, 0, 0, k))
        if first:
            operands = [*parts, raw.T, norm_column, router_slice, pos_slot, route_slot]
            in_specs = [full_spec(x.shape) for x in operands] + [
                weight_spec,
                pl.BlockSpec((1, width, 2, LANES), lambda e, *_: (e, 0, 0, tail_block)),
            ]
            operands += [gate_up, gate_up]
            outs = [half_out, half_out, resid_shape, spread]
            scratch = [pltpu.VMEM((pairs, out_width), BF16), pltpu.VMEM((pairs, LANES), F32)]
        else:
            operands = [spread_value, gate_up]
            in_specs = [full_spec(spread.shape), weight_spec]
            outs = [half_out, half_out]
            scratch = [pltpu.VMEM((pairs, out_width), BF16)]
        result = pl.pallas_call(
            functools.partial(gate_kernel, len(parts) if first else 0, columns, tail, window),
            grid_spec=pltpu.PrefetchScalarGridSpec(
                num_scalar_prefetch=2,
                grid=(experts,),
                in_specs=in_specs,
                out_specs=[full_spec(x.shape) for x in outs],
                scratch_shapes=scratch,
            ),
            out_shape=outs,
            compiler_params=params(40 if pairs <= 1024 else 60),
            cost_estimate=pl.CostEstimate(
                flops=8 * experts * window * width * columns,
                bytes_accessed=4 * experts * width * columns,
                transcendentals=0,
            ),
            name=f"gate_up_{index}",
        )(offsets, order, *operands)
        if first:
            keep, send, resid, spread_value = result
        else:
            keep, send = result
        aux_at = 2 * columns + tail[2] if first else None
        sums = core_sum(keep, swap(send), aux_at, f"core_sum_{index}")
        reduced.append([sums[0]] + [over_chips(sums[s], s) for s in range(1, half)])

    result = None
    for index, (number, columns) in enumerate(chunks):
        first, last = index == 0, index == len(chunks) - 1
        act, stats = activation(
            reduced[index], stats, columns, tail if first else None, float(features), f"activation_{index}"
        )
        parts = [act] + [over_chips(act, s) for s in range(1, half)]
        other = swap(jnp.stack(parts))
        operands = [*parts, other]
        in_specs = [full_spec(x.shape) for x in operands]
        operands.append(expert_down)
        in_specs.append(pl.BlockSpec((1, width, step), lambda e, *_, k=number: (e, 0, k)))
        if first:
            operands.append(expert_down)
            in_specs.append(pl.BlockSpec((1, width, LANES), lambda e, *_: (e, 0, tail_block)))
        else:
            operands.append(result)
            in_specs.append(full_spec(result.shape))
        sum_shape = jax.ShapeDtypeStruct((pairs, width), F32)
        scratch = [pltpu.VMEM((pairs, act.shape[1]), BF16)]
        outs = [sum_shape]
        if last:
            operands += [place_table, resid]
            in_specs += [full_spec(place_table.shape), full_spec(resid.shape)]
            outs = [jax.ShapeDtypeStruct((total, width), BF16)]
            scratch = [pltpu.VMEM(sum_shape.shape, F32)] + scratch
        result = pl.pallas_call(
            functools.partial(
                down_kernel, len(parts), columns, tail if first else None, window, first, last, total
            ),
            grid_spec=pltpu.PrefetchScalarGridSpec(
                num_scalar_prefetch=2,
                grid=(experts,),
                in_specs=in_specs,
                out_specs=[full_spec(x.shape) for x in outs],
                scratch_shapes=scratch,
            ),
            out_shape=outs,
            compiler_params=params(40 if pairs <= 1024 else 60),
            cost_estimate=pl.CostEstimate(
                flops=2 * experts * window * width * columns,
                bytes_accessed=2 * experts * width * columns,
                transcendentals=0,
            ),
            name=f"down_{index}",
        )(offsets, order, *operands)[0]

    back = lax.all_to_all(result.reshape(dp * fs, req, width), ("dp", "fsdp"), 0, 0, tiled=True)
    back = back.reshape(dp, fs, req, width).astype(F32)
    return jnp.sum(back, axis=1).transpose(1, 0, 2).reshape(req, features).astype(BF16)


def solution(mesh):
    placed = (
        P(("dp", "fsdp"), None),
        P("dp", None, None, "fsdp"),
        P("dp", None, "fsdp"),
        P("fsdp", "dp"),
        P(),
        P(),
        P(),
        P(None, "dp", None, "fsdp"),
        P(None, "dp", "fsdp"),
        P(),
        P("dp", None),
        P("dp", None),
        P("dp"),
        P(),
        P(("dp", "fsdp"), None),
    )
    return jax.shard_map(
        local, mesh=mesh, in_specs=placed, out_specs=P(("dp", "fsdp"), None), check_vma=False
    )
```

```python
import functools

import jax
import jax.numpy as jnp
from jax import lax
from jax.experimental import pallas as pl
from jax.experimental.pallas import tpu as pltpu
from jax.sharding import PartitionSpec as P

HD = 64
CAP = 4
PIECES = 3
LANES = 128
BF16 = jnp.bfloat16
F32 = jnp.float32
FAR = -3.0e38
SMALL, ATTENTION, LARGE = 12, 24, 60
SLOTS = 4


def params(mib=SMALL):
    return pltpu.CompilerParams(vmem_limit_bytes=mib * 2**20)


def room(tokens):
    return SMALL if tokens <= 512 else LARGE


def dot_nn(a, b):
    return lax.dot_general(a, b, (((1,), (0,)), ((), ())), preferred_element_type=F32)


def dot_nt(a, b):
    return lax.dot_general(a, b, (((1,), (1,)), ((), ())), preferred_element_type=F32)


def split_bf16(value, count=PIECES):
    pieces = []
    for _ in range(count):
        piece = value.astype(BF16).astype(F32)
        pieces.append(piece)
        value = value - piece
    return pieces


def full_spec(shape):
    zeros = (0,) * len(shape)
    return pl.BlockSpec(tuple(shape), lambda *_: zeros, pipeline_mode=pl.Buffered(1))


def pack_kernel(hidden_ref, routes_ref, out_ref):
    slices, copies, req, room = out_ref.shape
    features = hidden_ref.shape[1]
    width = features // slices
    values = hidden_ref[...].astype(F32)
    factor = lax.rsqrt(jnp.mean(values * values, axis=1, keepdims=True) + 1e-06)
    lane = lax.broadcasted_iota(jnp.int32, (req, room), 1)
    extra = jnp.zeros((req, room), F32)
    for k, piece in enumerate(split_bf16(factor)):
        extra = jnp.where(lane == width + k, piece, extra)
    spot = lax.broadcasted_iota(jnp.int32, (req, req), 1) == lax.broadcasted_iota(jnp.int32, (req, req), 0)
    for k in range(2):
        route = jnp.sum(jnp.where(spot, routes_ref[k : k + 1].astype(F32), 0.0), axis=1, keepdims=True)
        extra = jnp.where(lane == width + PIECES + k, route, extra)
    for index in range(slices):
        moved = pltpu.roll(values, (features - index * width) % features, 1) if index else values
        block = jnp.where(lane < width, moved[:, :room], extra).astype(BF16)
        for copy in range(copies):
            out_ref[index, copy] = block


def pack(hidden_in, routes, slices, copies):
    req, features = hidden_in.shape
    width = features // slices
    room = -(-(width + PIECES + 2) // LANES) * LANES
    out = (slices, copies, req, room)
    return pl.pallas_call(
        pack_kernel,
        grid=(1,),
        in_specs=[full_spec(hidden_in.shape), full_spec(routes.shape)],
        out_specs=full_spec(out),
        out_shape=jax.ShapeDtypeStruct(out, BF16),
        compiler_params=params(),
        cost_estimate=pl.CostEstimate(flops=hidden_in.size, bytes_accessed=4 * hidden_in.size, transcendentals=0),
        name="pack",
    )(hidden_in, routes)


def places_kernel(
    experts, width, staying, move_ref, order_ref, slot_ref, column_ref, recv_ref, _, off_ref, place_ref, line_ref, table, slots
):
    total = recv_ref.shape[0]
    rows_count, movers = move_ref.shape
    row = total // rows_count
    block = min(total, 256)
    lane = lax.broadcasted_iota(jnp.int32, (block, LANES), 1)
    above = lax.broadcasted_iota(jnp.int32, (block, block), 0)
    beside = lax.broadcasted_iota(jnp.int32, (block, block), 1)
    before = (beside < above).astype(F32).astype(BF16)
    counts = jnp.zeros((1, LANES), F32)
    for start in range(0, total, block):
        here = slice(start, start + block)
        first = recv_ref[here, width + PIECES : width + PIECES + 1].astype(F32).astype(jnp.int32)
        second = recv_ref[here, width + PIECES + 1 : width + PIECES + 2].astype(F32).astype(jnp.int32)
        member = (lane == first).astype(F32) + (lane == second).astype(F32)
        rank = dot_nn(before, member.astype(BF16)) + counts
        counts = counts + jnp.sum(member, axis=0, keepdims=True)
        mine = jnp.sum(jnp.where(lane == first, rank, 0.0), axis=1, keepdims=True)
        other = jnp.sum(jnp.where(lane == second, rank, 0.0), axis=1, keepdims=True)
        block_table = jnp.where(lane == 0, mine, jnp.where(lane == 1, other, 0.0))
        block_table = jnp.where(lane == 2, first.astype(F32), block_table)
        table[here] = jnp.where(lane == 3, second.astype(F32), block_table)
    single = lax.broadcasted_iota(jnp.int32, (1, LANES), 1)
    sums = [jnp.sum(jnp.where(single == e, counts, 0.0)) for e in range(experts)]
    off_ref[0] = 0
    running = jnp.float32(0.0)
    begins = jnp.zeros((1, LANES), F32)
    for e in range(experts):
        begins = jnp.where(single == e, running, begins)
        running = running + sums[e]
        off_ref[e + 1] = running.astype(jnp.int32)
    for start in range(0, total, block):
        here = slice(start, start + block)
        values = table[here]
        first = values[:, 2:3].astype(jnp.int32)
        second = values[:, 3:4].astype(jnp.int32)
        begin_first = jnp.sum(jnp.where(lane == first, begins, 0.0), axis=1, keepdims=True)
        begin_second = jnp.sum(jnp.where(lane == second, begins, 0.0), axis=1, keepdims=True)
        values = values + jnp.where(lane == 0, begin_first, jnp.where(lane == 1, begin_second, 0.0))
        table[here] = values
        place_ref[here] = values
    within = lax.broadcasted_iota(jnp.int32, (row, LANES), 0)
    wide = lax.broadcasted_iota(jnp.int32, (row, LANES), 1)
    req = row // column_ref[1]
    mine = (within >= column_ref[0] * req) & (within < (column_ref[0] + 1) * req)
    for r in range(rows_count):
        here = slice(r * row, (r + 1) * row)
        lies = jnp.where(mine, (within + slot_ref[r] * row).astype(F32), -1.0)
        place_ref[here] = jnp.where(wide == 2, lies, place_ref[here])
    for r in range(rows_count):
        for j in range(movers):
            at = staying + j
            target = pl.ds(move_ref[r, j] * row + at, 1)
            held = (at >= column_ref[0] * req) & (at < (column_ref[0] + 1) * req)
            lies = jnp.where(held, slot_ref[r] * row + at, -1).astype(F32)
            place_ref[target] = jnp.where(single == 2, lies, place_ref[target])
    for b in range(rows_count):
        slots[b * row : (b + 1) * row] = table[pl.ds(pl.multiple_of(order_ref[b] * row, row), row)]
        for j in range(movers):
            at = staying + j
            source = pl.ds(move_ref[order_ref[b], j] * row + at, 1)
            slots[b * row + at : b * row + at + 1] = table[source]
    line_ref[...] = slots[...].T[:8]


def pair_places(move_target, order, slot_of, column, recv, after, experts, width):
    total = recv.shape[0]
    rows_count, movers = move_target.shape
    staying = total // rows_count - movers
    outs = [
        jax.ShapeDtypeStruct((experts + 1,), jnp.int32),
        jax.ShapeDtypeStruct((total, LANES), F32),
        jax.ShapeDtypeStruct((8, total), F32),
    ]
    return pl.pallas_call(
        functools.partial(places_kernel, experts, width, staying),
        grid_spec=pltpu.PrefetchScalarGridSpec(
            num_scalar_prefetch=4,
            grid=(1,),
            in_specs=[full_spec(recv.shape), pl.BlockSpec(memory_space=pl.ANY)],
            out_specs=[
                pl.BlockSpec(memory_space=pltpu.SMEM),
                full_spec(outs[1].shape),
                full_spec(outs[2].shape),
            ],
            scratch_shapes=[pltpu.VMEM((total, LANES), F32), pltpu.VMEM((total, LANES), F32)],
        ),
        out_shape=outs,
        compiler_params=params(room(total)),
        cost_estimate=pl.CostEstimate(
            flops=total * total * LANES, bytes_accessed=16 * total * LANES, transcendentals=0
        ),
        name="pair_places",
    )(move_target, order, slot_of, column, recv, after)


def pool_kernel(prompt_ref, lists_ref, pool_ref, _, key_ref, value_ref, bias_ref):
    pages, page_len, _, cols = pool_ref.shape
    rows = pages * page_len
    both = pool_ref[...].reshape(2 * rows, cols)
    wide = lax.broadcasted_iota(jnp.int32, (rows, 2 * rows), 1)
    high = lax.broadcasted_iota(jnp.int32, (rows, 2 * rows), 0)
    key_ref[...] = dot_nn((wide == 2 * high).astype(BF16), both).astype(BF16)
    value_ref[...] = dot_nn((wide == 2 * high + 1).astype(BF16), both).astype(BF16)
    requests = bias_ref.shape[0]
    prompts, prompt_len = prompt_ref.shape
    own_len = lists_ref.shape[1] - 2
    group, length = lists_ref[:, own_len : own_len + 1], lists_ref[:, own_len + 1 :]
    spot = lax.broadcasted_iota(jnp.int32, (requests, rows), 1)
    page = spot // page_len + pl.program_id(0) * pages
    reach = jnp.zeros((requests, rows), jnp.int32)
    for k in range(prompt_len):
        listed = jnp.zeros((requests, 1), jnp.int32)
        for g in range(prompts):
            listed = jnp.where(group == g, prompt_ref[g, k], listed)
        reach = jnp.where(page == listed, length - page_len * k, reach)
    for k in range(own_len):
        reach = jnp.where(page == lists_ref[:, k : k + 1], length - page_len * (prompt_len + k), reach)
    bias_ref[...] = jnp.where(spot % page_len < reach, 0.0, FAR)


def split_pool(prompt_pages, lists, cache_pool, after):
    pages, page_len, _, cols = cache_pool.shape
    requests = lists.shape[0]
    block = next(b for b in (16, 8, 4, 2, 1) if pages % b == 0)
    out = jax.ShapeDtypeStruct((pages * page_len, cols), BF16)
    spec = pl.BlockSpec((block * page_len, cols), lambda b, *_: (b, 0))
    return pl.pallas_call(
        pool_kernel,
        grid_spec=pltpu.PrefetchScalarGridSpec(
            num_scalar_prefetch=1,
            grid=(pages // block,),
            in_specs=[
                full_spec(lists.shape),
                pl.BlockSpec((block, page_len, 2, cols), lambda b, *_: (b, 0, 0, 0)),
                pl.BlockSpec(memory_space=pl.ANY),
            ],
            out_specs=[spec, spec, pl.BlockSpec((requests, block * page_len), lambda b, *_: (0, b))],
        ),
        out_shape=[out, out, jax.ShapeDtypeStruct((requests, pages * page_len), F32)],
        compiler_params=params(),
        cost_estimate=pl.CostEstimate(
            flops=8 * block * page_len * cache_pool.size,
            bytes_accessed=4 * cache_pool.size,
            transcendentals=0,
        ),
        name="pool_split",
    )(prompt_pages, lists, cache_pool, after)


def qkv_kernel(order_ref, recv_ref, norm_ref, w_ref, _, keep_ref, send_ref, raw_ref, normed, slots):
    width = norm_ref.shape[1]
    half, row, _ = keep_ref.shape
    cols = w_ref.shape[2]
    values = recv_ref[:, :width]
    scale = recv_ref[:, width : width + 1].astype(F32)
    for piece in range(1, PIECES):
        scale = scale + recv_ref[:, width + piece : width + piece + 1].astype(F32)
    normed[...] = (values.astype(F32) * scale * norm_ref[...]).astype(BF16)
    for slot in range(2 * half):
        rows = pl.ds(pl.multiple_of(order_ref[slot] * row, row), row)
        slots[slot * row : (slot + 1) * row] = normed[rows]
        raw_ref[slot * row : (slot + 1) * row] = recv_ref[rows, :width]
    for part in range(3):
        here = slice(part * cols, (part + 1) * cols)
        result = dot_nn(slots[...], w_ref[part]).astype(BF16).reshape(2 * half, row, cols)
        keep_ref[:, :, here] = result[:half]
        send_ref[:, :, here] = result[half:]


def project_qkv(order, recv, norm_slice, weights, half, row, after):
    total, _ = recv.shape
    width, cols = weights.shape[1:]
    out = jax.ShapeDtypeStruct((half, row, 3 * cols), BF16)
    raw = jax.ShapeDtypeStruct((total, width), BF16)
    return pl.pallas_call(
        qkv_kernel,
        grid_spec=pltpu.PrefetchScalarGridSpec(
            num_scalar_prefetch=1,
            grid=(1,),
            in_specs=[full_spec(x.shape) for x in (recv, norm_slice, weights)] + [pl.BlockSpec(memory_space=pl.ANY)],
            out_specs=[full_spec(out.shape), full_spec(out.shape), full_spec(raw.shape)],
            scratch_shapes=[pltpu.VMEM((total, width), BF16), pltpu.VMEM((total, width), BF16)],
        ),
        out_shape=[out, out, raw],
        compiler_params=params(room(total)),
        cost_estimate=pl.CostEstimate(
            flops=6 * total * width * cols, bytes_accessed=6 * total * cols + 6 * width * cols, transcendentals=0
        ),
        name="qkv",
    )(order, recv, norm_slice, weights, after)


def attention_kernel(*refs):
    parts, refs = refs[:-9], refs[-9:]
    cos_ref, sin_ref, bias_ref, key_ref, value_ref, _, out_ref, scores, probs = refs
    row, cols = out_ref.shape
    heads = cols // HD
    total = parts[0][0].astype(F32)
    for part in parts[1:]:
        total = total + part[0].astype(F32)
    lane = lax.broadcasted_iota(jnp.int32, (row, cols), 1)
    first_half = lane % HD < HD // 2

    def rotate(values):
        partner = jnp.where(
            first_half, pltpu.roll(values, cols - HD // 2, 1), pltpu.roll(values, HD // 2, 1)
        )
        return (values * cos_ref[...] + partner * sin_ref[...]).astype(BF16)

    query = rotate(total[:, :cols]).astype(F32)
    key_new = rotate(total[:, cols : 2 * cols]).astype(F32)
    value_new = total[:, 2 * cols :].astype(BF16).astype(F32)
    spread = jnp.concatenate(
        [jnp.where(lane // HD == h, query, 0.0).astype(BF16) for h in range(heads)], axis=0
    )
    scores[...] = dot_nt(spread, key_ref[...])
    own_parts = []
    for h in range(heads):
        here = slice(h * row, (h + 1) * row)
        mine = lane // HD == h
        own = jnp.sum(jnp.where(mine, query * key_new, 0.0), axis=1, keepdims=True) * HD**-0.5
        score = scores[here] * HD**-0.5 + bias_ref[...]
        highest = jnp.maximum(jnp.max(score, axis=1, keepdims=True), own)
        weight = jnp.exp(score - highest)
        weight_own = jnp.exp(own - highest)
        inverse = 1.0 / (jnp.sum(weight, axis=1, keepdims=True) + weight_own)
        probs[here] = (weight * inverse).astype(BF16)
        own_parts.append((weight_own * inverse).astype(BF16).astype(F32))
    mixture = dot_nn(probs[...], value_ref[...])
    result = jnp.zeros((row, cols), F32)
    for h in range(heads):
        mixed = mixture[h * row : (h + 1) * row] + own_parts[h] * value_new
        result = jnp.where(lane // HD == h, mixed, result)
    out_ref[...] = result.astype(BF16)


def attend(parts, cosine, sine, bias, keys, values, after):
    row, cols = cosine.shape
    stretch = keys.shape[0]
    heads = cols // HD
    operands = [*parts, cosine, sine, bias, keys, values]
    return pl.pallas_call(
        attention_kernel,
        grid=(1,),
        in_specs=[full_spec(x.shape) for x in operands] + [pl.BlockSpec(memory_space=pl.ANY)],
        out_specs=full_spec((row, cols)),
        out_shape=jax.ShapeDtypeStruct((row, cols), BF16),
        scratch_shapes=[
            pltpu.VMEM((heads * row, stretch), F32),
            pltpu.VMEM((heads * row, stretch), BF16),
        ],
        compiler_params=params(ATTENTION),
        cost_estimate=pl.CostEstimate(
            flops=4 * heads * row * stretch * cols,
            bytes_accessed=4 * stretch * cols,
            transcendentals=heads * row * stretch,
        ),
        name="attention",
    )(*operands, after)


def out_kernel(*refs):
    parts, (other_ref, w_ref, out_ref) = refs[:-3], refs[-3:]
    half = len(parts) * parts[0].shape[0]
    mine = jnp.concatenate([part[...] for part in parts], axis=0)
    out_ref[:, :half] = dot_nt(w_ref[...], mine).astype(BF16)
    out_ref[:, half:] = dot_nt(w_ref[...], other_ref[...]).astype(BF16)


def project_heads(parts, other, weights):
    half = other.shape[0]
    operands = [*parts, other, weights]
    out = (weights.shape[0], 2 * half)
    return pl.pallas_call(
        out_kernel,
        grid=(1,),
        in_specs=[full_spec(x.shape) for x in operands],
        out_specs=full_spec(out),
        out_shape=jax.ShapeDtypeStruct(out, BF16),
        compiler_params=params(room(2 * half)),
        cost_estimate=pl.CostEstimate(
            flops=2 * weights.size * out[1], bytes_accessed=4 * weights.size, transcendentals=0
        ),
        name="out_projection",
    )(*operands)


def pair_block(pairs):
    return next(b for b in (256, 128, 64, 32, 16) if pairs % b == 0)


def dispatch(parts, hid_ref, norm_ref, router_ref, line_ref, resid_ref, spread_ref, aux_ref, aux_at):
    width, total = hid_ref.shape
    pairs = spread_ref.shape[1]
    resid = hid_ref[...].astype(F32)
    for part in parts:
        resid = resid + part[...].astype(F32)
    resid_ref[...] = resid
    moe = (resid * norm_ref[...]).astype(BF16)
    squares = jnp.sum(resid * resid, axis=0, keepdims=True)
    logits = dot_nn(router_ref[...], moe)
    expert = lax.broadcasted_iota(jnp.int32, logits.shape, 0)
    line = line_ref[...].astype(jnp.int32)
    sign = (expert == line[2:3]).astype(F32) - (expert == line[3:4]).astype(F32)
    gap = jnp.sum(logits * sign, axis=0, keepdims=True)
    high = lax.broadcasted_iota(jnp.int32, (LANES, total), 0)
    aux_plain = jnp.zeros((LANES, total), F32)
    aux_signed = jnp.zeros((LANES, total), F32)
    for k, piece in enumerate(split_bf16(squares)):
        aux_plain = jnp.where(high == aux_at + k, piece, aux_plain)
    for k, piece in enumerate(split_bf16(gap)):
        aux_signed = jnp.where(high == aux_at + PIECES + k, piece, aux_signed)
    aux_plain = aux_plain.astype(BF16)
    aux_signed = aux_signed.astype(BF16)
    feature = lax.broadcasted_iota(jnp.int32, (width, 2 * width), 0)
    lane = lax.broadcasted_iota(jnp.int32, (width, 2 * width), 1)
    even = (lane == 2 * feature).astype(BF16)
    odd = (lane == 2 * feature + 1).astype(BF16)
    block = pair_block(pairs)
    for start in range(0, pairs, block):
        here = slice(start, start + block)
        pair = lax.broadcasted_iota(jnp.int32, (block, total), 0) + start
        first = (pair == line[0:1]).astype(F32)
        second = (pair == line[1:2]).astype(F32)
        both = (first + second).astype(BF16)
        rows = dot_nt(both, moe).astype(BF16)
        spread_ref[0, here] = dot_nn(rows, even).astype(BF16)
        spread_ref[1, here] = dot_nn(rows, odd).astype(BF16)
        aux_ref[here] = dot_nt(both, aux_plain) + dot_nt((first - second).astype(BF16), aux_signed)


def windows(pairs, per_expert):
    return min(per_expert + 16, pairs)


def window_of(offset_ref, expert, pairs, window):
    first = offset_ref[expert]
    start = pl.multiple_of(jnp.minimum(first // 16 * 16, pairs - window), 16)
    rows = lax.broadcasted_iota(jnp.int32, (window, 1), 0) + start
    return pl.ds(start, window), (rows >= first) & (rows < offset_ref[expert + 1])


def gate_kernel(count_parts, begin, columns, tail, window, offset_ref, order_ref, *refs):
    first = count_parts > 0
    if first:
        parts, refs = refs[:count_parts], refs[count_parts:]
        hid_ref, norm_ref, router_ref, line_ref, tail_ref, w_ref, _ = refs[:7]
        keep_ref, send_ref, resid_ref, spread_ref, held, aux, w_held, w_sems, tail_held, tail_sem = refs[7:]
    else:
        spread_ref, w_ref, _, keep_ref, send_ref, held, w_held, w_sems = refs
    experts = w_ref.shape[0]
    pairs = spread_ref.shape[1]
    width = spread_ref.shape[2] // 2
    copies = [
        pltpu.make_async_copy(w_ref.at[e, :, :, pl.ds(begin, columns)], w_held.at[e % SLOTS], w_sems.at[e % SLOTS])
        for e in range(experts)
    ]
    for copy in copies[:SLOTS]:
        copy.start()
    if first:
        tail_width, _, aux_at, size = tail
        tail_copy = pltpu.make_async_copy(tail_ref, tail_held, tail_sem)
        tail_copy.start()
        dispatch(parts, hid_ref, norm_ref, router_ref, line_ref, resid_ref, spread_ref, aux, aux_at % LANES)
        tail_copy.wait()

    for expert in range(experts):
        rows, valid = window_of(offset_ref, expert, pairs, window)
        left = jnp.concatenate([spread_ref[0, rows], spread_ref[1, rows]], axis=0)
        copies[expert].wait()
        result = dot_nn(left, w_held[expert % SLOTS].reshape(2 * width, columns)).astype(BF16)
        if expert + SLOTS < experts:
            copies[expert + SLOTS].start()
        held[rows, :columns] = jnp.where(valid, result[:window], held[rows, :columns])
        held[rows, columns : 2 * columns] = jnp.where(
            valid, result[window:], held[rows, columns : 2 * columns]
        )
        if first:
            result = dot_nn(left, tail_held[expert])
            lane = lax.broadcasted_iota(jnp.int32, (window, LANES), 1)
            gate, up = result[:window], result[window:]
            if tail_width == LANES:
                block = jnp.where(lane < size, gate, pltpu.roll(up, size, 1))
                block = jnp.where(lane < 2 * size, block, aux[rows])
            else:
                block = jnp.concatenate([gate, up, aux[rows]], axis=1)
            here = slice(2 * columns, 2 * columns + tail_width)
            held[rows, here] = jnp.where(valid, block.astype(BF16), held[rows, here])

    half, block, _ = keep_ref.shape
    for slot in range(half):
        mine = pl.ds(pl.multiple_of(order_ref[slot] * block, block), block)
        other = pl.ds(pl.multiple_of(order_ref[half + slot] * block, block), block)
        keep_ref[slot] = held[mine]
        send_ref[slot] = held[other]


def gate_tail_kernel(size, gate_ref, _, out_ref):
    experts, width, _, lanes = gate_ref.shape
    lane = lax.broadcasted_iota(jnp.int32, (2 * width, lanes), 1)
    for e in range(experts):
        out_ref[e] = jnp.where(lane < size, gate_ref[e].reshape(2 * width, lanes).astype(F32), 0.0).astype(BF16)


def down_tail_kernel(size, down_ref, _, out_ref):
    lane = lax.broadcasted_iota(jnp.int32, down_ref.shape[1:], 1)
    for e in range(down_ref.shape[0]):
        out_ref[e] = jnp.where(lane < size, down_ref[e].astype(F32), 0.0).astype(BF16)


def last_units(weights, after, kernel, rows, name):
    number, size = weights.shape[-1] // LANES, weights.shape[-1] % LANES
    lead = weights.shape[:-1]
    out = (weights.shape[0], rows, LANES)
    return pl.pallas_call(
        functools.partial(kernel, size),
        grid=(1,),
        in_specs=[
            pl.BlockSpec((*lead, LANES), lambda *_: (0,) * len(lead) + (number,)),
            pl.BlockSpec(memory_space=pl.ANY),
        ],
        out_specs=full_spec(out),
        out_shape=jax.ShapeDtypeStruct(out, BF16),
        compiler_params=params(),
        cost_estimate=pl.CostEstimate(flops=0, bytes_accessed=4 * out[0] * rows * LANES, transcendentals=0),
        name=name,
    )(weights, after)


def tail_layout(units):
    size = units % LANES
    if 2 * size + 2 * PIECES <= LANES:
        return LANES, size, 2 * size, size
    return 3 * LANES, LANES, 2 * LANES, size


def sum_kernel(aux_at, groups, keep_ref, recv_ref, _, *outs):
    outs = outs[-len(groups) :]
    width = keep_ref.shape[2]

    def added(slot):
        total = keep_ref[slot].astype(F32) + recv_ref[slot].astype(F32)
        if aux_at is None:
            return [(slice(0, width), total)]
        base = aux_at // LANES * LANES
        tile = total[:, base : base + LANES]
        lane = lax.broadcasted_iota(jnp.int32, tile.shape, 1)
        for start in (aux_at - base, aux_at - base + PIECES):
            value = tile[:, start : start + 1]
            for k in range(1, PIECES):
                value = value + tile[:, start + k : start + k + 1]
            for k, piece in enumerate(split_bf16(value)):
                tile = jnp.where(lane == start + k, piece, tile)
        spans = [(slice(base, base + LANES), tile)]
        if base:
            spans.append((slice(0, base), total[:, :base]))
        if base + LANES < width:
            spans.append((slice(base + LANES, width), total[:, base + LANES :]))
        return spans

    for group, out in zip(groups, outs):
        for k, slot in enumerate(group):
            for span, value in added(slot):
                out[k, :, span] = value.astype(BF16)


def sum_parts(keep, recv, groups, aux_at, name, after=None, hold=None):
    _, block, width = keep.shape
    outs = [jax.ShapeDtypeStruct((len(group), block, width), BF16) for group in groups]
    in_specs = [full_spec(keep.shape)] * 2 + [pl.BlockSpec(memory_space=pl.ANY)]
    out_specs = [full_spec(out.shape) for out in outs]
    operands = [keep, recv, keep if after is None else after]
    aliases = {}
    if hold is not None:
        operands.append(hold)
        in_specs.append(pl.BlockSpec(memory_space=pl.ANY))
        outs.insert(0, jax.ShapeDtypeStruct(hold.shape, hold.dtype))
        out_specs.insert(0, pl.BlockSpec(memory_space=pl.ANY))
        aliases = {3: 0}
    return pl.pallas_call(
        functools.partial(sum_kernel, aux_at, groups),
        grid=(1,),
        in_specs=in_specs,
        out_specs=out_specs,
        out_shape=outs,
        input_output_aliases=aliases,
        compiler_params=params(),
        cost_estimate=pl.CostEstimate(flops=keep.size, bytes_accessed=6 * keep.size, transcendentals=0),
        name=name,
    )(*operands)


def halves(count):
    return [list(range(0, count, 2)), list(range(1, count, 2))] if count > 1 else [[0]]


def act_kernel(count_parts, columns, tail, features, *refs):
    parts, refs = refs[:count_parts], refs[count_parts:]
    total = parts[0][0].astype(F32)
    for part in parts[1:]:
        total = total + part[0].astype(F32)
    if tail is None:
        stat_ref, _, act_ref = refs
        inverse, weight = stat_ref[:, 0:1], stat_ref[:, 1:2]
    else:
        _, act_ref, stat_ref = refs
        tail_width, up_at, aux_at, size = tail
        base = 2 * columns + aux_at
        squares = total[:, base : base + 1]
        gap = total[:, base + PIECES : base + PIECES + 1]
        for k in range(1, PIECES):
            squares = squares + total[:, base + k : base + k + 1]
            gap = gap + total[:, base + PIECES + k : base + PIECES + k + 1]
        inverse = lax.rsqrt(squares / features + 1e-06)
        weight = 1.0 / (1.0 + jnp.exp(-gap * inverse))
        lane = lax.broadcasted_iota(jnp.int32, (total.shape[0], LANES), 1)
        stat_ref[...] = jnp.where(lane == 0, inverse, weight)

    def activate(gate, up):
        gate = gate * inverse
        return gate / (1.0 + jnp.exp(-gate)) * (up * inverse) * weight

    act_ref[:, :columns] = activate(total[:, :columns], total[:, columns : 2 * columns]).astype(BF16)
    if tail is not None:
        block = total[:, 2 * columns : 2 * columns + LANES]
        if tail_width == LANES:
            up = pltpu.roll(block, LANES - size, 1)
        else:
            up = total[:, 2 * columns + LANES : 2 * columns + 2 * LANES]
        last = jnp.where(lane < size, activate(block, up), 0.0)
        act_ref[:, columns:] = last.astype(BF16)


def activation(parts, stats, columns, tail, features, name, after):
    rows = parts[0].shape[1]
    out = jax.ShapeDtypeStruct((rows, columns + (LANES if tail else 0)), BF16)
    stat = jax.ShapeDtypeStruct((rows, LANES), F32)
    operands = [*parts] + ([] if tail else [stats])
    outs = [out, stat] if tail else [out]
    in_specs = [full_spec(x.shape) for x in operands] + [pl.BlockSpec(memory_space=pl.ANY)]
    result = pl.pallas_call(
        functools.partial(act_kernel, len(parts), columns, tail, features),
        grid=(1,),
        in_specs=in_specs,
        out_specs=[full_spec(x.shape) for x in outs],
        out_shape=outs,
        compiler_params=params(),
        cost_estimate=pl.CostEstimate(
            flops=16 * rows * columns, bytes_accessed=20 * rows * columns, transcendentals=rows * columns
        ),
        name=name,
    )(*operands, after)
    return (result[0], result[1]) if tail else (result[0], stats)


def down_kernel(count_parts, begin, columns, tail, window, begins, ends, offset_ref, order_ref, *refs):
    parts, refs = refs[:count_parts], refs[count_parts:]
    other_ref, w_ref, _, refs = refs[0], refs[1], refs[2], refs[3:]
    if tail:
        tail_ref, refs = refs[0], refs[1:]
    if not begins:
        before_ref, refs = refs[0], refs[1:]
    if ends:
        place_ref, resid_ref, out_ref, total_ref, held, w_held, w_sems = refs
    else:
        total_ref, held, w_held, w_sems = refs
    block = parts[0].shape[0]
    half = len(parts)
    pairs = held.shape[0]
    experts = w_ref.shape[0]
    copies = [
        pltpu.make_async_copy(w_ref.at[e, :, pl.ds(begin, columns)], w_held.at[e % SLOTS], w_sems.at[e % SLOTS])
        for e in range(experts)
    ]
    for copy in copies[:SLOTS]:
        copy.start()
    for slot in range(half):
        mine = pl.ds(pl.multiple_of(order_ref[slot] * block, block), block)
        other = pl.ds(pl.multiple_of(order_ref[half + slot] * block, block), block)
        held[mine] = parts[slot][...]
        held[other] = other_ref[slot]
    total_ref[...] = jnp.zeros_like(total_ref) if begins else before_ref[...]
    for expert in range(experts):
        rows, valid = window_of(offset_ref, expert, pairs, window)
        copies[expert].wait()
        result = dot_nt(held[rows, :columns], w_held[expert % SLOTS])
        if expert + SLOTS < experts:
            copies[expert + SLOTS].start()
        if tail:
            result = result + dot_nt(held[rows, columns:], tail_ref[expert])
        total_ref[rows] = total_ref[rows] + jnp.where(valid, result, 0.0)

    if ends:
        total = out_ref.shape[0]
        pieces = [x.astype(BF16) for x in split_bf16(total_ref[...], 2)]
        resid = [x.astype(BF16) for x in split_bf16(resid_ref[...], 2)]
        step = pair_block(total) if total > 256 else total
        step = min(step, 256)
        for start in range(0, total, step):
            here = slice(start, start + step)
            pair = lax.broadcasted_iota(jnp.int32, (step, pairs), 1)
            place = place_ref[here].astype(jnp.int32)
            pick = (pair == place[:, 0:1]) | (pair == place[:, 1:2])
            pick = pick.astype(F32).astype(BF16)
            token = lax.broadcasted_iota(jnp.int32, (step, total), 1)
            move = (token == place[:, 2:3]).astype(F32).astype(BF16)
            result = dot_nn(pick, pieces[0]) + dot_nn(pick, pieces[1])
            result = result + dot_nt(move, resid[0]) + dot_nt(move, resid[1])
            out_ref[here] = result.astype(BF16)


def chunk_columns(units):
    full = units // LANES
    count = 3 if full >= 6 else 1
    ends = [full * (k + 1) // count for k in range(count)]
    return [(LANES * (e - n), LANES * n) for e, n in zip(ends, [b - a for a, b in zip([0, *ends], ends)])]


def local(
    hidden_in,
    cache_pool,
    project_in,
    project_out,
    norm_first,
    norm_second,
    router,
    gate_up,
    expert_down,
    lengths,
    prompt_pages,
    own_pages,
    groups,
    move_target,
    routes,
):
    dp = lax.axis_size("dp")
    fs = lax.axis_size("fsdp")
    half = dp // 2
    my_row = lax.axis_index("dp")
    my_column = lax.axis_index("fsdp")
    my_chip, my_core = my_row // 2, my_row % 2
    req, features = hidden_in.shape
    row = req * fs
    total = row * dp
    pairs = 2 * total
    width = project_in.shape[0]
    cols = cache_pool.shape[3]
    heads = cols // HD
    page_len = cache_pool.shape[1]
    movers = move_target.shape[1]
    staying = row - movers
    experts = router.shape[1]
    units = gate_up.shape[3]
    window = windows(pairs, CAP * dp * fs)

    gate_up = pltpu.with_memory_space_constraint(gate_up, pltpu.HBM)
    expert_down = pltpu.with_memory_space_constraint(expert_down, pltpu.HBM)

    chip = jnp.arange(half, dtype=jnp.int32)
    row_ids = jnp.arange(dp, dtype=jnp.int32)
    order = jnp.concatenate([(chip ^ my_chip) * 2 + my_core, (chip ^ my_chip) * 2 + 1 - my_core])

    def swap(x):
        return lax.ppermute(x, "dp", [(i, i ^ 1) for i in range(dp)])

    def over_chips(x, s):
        return lax.ppermute(x, "dp", [(i, i ^ (2 * s)) for i in range(dp)])

    def over_columns(x, s):
        return lax.ppermute(x, "fsdp", [(i, i ^ s) for i in range(fs)])

    payload = pack(hidden_in, routes.T, dp, fs)
    recv = lax.all_to_all(
        payload.reshape(dp * fs, req, payload.shape[3]), ("dp", "fsdp"), 0, 0, tiled=True
    ).reshape(total, payload.shape[3])

    row_lengths = lax.dynamic_slice_in_dim(lengths, my_row * row, row)
    lists = jnp.concatenate([own_pages, groups[:, None], row_lengths[:, None]], axis=1)
    lane = jnp.arange(cols, dtype=jnp.int32)
    channel = (lane % (HD // 2)).astype(F32)
    inverse = jnp.exp(-jnp.log(10000.0) * 2.0 * channel / HD)
    angles = row_lengths.astype(F32)[:, None] * inverse[None, :]
    cosine = jnp.cos(angles)
    sine = jnp.where((lane % HD < HD // 2)[None, :], -1.0, 1.0) * jnp.sin(angles)

    def slice_of(vector):
        return lax.dynamic_slice_in_dim(vector, my_row * width, width)

    keys, values, bias = split_pool(prompt_pages, lists, cache_pool, payload)
    keep, send, raw = project_qkv(
        order,
        recv,
        slice_of(norm_first).astype(F32)[None, :],
        project_in.transpose(1, 0, 2),
        half,
        row,
        bias,
    )
    sums = sum_parts(keep, swap(send), [[s] for s in range(half)], None, "core_sum_qkv")
    slot_of = (row_ids % 2 ^ my_core) * half + (row_ids // 2 ^ my_chip)
    column = jnp.stack([my_column, jnp.int32(fs)]).astype(jnp.int32)
    offsets, place_table, line_table = pair_places(
        move_target, order, slot_of, column, recv, sums[0], experts, width
    )
    gate_tail = last_units(gate_up, place_table, gate_tail_kernel, 2 * width, "gate_tail")
    parts = [sums[0]] + [over_chips(sums[s], s) for s in range(1, half)]
    heads_out = attend(parts, cosine, sine, bias, keys, values, gate_tail)

    parts = [heads_out] + [over_chips(heads_out, s) for s in range(1, half)]
    other = swap(jnp.concatenate(parts, axis=0))
    projected = project_heads(parts, other, project_out.T)
    parts = [projected] + [over_columns(projected, s) for s in range(1, fs)]

    chunks = chunk_columns(units)
    tail = tail_layout(units)
    block = pairs // dp
    hbm = pl.BlockSpec(memory_space=pltpu.HBM)
    anywhere = pl.BlockSpec(memory_space=pl.ANY)
    spread = jax.ShapeDtypeStruct((2, pairs, 2 * width), BF16)
    resid_shape = jax.ShapeDtypeStruct((width, total), F32)
    norm_column = slice_of(norm_second).astype(F32)[:, None]
    router_slice = lax.dynamic_slice_in_dim(router, my_row * width, width).T
    state = {"after": line_table}

    def gate(index):
        begin, columns = chunks[index]
        first = index == 0
        out_width = 2 * columns + (tail[0] if first else 0)
        half_out = jax.ShapeDtypeStruct((half, block, out_width), BF16)
        scratch = [pltpu.VMEM((pairs, out_width), BF16)]
        weights = [pltpu.VMEM((SLOTS, width, 2, columns), BF16), pltpu.SemaphoreType.DMA((SLOTS,))]
        if first:
            operands = [*parts, raw.T, norm_column, router_slice, line_table]
            in_specs = [full_spec(x.shape) for x in operands] + [hbm]
            operands.append(gate_tail)
            outs = [half_out, half_out, resid_shape, spread]
            scratch += [pltpu.VMEM((pairs, LANES), F32), *weights]
            scratch += [pltpu.VMEM(gate_tail.shape, BF16), pltpu.SemaphoreType.DMA]
        else:
            operands = [state["spread"]]
            in_specs = [full_spec(spread.shape)]
            outs = [half_out, half_out]
            scratch += weights
        result = pl.pallas_call(
            functools.partial(gate_kernel, len(parts) if first else 0, begin, columns, tail, window),
            grid_spec=pltpu.PrefetchScalarGridSpec(
                num_scalar_prefetch=2,
                grid=(1,),
                in_specs=[*in_specs, anywhere, anywhere],
                out_specs=[full_spec(x.shape) for x in outs],
                scratch_shapes=scratch,
            ),
            out_shape=outs,
            compiler_params=params(room(total)),
            cost_estimate=pl.CostEstimate(
                flops=8 * experts * window * width * columns,
                bytes_accessed=4 * experts * width * columns,
                transcendentals=0,
            ),
            name=f"gate_up_{index}",
        )(offsets, order, *operands, gate_up, state["after"])
        if first:
            state["resid"], state["spread"] = result[2:]
        state["after"] = result[0]
        return result[:2]

    def combine(index, bit, held, hold=None):
        aux_at = 2 * chunks[index][1] + tail[2] if index == 0 else None
        sums = sum_parts(
            *held, halves(held[0].shape[0]), aux_at, f"sum_{index}_{bit}", state["after"], hold
        )
        kept, sent = sums[-2:]
        state["after"] = kept
        return [kept, over_chips(sent, 1 << bit)], sums[0]

    def activate(index, held):
        act, state["stats"] = activation(
            held,
            state.get("stats"),
            chunks[index][1],
            tail if index == 0 else None,
            float(features),
            f"activation_{index}",
            state["after"],
        )
        state["after"] = act
        parts = {0: act}
        for bit in reversed(range(stages)):
            parts.update({s | 1 << bit: over_chips(x, 1 << bit) for s, x in list(parts.items())})
        return [parts[s] for s in range(half)]

    def down(index, parts):
        begin, columns = chunks[index]
        first, last = index == 0, index == len(chunks) - 1
        operands = [*parts, swap(jnp.stack(parts))]
        in_specs = [full_spec(x.shape) for x in operands] + [anywhere, anywhere]
        operands += [expert_down, state["after"]]
        if first:
            operands.append(state["tail"])
            in_specs.append(full_spec(state["tail"].shape))
        else:
            operands.append(state["sum"])
            in_specs.append(full_spec(state["sum"].shape))
        sum_shape = jax.ShapeDtypeStruct((pairs, width), F32)
        scratch = [
            pltpu.VMEM((pairs, parts[0].shape[1]), BF16),
            pltpu.VMEM((SLOTS, width, columns), BF16),
            pltpu.SemaphoreType.DMA((SLOTS,)),
        ]
        outs = [sum_shape]
        if last:
            operands += [place_table, state["resid"]]
            in_specs += [full_spec(place_table.shape), full_spec(state["resid"].shape)]
            outs = [jax.ShapeDtypeStruct((total, width), BF16)]
            scratch = [pltpu.VMEM(sum_shape.shape, F32)] + scratch
        result = pl.pallas_call(
            functools.partial(
                down_kernel, len(parts), begin, columns, tail if first else None, window, first, last
            ),
            grid_spec=pltpu.PrefetchScalarGridSpec(
                num_scalar_prefetch=2,
                grid=(1,),
                in_specs=in_specs,
                out_specs=[full_spec(x.shape) for x in outs],
                scratch_shapes=scratch,
            ),
            out_shape=outs,
            compiler_params=params(room(total)),
            cost_estimate=pl.CostEstimate(
                flops=2 * experts * window * width * columns,
                bytes_accessed=2 * experts * width * columns,
                transcendentals=0,
            ),
            name=f"down_{index}",
        )(offsets, order, *operands)[0]
        state["sum"] = state["after"] = result
        return result

    stages = half.bit_length() - 1
    count = len(chunks)
    held, gathered = {}, {}
    for step in range(count + stages + 3):
        sent = None
        if step < count:
            kept, sent = gate(step)
        if step == count - 1:
            state["tail"] = last_units(expert_down, state["after"], down_tail_kernel, width, "down_tail")
        for k in range(count):
            if step - k == stages + 2:
                result = down(k, gathered[k])
        for k in range(count):
            if step >= count and step - k == stages:
                gathered[k] = activate(k, held[k])
        for k in range(count):
            if 1 <= step - k < stages:
                held[k], through = combine(k, step - k, held[k], sent)
                sent = None if sent is None else through
        if step < count:
            held[step], _ = combine(step, 0, [kept, swap(sent)])
        for k in range(count):
            if step < count and step - k == stages:
                gathered[k] = activate(k, held[k])

    back = lax.all_to_all(result.reshape(dp * fs, req, width), ("dp", "fsdp"), 0, 0, tiled=True)
    back = back.reshape(dp, fs, req, width).astype(F32)
    return jnp.sum(back, axis=1).transpose(1, 0, 2).reshape(req, features).astype(BF16)


def solution(mesh):
    placed = (
        P(("dp", "fsdp"), None),
        P("dp", None, None, "fsdp"),
        P("dp", None, "fsdp"),
        P("fsdp", "dp"),
        P(),
        P(),
        P(),
        P(None, "dp", None, "fsdp"),
        P(None, "dp", "fsdp"),
        P(),
        P("dp", None),
        P("dp", None),
        P("dp"),
        P(),
        P(("dp", "fsdp"), None),
    )
    return jax.shard_map(
        local, mesh=mesh, in_specs=placed, out_specs=P(("dp", "fsdp"), None), check_vma=False
    )
```

```python
import functools

import jax
import jax.numpy as jnp
from jax import lax
from jax.experimental import pallas as pl
from jax.experimental.pallas import tpu as pltpu
from jax.sharding import PartitionSpec as P

HD = 64
CAP = 4
PIECES = 3
LANES = 128
BF16 = jnp.bfloat16
F32 = jnp.float32
FAR = -3.0e38
SMALL, ATTENTION, LARGE = 16, 24, 60
SLOTS = 8


def params(mib=SMALL):
    return pltpu.CompilerParams(vmem_limit_bytes=mib * 2**20)


def room(tokens):
    return SMALL if tokens <= 512 else LARGE


def dot_nn(a, b):
    return lax.dot_general(a, b, (((1,), (0,)), ((), ())), preferred_element_type=F32)


def dot_nt(a, b):
    return lax.dot_general(a, b, (((1,), (1,)), ((), ())), preferred_element_type=F32)


def split_bf16(value, count=PIECES):
    pieces = []
    for _ in range(count):
        piece = value.astype(BF16).astype(F32)
        pieces.append(piece)
        value = value - piece
    return pieces


def full_spec(shape):
    return pl.BlockSpec(memory_space=pltpu.VMEM)


def block_spec(shape):
    zeros = (0,) * len(shape)
    return pl.BlockSpec(tuple(shape), lambda *_: zeros)


SCALARS = pl.BlockSpec(memory_space=pltpu.SMEM)


def pack_kernel(hidden_ref, routes_ref, out_ref):
    slices, copies, req, room = out_ref.shape
    features = hidden_ref.shape[1]
    width = features // slices
    values = hidden_ref[...].astype(F32)
    factor = lax.rsqrt(jnp.mean(values * values, axis=1, keepdims=True) + 1e-06)
    lane = lax.broadcasted_iota(jnp.int32, (req, room), 1)
    extra = jnp.zeros((req, room), F32)
    for k, piece in enumerate(split_bf16(factor)):
        extra = jnp.where(lane == width + k, piece, extra)
    spot = lax.broadcasted_iota(jnp.int32, (req, req), 1) == lax.broadcasted_iota(jnp.int32, (req, req), 0)
    for k in range(2):
        route = jnp.sum(jnp.where(spot, routes_ref[k : k + 1].astype(F32), 0.0), axis=1, keepdims=True)
        extra = jnp.where(lane == width + PIECES + k, route, extra)
    for index in range(slices):
        moved = pltpu.roll(values, (features - index * width) % features, 1) if index else values
        block = jnp.where(lane < width, moved[:, :room], extra).astype(BF16)
        for copy in range(copies):
            out_ref[index, copy] = block


def pack(hidden_in, routes, slices, copies):
    req, features = hidden_in.shape
    width = features // slices
    room = -(-(width + PIECES + 2) // LANES) * LANES
    out = (slices, copies, req, room)
    return pl.pallas_call(
        pack_kernel,
        in_specs=[full_spec(hidden_in.shape), full_spec(routes.shape)],
        out_specs=full_spec(out),
        out_shape=jax.ShapeDtypeStruct(out, BF16),
        compiler_params=params(),
        cost_estimate=pl.CostEstimate(flops=1, bytes_accessed=1, transcendentals=0),
        name="pack",
    )(hidden_in, routes)


def places_kernel(
    experts, width, staying, move_ref, order_ref, slot_ref, column_ref, recv_ref, _, off_ref, place_ref, line_ref, table, slots
):
    total = recv_ref.shape[0]
    rows_count, movers = move_ref.shape
    row = total // rows_count
    block = min(total, 256)
    lane = lax.broadcasted_iota(jnp.int32, (block, LANES), 1)
    above = lax.broadcasted_iota(jnp.int32, (block, block), 0)
    beside = lax.broadcasted_iota(jnp.int32, (block, block), 1)
    before = (beside < above).astype(F32).astype(BF16)
    counts = jnp.zeros((1, LANES), F32)
    for start in range(0, total, block):
        here = slice(start, start + block)
        first = recv_ref[here, width + PIECES : width + PIECES + 1].astype(F32).astype(jnp.int32)
        second = recv_ref[here, width + PIECES + 1 : width + PIECES + 2].astype(F32).astype(jnp.int32)
        member = (lane == first).astype(F32) + (lane == second).astype(F32)
        rank = dot_nn(before, member.astype(BF16)) + counts
        counts = counts + jnp.sum(member, axis=0, keepdims=True)
        mine = jnp.sum(jnp.where(lane == first, rank, 0.0), axis=1, keepdims=True)
        other = jnp.sum(jnp.where(lane == second, rank, 0.0), axis=1, keepdims=True)
        block_table = jnp.where(lane == 0, mine, jnp.where(lane == 1, other, 0.0))
        block_table = jnp.where(lane == 2, first.astype(F32), block_table)
        table[here] = jnp.where(lane == 3, second.astype(F32), block_table)
    single = lax.broadcasted_iota(jnp.int32, (1, LANES), 1)
    sums = [jnp.sum(jnp.where(single == e, counts, 0.0)) for e in range(experts)]
    off_ref[0] = 0
    running = jnp.float32(0.0)
    begins = jnp.zeros((1, LANES), F32)
    for e in range(experts):
        begins = jnp.where(single == e, running, begins)
        running = running + sums[e]
        off_ref[e + 1] = running.astype(jnp.int32)
    for start in range(0, total, block):
        here = slice(start, start + block)
        values = table[here]
        first = values[:, 2:3].astype(jnp.int32)
        second = values[:, 3:4].astype(jnp.int32)
        begin_first = jnp.sum(jnp.where(lane == first, begins, 0.0), axis=1, keepdims=True)
        begin_second = jnp.sum(jnp.where(lane == second, begins, 0.0), axis=1, keepdims=True)
        values = values + jnp.where(lane == 0, begin_first, jnp.where(lane == 1, begin_second, 0.0))
        table[here] = values
        place_ref[here] = values
    within = lax.broadcasted_iota(jnp.int32, (row, LANES), 0)
    wide = lax.broadcasted_iota(jnp.int32, (row, LANES), 1)
    req = row // column_ref[1]
    mine = (within >= column_ref[0] * req) & (within < (column_ref[0] + 1) * req)
    for r in range(rows_count):
        here = slice(r * row, (r + 1) * row)
        lies = jnp.where(mine, (within + slot_ref[r] * row).astype(F32), -1.0)
        place_ref[here] = jnp.where(wide == 2, lies, place_ref[here])
    for r in range(rows_count):
        for j in range(movers):
            at = staying + j
            target = pl.ds(move_ref[r, j] * row + at, 1)
            held = (at >= column_ref[0] * req) & (at < (column_ref[0] + 1) * req)
            lies = jnp.where(held, slot_ref[r] * row + at, -1).astype(F32)
            place_ref[target] = jnp.where(single == 2, lies, place_ref[target])
    for b in range(rows_count):
        slots[b * row : (b + 1) * row] = table[pl.ds(pl.multiple_of(order_ref[b] * row, row), row)]
        for j in range(movers):
            at = staying + j
            source = pl.ds(move_ref[order_ref[b], j] * row + at, 1)
            slots[b * row + at : b * row + at + 1] = table[source]
    line_ref[...] = slots[...].T[:8]


def pair_places(move_target, order, slot_of, column, recv, after, experts, width):
    total = recv.shape[0]
    rows_count, movers = move_target.shape
    staying = total // rows_count - movers
    outs = [
        jax.ShapeDtypeStruct((experts + 1,), jnp.int32),
        jax.ShapeDtypeStruct((total, LANES), F32),
        jax.ShapeDtypeStruct((8, total), F32),
    ]
    return pl.pallas_call(
        functools.partial(places_kernel, experts, width, staying),
        in_specs=[SCALARS] * 4 + [full_spec(recv.shape), pl.BlockSpec(memory_space=pl.ANY)],
        out_specs=[
            pl.BlockSpec(memory_space=pltpu.SMEM),
            full_spec(outs[1].shape),
            full_spec(outs[2].shape),
        ],
        scratch_shapes=[pltpu.VMEM((total, LANES), F32), pltpu.VMEM((total, LANES), F32)],
        out_shape=outs,
        compiler_params=params(room(total)),
        cost_estimate=pl.CostEstimate(flops=1, bytes_accessed=1, transcendentals=0),
        name="pair_places",
    )(move_target, order, slot_of, column, recv, after)


def pool_kernel(prompt_ref, lists_ref, pool_ref, _, key_ref, value_ref, bias_ref):
    pages, page_len, _, cols = pool_ref.shape
    rows = pages * page_len
    both = pool_ref[...].reshape(2 * rows, cols)
    part = min(rows, LANES)
    wide = lax.broadcasted_iota(jnp.int32, (part, 2 * part), 1)
    high = lax.broadcasted_iota(jnp.int32, (part, 2 * part), 0)
    even = (wide == 2 * high).astype(F32).astype(BF16)
    odd = (wide == 2 * high + 1).astype(F32).astype(BF16)
    for start in range(0, rows, part):
        piece = both[2 * start : 2 * (start + part)]
        key_ref[start : start + part] = dot_nn(even, piece).astype(BF16)
        value_ref[start : start + part] = dot_nn(odd, piece).astype(BF16)
    requests = bias_ref.shape[0]
    prompts, prompt_len = prompt_ref.shape
    own_len = lists_ref.shape[1] - 2
    group, length = lists_ref[:, own_len : own_len + 1], lists_ref[:, own_len + 1 :]
    spot = lax.broadcasted_iota(jnp.int32, (requests, rows), 1)
    page = spot // page_len + pl.program_id(0) * pages
    reach = jnp.zeros((requests, rows), jnp.int32)
    for k in range(prompt_len):
        listed = jnp.zeros((requests, 1), jnp.int32)
        for g in range(prompts):
            listed = jnp.where(group == g, prompt_ref[g, k], listed)
        reach = jnp.where(page == listed, length - page_len * k, reach)
    for k in range(own_len):
        reach = jnp.where(page == lists_ref[:, k : k + 1], length - page_len * (prompt_len + k), reach)
    bias_ref[...] = jnp.where(spot % page_len < reach, 0.0, FAR)


def split_pool(prompt_pages, lists, cache_pool, after):
    pages, page_len, _, cols = cache_pool.shape
    requests = lists.shape[0]
    block = next(b for b in (16, 8, 4, 2, 1) if pages % b == 0)
    out = jax.ShapeDtypeStruct((pages * page_len, cols), BF16)
    spec = pl.BlockSpec((block * page_len, cols), lambda b, *_: (b, 0))
    return pl.pallas_call(
        pool_kernel,
        grid_spec=pltpu.PrefetchScalarGridSpec(
            num_scalar_prefetch=1,
            grid=(pages // block,),
            in_specs=[
                block_spec(lists.shape),
                pl.BlockSpec((block, page_len, 2, cols), lambda b, *_: (b, 0, 0, 0)),
                pl.BlockSpec(memory_space=pl.ANY),
            ],
            out_specs=[spec, spec, pl.BlockSpec((requests, block * page_len), lambda b, *_: (0, b))],
        ),
        out_shape=[out, out, jax.ShapeDtypeStruct((requests, pages * page_len), F32)],
        compiler_params=params(),
        cost_estimate=pl.CostEstimate(flops=1, bytes_accessed=1, transcendentals=0),
        name="pool_split",
    )(prompt_pages, lists, cache_pool, after)


def qkv_kernel(order_ref, recv_ref, norm_ref, w_ref, _, keep_ref, send_ref, raw_ref, normed, slots):
    width = norm_ref.shape[1]
    half, row, _ = keep_ref.shape
    cols = w_ref.shape[2]
    values = recv_ref[:, :width]
    scale = recv_ref[:, width : width + 1].astype(F32)
    for piece in range(1, PIECES):
        scale = scale + recv_ref[:, width + piece : width + piece + 1].astype(F32)
    normed[...] = (values.astype(F32) * scale * norm_ref[...]).astype(BF16)
    for slot in range(2 * half):
        rows = pl.ds(pl.multiple_of(order_ref[slot] * row, row), row)
        slots[slot * row : (slot + 1) * row] = normed[rows]
        raw_ref[slot * row : (slot + 1) * row] = recv_ref[rows, :width]
    for part in range(3):
        here = slice(part * cols, (part + 1) * cols)
        result = dot_nn(slots[...], w_ref[part]).astype(BF16).reshape(2 * half, row, cols)
        keep_ref[:, :, here] = result[:half]
        send_ref[:, :, here] = result[half:]


def project_qkv(order, recv, norm_slice, weights, half, row, after):
    total, _ = recv.shape
    width, cols = weights.shape[1:]
    out = jax.ShapeDtypeStruct((half, row, 3 * cols), BF16)
    raw = jax.ShapeDtypeStruct((total, width), BF16)
    return pl.pallas_call(
        qkv_kernel,
        in_specs=[SCALARS] * 1 + [full_spec(x.shape) for x in (recv, norm_slice, weights)] + [pl.BlockSpec(memory_space=pl.ANY)],
        out_specs=[full_spec(out.shape), full_spec(out.shape), full_spec(raw.shape)],
        scratch_shapes=[pltpu.VMEM((total, width), BF16), pltpu.VMEM((total, width), BF16)],
        out_shape=[out, out, raw],
        compiler_params=params(room(total)),
        cost_estimate=pl.CostEstimate(flops=1, bytes_accessed=1, transcendentals=0),
        name="qkv",
    )(order, recv, norm_slice, weights, after)


def attention_kernel(*refs):
    parts, refs = refs[:-9], refs[-9:]
    cos_ref, sin_ref, bias_ref, key_ref, value_ref, _, out_ref, scores, probs = refs
    row, cols = out_ref.shape
    heads = cols // HD
    total = parts[0][0].astype(F32)
    for part in parts[1:]:
        total = total + part[0].astype(F32)
    lane = lax.broadcasted_iota(jnp.int32, (row, cols), 1)
    first_half = lane % HD < HD // 2

    def rotate(values):
        partner = jnp.where(
            first_half, pltpu.roll(values, cols - HD // 2, 1), pltpu.roll(values, HD // 2, 1)
        )
        return (values * cos_ref[...] + partner * sin_ref[...]).astype(BF16)

    query = rotate(total[:, :cols]).astype(F32)
    key_new = rotate(total[:, cols : 2 * cols]).astype(F32)
    value_new = total[:, 2 * cols :].astype(BF16).astype(F32)
    spread = jnp.concatenate(
        [jnp.where(lane // HD == h, query, 0.0).astype(BF16) for h in range(heads)], axis=0
    )
    scores[...] = dot_nt(spread, key_ref[...])
    own_parts = []
    for h in range(heads):
        here = slice(h * row, (h + 1) * row)
        mine = lane // HD == h
        own = jnp.sum(jnp.where(mine, query * key_new, 0.0), axis=1, keepdims=True) * HD**-0.5
        score = scores[here] * HD**-0.5 + bias_ref[...]
        highest = jnp.maximum(jnp.max(score, axis=1, keepdims=True), own)
        weight = jnp.exp(score - highest)
        weight_own = jnp.exp(own - highest)
        inverse = 1.0 / (jnp.sum(weight, axis=1, keepdims=True) + weight_own)
        probs[here] = (weight * inverse).astype(BF16)
        own_parts.append((weight_own * inverse).astype(BF16).astype(F32))
    mixture = dot_nn(probs[...], value_ref[...])
    result = jnp.zeros((row, cols), F32)
    for h in range(heads):
        mixed = mixture[h * row : (h + 1) * row] + own_parts[h] * value_new
        result = jnp.where(lane // HD == h, mixed, result)
    out_ref[...] = result.astype(BF16)


def attend(parts, cosine, sine, bias, keys, values, after):
    row, cols = cosine.shape
    stretch = keys.shape[0]
    heads = cols // HD
    operands = [*parts, cosine, sine, bias, keys, values]
    return pl.pallas_call(
        attention_kernel,
        in_specs=[full_spec(x.shape) for x in operands] + [pl.BlockSpec(memory_space=pl.ANY)],
        out_specs=full_spec((row, cols)),
        out_shape=jax.ShapeDtypeStruct((row, cols), BF16),
        scratch_shapes=[
            pltpu.VMEM((heads * row, stretch), F32),
            pltpu.VMEM((heads * row, stretch), BF16),
        ],
        compiler_params=params(ATTENTION),
        cost_estimate=pl.CostEstimate(flops=1, bytes_accessed=1, transcendentals=0),
        name="attention",
    )(*operands, after)


def out_kernel(*refs):
    parts, (other_ref, w_ref, out_ref) = refs[:-3], refs[-3:]
    half = len(parts) * parts[0].shape[0]
    mine = jnp.concatenate([part[...] for part in parts], axis=0)
    out_ref[:, :half] = dot_nt(w_ref[...], mine).astype(BF16)
    out_ref[:, half:] = dot_nt(w_ref[...], other_ref[...]).astype(BF16)


def project_heads(parts, other, weights):
    half = other.shape[0]
    operands = [*parts, other, weights]
    out = (weights.shape[0], 2 * half)
    return pl.pallas_call(
        out_kernel,
        in_specs=[full_spec(x.shape) for x in operands],
        out_specs=full_spec(out),
        out_shape=jax.ShapeDtypeStruct(out, BF16),
        compiler_params=params(room(2 * half)),
        cost_estimate=pl.CostEstimate(flops=1, bytes_accessed=1, transcendentals=0),
        name="out_projection",
    )(*operands)


def pair_block(pairs):
    return next(b for b in (256, 128, 64, 32, 16) if pairs % b == 0)


def dispatch(parts, hid_ref, norm_ref, router_ref, line_ref, resid_ref, spread_ref, aux_ref, aux_at):
    width, total = hid_ref.shape
    pairs = spread_ref.shape[1]
    resid = hid_ref[...].astype(F32)
    for part in parts:
        resid = resid + part[...].astype(F32)
    resid_ref[...] = resid
    moe = (resid * norm_ref[...]).astype(BF16)
    squares = jnp.sum(resid * resid, axis=0, keepdims=True)
    logits = dot_nn(router_ref[...], moe)
    expert = lax.broadcasted_iota(jnp.int32, logits.shape, 0)
    line = line_ref[...].astype(jnp.int32)
    sign = (expert == line[2:3]).astype(F32) - (expert == line[3:4]).astype(F32)
    gap = jnp.sum(logits * sign, axis=0, keepdims=True)
    high = lax.broadcasted_iota(jnp.int32, (LANES, total), 0)
    aux_plain = jnp.zeros((LANES, total), F32)
    aux_signed = jnp.zeros((LANES, total), F32)
    for k, piece in enumerate(split_bf16(squares)):
        aux_plain = jnp.where(high == aux_at + k, piece, aux_plain)
    for k, piece in enumerate(split_bf16(gap)):
        aux_signed = jnp.where(high == aux_at + PIECES + k, piece, aux_signed)
    aux_plain = aux_plain.astype(BF16)
    aux_signed = aux_signed.astype(BF16)
    feature = lax.broadcasted_iota(jnp.int32, (width, 2 * width), 0)
    lane = lax.broadcasted_iota(jnp.int32, (width, 2 * width), 1)
    even = (lane == 2 * feature).astype(BF16)
    odd = (lane == 2 * feature + 1).astype(BF16)
    block = pair_block(pairs)
    for start in range(0, pairs, block):
        here = slice(start, start + block)
        pair = lax.broadcasted_iota(jnp.int32, (block, total), 0) + start
        first = (pair == line[0:1]).astype(F32)
        second = (pair == line[1:2]).astype(F32)
        both = (first + second).astype(BF16)
        rows = dot_nt(both, moe).astype(BF16)
        spread_ref[0, here] = dot_nn(rows, even).astype(BF16)
        spread_ref[1, here] = dot_nn(rows, odd).astype(BF16)
        aux_ref[here] = dot_nt(both, aux_plain) + dot_nt((first - second).astype(BF16), aux_signed)


def windows(pairs, per_expert):
    return min(per_expert + 16, pairs)


def window_of(offset_ref, expert, pairs, window):
    first = offset_ref[expert]
    start = pl.multiple_of(jnp.minimum(first // 16 * 16, pairs - window), 16)
    rows = lax.broadcasted_iota(jnp.int32, (window, 1), 0) + start
    return pl.ds(start, window), (rows >= first) & (rows < offset_ref[expert + 1])


def gate_kernel(count_parts, begin, columns, tail, window, waits, offset_ref, order_ref, *refs):
    first = count_parts > 0
    refs = refs[waits:]
    if first:
        parts, refs = refs[:count_parts], refs[count_parts:]
        hid_ref, norm_ref, router_ref, line_ref, tail_ref, w_ref = refs[:6]
        keep_ref, send_ref, resid_ref, spread_ref, held, aux, w_held, w_sems, tail_held, tail_sem = refs[6:]
    else:
        spread_ref, w_ref, keep_ref, send_ref, held, w_held, w_sems = refs
    experts = w_ref.shape[0]
    pairs = spread_ref.shape[1]
    width = spread_ref.shape[2] // 2
    copies = [
        pltpu.make_async_copy(w_ref.at[e, :, :, pl.ds(begin, columns)], w_held.at[e % SLOTS], w_sems.at[e % SLOTS])
        for e in range(experts)
    ]
    for copy in copies[:SLOTS]:
        copy.start()
    if first:
        tail_width, _, aux_at, size = tail
        tail_copy = pltpu.make_async_copy(tail_ref, tail_held, tail_sem)
        tail_copy.start()
        dispatch(parts, hid_ref, norm_ref, router_ref, line_ref, resid_ref, spread_ref, aux, aux_at % LANES)
        tail_copy.wait()

    for expert in range(experts):
        rows, valid = window_of(offset_ref, expert, pairs, window)
        left = jnp.concatenate([spread_ref[0, rows], spread_ref[1, rows]], axis=0)
        copies[expert].wait()
        result = dot_nn(left, w_held[expert % SLOTS].reshape(2 * width, columns)).astype(BF16)
        if expert + SLOTS < experts:
            copies[expert + SLOTS].start()
        held[rows, :columns] = jnp.where(valid, result[:window], held[rows, :columns])
        held[rows, columns : 2 * columns] = jnp.where(
            valid, result[window:], held[rows, columns : 2 * columns]
        )
        if first:
            result = dot_nn(left, tail_held[expert])
            lane = lax.broadcasted_iota(jnp.int32, (window, LANES), 1)
            gate, up = result[:window], result[window:]
            if tail_width == LANES:
                block = jnp.where(lane < size, gate, pltpu.roll(up, size, 1))
                block = jnp.where(lane < 2 * size, block, aux[rows])
            else:
                block = jnp.concatenate([gate, up, aux[rows]], axis=1)
            here = slice(2 * columns, 2 * columns + tail_width)
            held[rows, here] = jnp.where(valid, block.astype(BF16), held[rows, here])

    half, block, _ = keep_ref.shape
    for slot in range(half):
        mine = pl.ds(pl.multiple_of(order_ref[slot] * block, block), block)
        other = pl.ds(pl.multiple_of(order_ref[half + slot] * block, block), block)
        keep_ref[slot] = held[mine]
        send_ref[slot] = held[other]


def gate_tail_kernel(size, gate_ref, _, out_ref):
    experts, width, _, lanes = gate_ref.shape
    lane = lax.broadcasted_iota(jnp.int32, (2 * width, lanes), 1)
    for e in range(experts):
        out_ref[e] = jnp.where(lane < size, gate_ref[e].reshape(2 * width, lanes).astype(F32), 0.0).astype(BF16)


def down_tail_kernel(size, down_ref, _, out_ref):
    lane = lax.broadcasted_iota(jnp.int32, down_ref.shape[1:], 1)
    for e in range(down_ref.shape[0]):
        out_ref[e] = jnp.where(lane < size, down_ref[e].astype(F32), 0.0).astype(BF16)


def last_units(weights, after, kernel, rows, name):
    number, size = weights.shape[-1] // LANES, weights.shape[-1] % LANES
    lead = weights.shape[:-1]
    out = (weights.shape[0], rows, LANES)
    return pl.pallas_call(
        functools.partial(kernel, size),
        grid=(1,),
        in_specs=[
            pl.BlockSpec((*lead, LANES), lambda *_: (0,) * len(lead) + (number,)),
            pl.BlockSpec(memory_space=pl.ANY),
        ],
        out_specs=block_spec(out),
        out_shape=jax.ShapeDtypeStruct(out, BF16),
        compiler_params=params(),
        cost_estimate=pl.CostEstimate(flops=1, bytes_accessed=1, transcendentals=0),
        name=name,
    )(weights, after)


def tail_layout(units):
    size = units % LANES
    if 2 * size + 2 * PIECES <= LANES:
        return LANES, size, 2 * size, size
    return 3 * LANES, LANES, 2 * LANES, size


def sum_kernel(aux_at, groups, keep_ref, recv_ref, *outs):
    outs = outs[-len(groups) :]
    width = keep_ref.shape[2]

    def added(slot):
        total = keep_ref[slot].astype(F32) + recv_ref[slot].astype(F32)
        if aux_at is None:
            return [(slice(0, width), total)]
        base = aux_at // LANES * LANES
        tile = total[:, base : base + LANES]
        lane = lax.broadcasted_iota(jnp.int32, tile.shape, 1)
        for start in (aux_at - base, aux_at - base + PIECES):
            value = tile[:, start : start + 1]
            for k in range(1, PIECES):
                value = value + tile[:, start + k : start + k + 1]
            for k, piece in enumerate(split_bf16(value)):
                tile = jnp.where(lane == start + k, piece, tile)
        spans = [(slice(base, base + LANES), tile)]
        if base:
            spans.append((slice(0, base), total[:, :base]))
        if base + LANES < width:
            spans.append((slice(base + LANES, width), total[:, base + LANES :]))
        return spans

    for group, out in zip(groups, outs):
        for k, slot in enumerate(group):
            for span, value in added(slot):
                out[k, :, span] = value.astype(BF16)


def sum_parts(keep, recv, groups, aux_at, name, after=(), hold=None):
    _, block, width = keep.shape
    outs = [jax.ShapeDtypeStruct((len(group), block, width), BF16) for group in groups]
    in_specs = [full_spec(keep.shape)] * 2 + [pl.BlockSpec(memory_space=pl.ANY)] * len(after)
    out_specs = [full_spec(out.shape) for out in outs]
    operands = [keep, recv, *after]
    aliases = {}
    if hold is not None:
        operands.append(hold)
        in_specs.append(pl.BlockSpec(memory_space=pl.ANY))
        outs.insert(0, jax.ShapeDtypeStruct(hold.shape, hold.dtype))
        out_specs.insert(0, pl.BlockSpec(memory_space=pl.ANY))
        aliases = {len(operands) - 1: 0}
    return pl.pallas_call(
        functools.partial(sum_kernel, aux_at, groups),
        in_specs=in_specs,
        out_specs=out_specs,
        out_shape=outs,
        input_output_aliases=aliases,
        compiler_params=params(),
        cost_estimate=pl.CostEstimate(flops=1, bytes_accessed=1, transcendentals=0),
        name=name,
    )(*operands)


def halves(count):
    return [list(range(0, count, 2)), list(range(1, count, 2))] if count > 1 else [[0]]


def act_kernel(count_parts, columns, tail, features, *refs):
    parts, refs = refs[:count_parts], refs[count_parts:]
    total = parts[0][0].astype(F32)
    for part in parts[1:]:
        total = total + part[0].astype(F32)
    if tail is None:
        stat_ref, act_ref = refs[0], refs[-1]
        inverse, weight = stat_ref[:, 0:1], stat_ref[:, 1:2]
    else:
        act_ref, stat_ref = refs[-2:]
        tail_width, up_at, aux_at, size = tail
        base = 2 * columns + aux_at
        squares = total[:, base : base + 1]
        gap = total[:, base + PIECES : base + PIECES + 1]
        for k in range(1, PIECES):
            squares = squares + total[:, base + k : base + k + 1]
            gap = gap + total[:, base + PIECES + k : base + PIECES + k + 1]
        inverse = lax.rsqrt(squares / features + 1e-06)
        weight = 1.0 / (1.0 + jnp.exp(-gap * inverse))
        lane = lax.broadcasted_iota(jnp.int32, (total.shape[0], LANES), 1)
        stat_ref[...] = jnp.where(lane == 0, inverse, weight)

    def activate(gate, up):
        gate = gate * inverse
        return gate / (1.0 + jnp.exp(-gate)) * (up * inverse) * weight

    act_ref[:, :columns] = activate(total[:, :columns], total[:, columns : 2 * columns]).astype(BF16)
    if tail is not None:
        block = total[:, 2 * columns : 2 * columns + LANES]
        if tail_width == LANES:
            up = pltpu.roll(block, LANES - size, 1)
        else:
            up = total[:, 2 * columns + LANES : 2 * columns + 2 * LANES]
        last = jnp.where(lane < size, activate(block, up), 0.0)
        act_ref[:, columns:] = last.astype(BF16)


def activation(parts, stats, columns, tail, features, name, after):
    rows = parts[0].shape[1]
    out = jax.ShapeDtypeStruct((rows, columns + (LANES if tail else 0)), BF16)
    stat = jax.ShapeDtypeStruct((rows, LANES), F32)
    operands = [*parts] + ([] if tail else [stats])
    outs = [out, stat] if tail else [out]
    in_specs = [full_spec(x.shape) for x in operands] + [pl.BlockSpec(memory_space=pl.ANY)] * len(after)
    result = pl.pallas_call(
        functools.partial(act_kernel, len(parts), columns, tail, features),
        in_specs=in_specs,
        out_specs=[full_spec(x.shape) for x in outs],
        out_shape=outs,
        compiler_params=params(),
        cost_estimate=pl.CostEstimate(flops=1, bytes_accessed=1, transcendentals=0),
        name=name,
    )(*operands, *after)
    return (result[0], result[1]) if tail else (result[0], stats)


def lane_window(offset_ref, expert, pairs, window):
    first = offset_ref[expert]
    start = pl.multiple_of(jnp.minimum(first // LANES * LANES, pairs - window), LANES)
    lanes = lax.broadcasted_iota(jnp.int32, (1, window), 1) + start
    return pl.ds(start, window), (lanes >= first) & (lanes < offset_ref[expert + 1])


def down_kernel(half, chunks, tail, window, begins, ends, waits, offset_ref, order_ref, *refs):
    refs = refs[waits:]
    gathered = []
    for _ in chunks:
        gathered.append((refs[:half], refs[half]))
        refs = refs[half + 1 :]
    w_ref, refs = refs[0], refs[1:]
    if tail:
        tail_ref, refs = refs[0], refs[1:]
    if not begins:
        before_ref, refs = refs[0], refs[1:]
    if ends:
        place_ref, resid_ref, out_ref, total_ref, *held, w_held, w_sems = refs
    else:
        total_ref, *held, w_held, w_sems = refs
    experts = w_ref.shape[0]
    pairs = held[0].shape[0]
    copies = []
    for begin, columns in chunks:
        for e in range(experts):
            slot = len(copies) % SLOTS
            copies.append(
                pltpu.make_async_copy(
                    w_ref.at[e, :, pl.ds(begin, columns)], w_held.at[slot, :, pl.ds(0, columns)], w_sems.at[slot]
                )
            )
    for copy in copies[:SLOTS]:
        copy.start()
    for (parts, other_ref), into in zip(gathered, held):
        block = parts[0].shape[0]
        for slot in range(half):
            mine = pl.ds(pl.multiple_of(order_ref[slot] * block, block), block)
            other = pl.ds(pl.multiple_of(order_ref[half + slot] * block, block), block)
            into[mine] = parts[slot][...]
            into[other] = other_ref[slot]
    total_ref[...] = jnp.zeros_like(total_ref) if begins else before_ref[...]
    for index, (begin, columns) in enumerate(chunks):
        for expert in range(experts):
            number = index * experts + expert
            lanes, valid = lane_window(offset_ref, expert, pairs, window)
            copies[number].wait()
            result = dot_nt(w_held[number % SLOTS, :, :columns], held[index][lanes, :columns])
            if number + SLOTS < len(copies):
                copies[number + SLOTS].start()
            if tail and index == 0:
                result = result + dot_nt(tail_ref[expert], held[index][lanes, columns:])
            total_ref[:, lanes] = total_ref[:, lanes] + jnp.where(valid, result, 0.0)

    if ends:
        total = out_ref.shape[0]
        pieces = [x.astype(BF16) for x in split_bf16(total_ref[...], 2)]
        resid = [x.astype(BF16) for x in split_bf16(resid_ref[...], 2)]
        step = pair_block(total)
        for start in range(0, total, step):
            here = slice(start, start + step)
            pair = lax.broadcasted_iota(jnp.int32, (step, pairs), 1)
            place = place_ref[here].astype(jnp.int32)
            pick = (pair == place[:, 0:1]) | (pair == place[:, 1:2])
            pick = pick.astype(F32).astype(BF16)
            token = lax.broadcasted_iota(jnp.int32, (step, total), 1)
            move = (token == place[:, 2:3]).astype(F32).astype(BF16)
            result = dot_nt(pick, pieces[0]) + dot_nt(pick, pieces[1])
            result = result + dot_nt(move, resid[0]) + dot_nt(move, resid[1])
            out_ref[here] = result.astype(BF16)


def stack_kernel(counts, *refs):
    outs = refs[-len(counts) :]
    for count, out in zip(counts, outs):
        parts, refs = refs[:count], refs[count:]
        for k, part in enumerate(parts):
            out[k] = part[...]


def stack_parts(lists, after):
    operands = [x for parts in lists for x in parts]
    outs = [jax.ShapeDtypeStruct((len(parts), *parts[0].shape), BF16) for parts in lists]
    return pl.pallas_call(
        functools.partial(stack_kernel, [len(parts) for parts in lists]),
        in_specs=[full_spec(x.shape) for x in operands] + [pl.BlockSpec(memory_space=pl.ANY)] * len(after),
        out_specs=[full_spec(x.shape) for x in outs],
        out_shape=outs,
        compiler_params=params(),
        cost_estimate=pl.CostEstimate(flops=1, bytes_accessed=1, transcendentals=0),
        name="stack_parts",
    )(*operands, *after)


def chunk_columns(units):
    full = units // LANES
    count = 3 if full >= 6 else 1
    ends = [full * (k + 1) // count for k in range(count)]
    return [(LANES * (e - n), LANES * n) for e, n in zip(ends, [b - a for a, b in zip([0, *ends], ends)])]


def local(
    hidden_in,
    cache_pool,
    project_in,
    project_out,
    norm_first,
    norm_second,
    router,
    gate_up,
    expert_down,
    lengths,
    prompt_pages,
    own_pages,
    groups,
    move_target,
    routes,
):
    dp = lax.axis_size("dp")
    fs = lax.axis_size("fsdp")
    half = dp // 2
    my_row = lax.axis_index("dp")
    my_column = lax.axis_index("fsdp")
    my_chip, my_core = my_row // 2, my_row % 2
    req, features = hidden_in.shape
    row = req * fs
    total = row * dp
    pairs = 2 * total
    width = project_in.shape[0]
    cols = cache_pool.shape[3]
    heads = cols // HD
    page_len = cache_pool.shape[1]
    movers = move_target.shape[1]
    staying = row - movers
    experts = router.shape[1]
    units = gate_up.shape[3]
    window = windows(pairs, CAP * dp * fs)

    hidden_in = pltpu.with_memory_space_constraint(hidden_in, pltpu.HBM)
    gate_up = pltpu.with_memory_space_constraint(gate_up, pltpu.HBM)
    expert_down = pltpu.with_memory_space_constraint(expert_down, pltpu.HBM)

    chip = jnp.arange(half, dtype=jnp.int32)
    row_ids = jnp.arange(dp, dtype=jnp.int32)
    order = jnp.concatenate([(chip ^ my_chip) * 2 + my_core, (chip ^ my_chip) * 2 + 1 - my_core])

    def swap(x):
        return lax.ppermute(x, "dp", [(i, i ^ 1) for i in range(dp)])

    def over_chips(x, s):
        return lax.ppermute(x, "dp", [(i, i ^ (2 * s)) for i in range(dp)])

    def over_columns(x, s):
        return lax.ppermute(x, "fsdp", [(i, i ^ s) for i in range(fs)])

    payload = pack(hidden_in, routes.T, dp, fs)
    recv = lax.all_to_all(
        payload.reshape(dp * fs, req, payload.shape[3]), ("dp", "fsdp"), 0, 0, tiled=True
    ).reshape(total, payload.shape[3])

    row_lengths = lax.dynamic_slice_in_dim(lengths, my_row * row, row)
    lists = jnp.concatenate([own_pages, groups[:, None], row_lengths[:, None]], axis=1)
    lane = jnp.arange(cols, dtype=jnp.int32)
    channel = (lane % (HD // 2)).astype(F32)
    inverse = jnp.exp(-jnp.log(10000.0) * 2.0 * channel / HD)
    angles = row_lengths.astype(F32)[:, None] * inverse[None, :]
    cosine = jnp.cos(angles)
    sine = jnp.where((lane % HD < HD // 2)[None, :], -1.0, 1.0) * jnp.sin(angles)

    def slice_of(vector):
        return lax.dynamic_slice_in_dim(vector, my_row * width, width)

    gate_tail = last_units(gate_up, payload, gate_tail_kernel, 2 * width, "gate_tail")
    keep, send, raw = project_qkv(
        order,
        recv,
        slice_of(norm_first).astype(F32)[None, :],
        project_in.transpose(1, 0, 2),
        half,
        row,
        gate_tail,
    )
    sums = sum_parts(keep, swap(send), [[s] for s in range(half)], None, "core_sum_qkv")
    slot_of = (row_ids % 2 ^ my_core) * half + (row_ids // 2 ^ my_chip)
    column = jnp.stack([my_column, jnp.int32(fs)]).astype(jnp.int32)
    offsets, place_table, line_table = pair_places(
        move_target, order, slot_of, column, recv, sums[0], experts, width
    )
    keys, values, bias = split_pool(prompt_pages, lists, cache_pool, place_table)
    parts = [sums[0]] + [over_chips(sums[s], s) for s in range(1, half)]
    heads_out = attend(parts, cosine, sine, bias, keys, values, place_table)

    parts = [heads_out] + [over_chips(heads_out, s) for s in range(1, half)]
    other = swap(jnp.concatenate(parts, axis=0))
    projected = project_heads(parts, other, project_out.T)
    parts = [projected] + [over_columns(projected, s) for s in range(1, fs)]

    chunks = chunk_columns(units)
    tail = tail_layout(units)
    block = pairs // dp
    hbm = pl.BlockSpec(memory_space=pltpu.HBM)
    anywhere = pl.BlockSpec(memory_space=pl.ANY)
    spread = jax.ShapeDtypeStruct((2, pairs, 2 * width), BF16)
    resid_shape = jax.ShapeDtypeStruct((width, total), F32)
    norm_column = slice_of(norm_second).astype(F32)[:, None]
    router_slice = lax.dynamic_slice_in_dim(router, my_row * width, width).T
    state = {"after": [line_table]}
    flight = []

    def waits():
        after, flight[:] = state["after"] + flight, []
        return after

    def gate(index):
        after = state["after"]
        begin, columns = chunks[index]
        first = index == 0
        out_width = 2 * columns + (tail[0] if first else 0)
        half_out = jax.ShapeDtypeStruct((half, block, out_width), BF16)
        scratch = [pltpu.VMEM((pairs, out_width), BF16)]
        weights = [pltpu.VMEM((SLOTS, width, 2, columns), BF16), pltpu.SemaphoreType.DMA((SLOTS,))]
        if first:
            operands = [*parts, raw.T, norm_column, router_slice, line_table]
            in_specs = [full_spec(x.shape) for x in operands] + [hbm]
            operands.append(gate_tail)
            outs = [half_out, half_out, resid_shape, spread]
            scratch += [pltpu.VMEM((pairs, LANES), F32), *weights]
            scratch += [pltpu.VMEM(gate_tail.shape, BF16), pltpu.SemaphoreType.DMA]
        else:
            operands = [state["spread"]]
            in_specs = [full_spec(spread.shape)]
            outs = [half_out, half_out]
            scratch += weights
        result = pl.pallas_call(
            functools.partial(gate_kernel, len(parts) if first else 0, begin, columns, tail, window, len(after)),
            in_specs=[SCALARS] * 2 + [anywhere] * len(after) + [*in_specs, anywhere],
            out_specs=[full_spec(x.shape) for x in outs],
            scratch_shapes=scratch,
            out_shape=outs,
            compiler_params=params(room(total)),
            cost_estimate=pl.CostEstimate(flops=1, bytes_accessed=1, transcendentals=0),
            name=f"gate_up_{index}",
        )(offsets, order, *after, *operands, gate_up)
        if first:
            state["resid"], state["spread"] = result[2:]
        state["after"] = [result[0]]
        return result[:2]

    def combine(index, bit, held, hold=None):
        aux_at = 2 * chunks[index][1] + tail[2] if index == 0 else None
        sums = sum_parts(
            *held, halves(held[0].shape[0]), aux_at, f"sum_{index}_{bit}", waits() if bit else state["after"], hold
        )
        kept, sent = sums[-2:]
        state["after"] = [kept]
        received = over_chips(sent, 1 << bit)
        flying.append(received)
        return [kept, received], sums[0]

    def activate(index, held):
        act, state["stats"] = activation(
            held,
            state.get("stats"),
            chunks[index][1],
            tail if index == 0 else None,
            float(features),
            f"activation_{index}",
            waits(),
        )
        state["after"] = [act]
        return act

    def spread_out(parts, fresh):
        more = {}
        for s in fresh:
            low = (s & -s).bit_length() - 1 if s else stages
            for bit in range(low):
                more[s | 1 << bit] = over_chips(parts[s], 1 << bit)
        flying.extend(more.values())
        parts.update(more)
        return list(more)

    def down(numbers, lists, after):
        first, last = numbers[0] == 0, numbers[-1] == len(chunks) - 1
        stacked = stack_parts(lists, after)
        others = [swap(x) for x in stacked]
        operands = [x for parts, other in zip(lists, others) for x in (*parts, other)]
        in_specs = [full_spec(x.shape) for x in operands] + [anywhere]
        operands.append(expert_down)
        if first:
            operands.append(state["tail"])
            in_specs.append(full_spec(state["tail"].shape))
        else:
            operands.append(state["sum"])
            in_specs.append(full_spec(state["sum"].shape))
        sum_shape = jax.ShapeDtypeStruct((width, pairs), F32)
        widest = max(chunks[k][1] for k in numbers)
        scratch = [pltpu.VMEM((pairs, parts[0].shape[1]), BF16) for parts in lists]
        scratch += [pltpu.VMEM((SLOTS, width, widest), BF16), pltpu.SemaphoreType.DMA((SLOTS,))]
        outs = [sum_shape]
        if last:
            operands += [place_table, state["resid"]]
            in_specs += [full_spec(place_table.shape), full_spec(state["resid"].shape)]
            outs = [jax.ShapeDtypeStruct((total, width), BF16)]
            scratch = [pltpu.VMEM(sum_shape.shape, F32)] + scratch
        result = pl.pallas_call(
            functools.partial(
                down_kernel,
                half,
                [chunks[k] for k in numbers],
                tail if first else None,
                min(-(-CAP * dp * fs // LANES) * LANES + LANES, pairs),
                first,
                last,
                0,
            ),
                    in_specs=[SCALARS] * 2 + in_specs,
            out_specs=[full_spec(x.shape) for x in outs],
            scratch_shapes=scratch,
            out_shape=outs,
            compiler_params=params(room(total)),
            cost_estimate=pl.CostEstimate(flops=1, bytes_accessed=1, transcendentals=0),
            name=f"down_{numbers[0]}",
        )(offsets, order, *operands)[0]
        state["sum"] = result
        return result

    stages = half.bit_length() - 1
    count = len(chunks)
    early = max(0, count - stages)
    held, gathered, fresh = {}, {}, {}
    flying = []
    for step in range(count + stages):
        sent = None
        if step < count:
            kept, sent = gate(step)
        if step == count - 1:
            state["tail"] = last_units(expert_down, state["after"][0], down_tail_kernel, width, "down_tail")
        for k in range(count):
            if step - k == stages:
                if step == count - 1 + stages:
                    flight.append(state["tail"])
                gathered[k] = {0: activate(k, held[k])}
                if k < count - 1:
                    fresh[k] = spread_out(gathered[k], [0])
                else:
                    gathered[k].update({s: over_chips(gathered[k][0], s) for s in range(1, half)})
            elif 1 <= step - k < stages:
                held[k], through = combine(k, step - k, held[k], sent)
                sent = None if sent is None else through
        if step < count:
            held[step], _ = combine(step, 0, [kept, swap(sent)])
        for k in range(count - 1):
            if stages < step - k:
                fresh[k] = spread_out(gathered[k], fresh[k])
        flight.extend(flying)
        flying.clear()
    while any(fresh.values()):
        fresh = {k: spread_out(gathered[k], fresh[k]) for k in fresh}
    lists = [[gathered[k][s] for s in range(half)] for k in range(count)]
    last_after = state["after"]
    if early:
        last_after = [down(list(range(early)), lists[:early], state["after"])]
    result = down(list(range(early, count)), lists[early:], last_after)

    back = lax.all_to_all(result.reshape(dp * fs, req, width), ("dp", "fsdp"), 0, 0, tiled=True)
    back = back.reshape(dp, fs, req, width).astype(F32)
    return jnp.sum(back, axis=1).transpose(1, 0, 2).reshape(req, features).astype(BF16)


def solution(mesh):
    placed = (
        P(("dp", "fsdp"), None),
        P("dp", None, None, "fsdp"),
        P("dp", None, "fsdp"),
        P("fsdp", "dp"),
        P(),
        P(),
        P(),
        P(None, "dp", None, "fsdp"),
        P(None, "dp", "fsdp"),
        P(),
        P("dp", None),
        P("dp", None),
        P("dp"),
        P(),
        P(("dp", "fsdp"), None),
    )
    return jax.shard_map(
        local, mesh=mesh, in_specs=placed, out_specs=P(("dp", "fsdp"), None), check_vma=False
    )
```

```python
import functools

import jax
import jax.numpy as jnp
from jax import lax
from jax.experimental import pallas as pl
from jax.experimental.pallas import tpu as pltpu
from jax.sharding import PartitionSpec as P

HD = 64
CAP = 4
PIECES = 3
LANES = 128
BF16 = jnp.bfloat16
F32 = jnp.float32
FAR = -3.0e38
SMALL, ATTENTION, LARGE = 16, 24, 60
SLOTS = 8


def params(mib=SMALL):
    return pltpu.CompilerParams(vmem_limit_bytes=mib * 2**20)


def room(tokens):
    return SMALL if tokens <= 512 else LARGE


def dot_nn(a, b):
    return lax.dot_general(a, b, (((1,), (0,)), ((), ())), preferred_element_type=F32)


def dot_nt(a, b):
    return lax.dot_general(a, b, (((1,), (1,)), ((), ())), preferred_element_type=F32)


def split_bf16(value, count=PIECES):
    pieces = []
    for _ in range(count):
        piece = value.astype(BF16).astype(F32)
        pieces.append(piece)
        value = value - piece
    return pieces


def full_spec(shape):
    return pl.BlockSpec(memory_space=pltpu.VMEM)


def block_spec(shape):
    zeros = (0,) * len(shape)
    return pl.BlockSpec(tuple(shape), lambda *_: zeros)


SCALARS = pl.BlockSpec(memory_space=pltpu.SMEM)


def pack_kernel(hidden_hbm, routes_hbm, out_ref, hidden_ref, routes_ref, sems):
    copies = [
        pltpu.make_async_copy(hidden_hbm, hidden_ref, sems.at[0]),
        pltpu.make_async_copy(routes_hbm, routes_ref, sems.at[1]),
    ]
    for copy in copies:
        copy.start()
    for copy in copies:
        copy.wait()
    slices, copies, req, room = out_ref.shape
    features = hidden_ref.shape[1]
    width = features // slices
    values = hidden_ref[...].astype(F32)
    factor = lax.rsqrt(jnp.mean(values * values, axis=1, keepdims=True) + 1e-06)
    lane = lax.broadcasted_iota(jnp.int32, (req, room), 1)
    extra = jnp.zeros((req, room), F32)
    for k, piece in enumerate(split_bf16(factor)):
        extra = jnp.where(lane == width + k, piece, extra)
    spot = lax.broadcasted_iota(jnp.int32, (req, req), 1) == lax.broadcasted_iota(jnp.int32, (req, req), 0)
    for k in range(2):
        route = jnp.sum(jnp.where(spot, routes_ref[k : k + 1].astype(F32), 0.0), axis=1, keepdims=True)
        extra = jnp.where(lane == width + PIECES + k, route, extra)
    for index in range(slices):
        moved = pltpu.roll(values, (features - index * width) % features, 1) if index else values
        block = jnp.where(lane < width, moved[:, :room], extra).astype(BF16)
        for copy in range(copies):
            out_ref[index, copy] = block


def pack(hidden_in, routes, slices, copies):
    req, features = hidden_in.shape
    width = features // slices
    room = -(-(width + PIECES + 2) // LANES) * LANES
    out = (slices, copies, req, room)
    return pl.pallas_call(
        pack_kernel,
        in_specs=[pl.BlockSpec(memory_space=pl.ANY)] * 2,
        out_specs=full_spec(out),
        scratch_shapes=[
            pltpu.VMEM(hidden_in.shape, BF16),
            pltpu.VMEM(routes.shape, jnp.int32),
            pltpu.SemaphoreType.DMA((2,)),
        ],
        out_shape=jax.ShapeDtypeStruct(out, BF16),
        compiler_params=params(),
        cost_estimate=pl.CostEstimate(flops=1, bytes_accessed=1, transcendentals=0),
        name="pack",
    )(hidden_in, routes)


def places_kernel(
    experts, width, staying, move_ref, order_ref, slot_ref, column_ref, recv_ref, _, off_ref, place_ref, line_ref, table, slots
):
    total = recv_ref.shape[0]
    rows_count, movers = move_ref.shape
    row = total // rows_count
    block = min(total, 256)
    lane = lax.broadcasted_iota(jnp.int32, (block, LANES), 1)
    above = lax.broadcasted_iota(jnp.int32, (block, block), 0)
    beside = lax.broadcasted_iota(jnp.int32, (block, block), 1)
    before = (beside < above).astype(F32).astype(BF16)
    counts = jnp.zeros((1, LANES), F32)
    for start in range(0, total, block):
        here = slice(start, start + block)
        first = recv_ref[here, width + PIECES : width + PIECES + 1].astype(F32).astype(jnp.int32)
        second = recv_ref[here, width + PIECES + 1 : width + PIECES + 2].astype(F32).astype(jnp.int32)
        member = (lane == first).astype(F32) + (lane == second).astype(F32)
        rank = dot_nn(before, member.astype(BF16)) + counts
        counts = counts + jnp.sum(member, axis=0, keepdims=True)
        mine = jnp.sum(jnp.where(lane == first, rank, 0.0), axis=1, keepdims=True)
        other = jnp.sum(jnp.where(lane == second, rank, 0.0), axis=1, keepdims=True)
        block_table = jnp.where(lane == 0, mine, jnp.where(lane == 1, other, 0.0))
        block_table = jnp.where(lane == 2, first.astype(F32), block_table)
        table[here] = jnp.where(lane == 3, second.astype(F32), block_table)
    single = lax.broadcasted_iota(jnp.int32, (1, LANES), 1)
    sums = [jnp.sum(jnp.where(single == e, counts, 0.0)) for e in range(experts)]
    off_ref[0] = 0
    running = jnp.float32(0.0)
    begins = jnp.zeros((1, LANES), F32)
    for e in range(experts):
        begins = jnp.where(single == e, running, begins)
        running = running + sums[e]
        off_ref[e + 1] = running.astype(jnp.int32)
    for start in range(0, total, block):
        here = slice(start, start + block)
        values = table[here]
        first = values[:, 2:3].astype(jnp.int32)
        second = values[:, 3:4].astype(jnp.int32)
        begin_first = jnp.sum(jnp.where(lane == first, begins, 0.0), axis=1, keepdims=True)
        begin_second = jnp.sum(jnp.where(lane == second, begins, 0.0), axis=1, keepdims=True)
        values = values + jnp.where(lane == 0, begin_first, jnp.where(lane == 1, begin_second, 0.0))
        table[here] = values
        place_ref[here] = values
    within = lax.broadcasted_iota(jnp.int32, (row, LANES), 0)
    wide = lax.broadcasted_iota(jnp.int32, (row, LANES), 1)
    req = row // column_ref[1]
    mine = (within >= column_ref[0] * req) & (within < (column_ref[0] + 1) * req)
    for r in range(rows_count):
        here = slice(r * row, (r + 1) * row)
        lies = jnp.where(mine, (within + slot_ref[r] * row).astype(F32), -1.0)
        place_ref[here] = jnp.where(wide == 2, lies, place_ref[here])
    for r in range(rows_count):
        for j in range(movers):
            at = staying + j
            target = pl.ds(move_ref[r, j] * row + at, 1)
            held = (at >= column_ref[0] * req) & (at < (column_ref[0] + 1) * req)
            lies = jnp.where(held, slot_ref[r] * row + at, -1).astype(F32)
            place_ref[target] = jnp.where(single == 2, lies, place_ref[target])
    for b in range(rows_count):
        slots[b * row : (b + 1) * row] = table[pl.ds(pl.multiple_of(order_ref[b] * row, row), row)]
        for j in range(movers):
            at = staying + j
            source = pl.ds(move_ref[order_ref[b], j] * row + at, 1)
            slots[b * row + at : b * row + at + 1] = table[source]
    line_ref[...] = slots[...].T[:8]


def pair_places(move_target, order, slot_of, column, recv, after, experts, width):
    total = recv.shape[0]
    rows_count, movers = move_target.shape
    staying = total // rows_count - movers
    outs = [
        jax.ShapeDtypeStruct((experts + 1,), jnp.int32),
        jax.ShapeDtypeStruct((total, LANES), F32),
        jax.ShapeDtypeStruct((8, total), F32),
    ]
    return pl.pallas_call(
        functools.partial(places_kernel, experts, width, staying),
        in_specs=[SCALARS] * 4 + [full_spec(recv.shape), pl.BlockSpec(memory_space=pl.ANY)],
        out_specs=[
            pl.BlockSpec(memory_space=pltpu.SMEM),
            full_spec(outs[1].shape),
            full_spec(outs[2].shape),
        ],
        scratch_shapes=[pltpu.VMEM((total, LANES), F32), pltpu.VMEM((total, LANES), F32)],
        out_shape=outs,
        compiler_params=params(room(total)),
        cost_estimate=pl.CostEstimate(flops=1, bytes_accessed=1, transcendentals=0),
        name="pair_places",
    )(move_target, order, slot_of, column, recv, after)


def pool_kernel(prompt_ref, lists_ref, pool_ref, _, key_ref, value_ref, bias_ref):
    pages, page_len, _, cols = pool_ref.shape
    rows = pages * page_len
    both = pool_ref[...].reshape(2 * rows, cols)
    part = min(rows, LANES)
    wide = lax.broadcasted_iota(jnp.int32, (part, 2 * part), 1)
    high = lax.broadcasted_iota(jnp.int32, (part, 2 * part), 0)
    even = (wide == 2 * high).astype(F32).astype(BF16)
    odd = (wide == 2 * high + 1).astype(F32).astype(BF16)
    for start in range(0, rows, part):
        piece = both[2 * start : 2 * (start + part)]
        key_ref[start : start + part] = dot_nn(even, piece).astype(BF16)
        value_ref[start : start + part] = dot_nn(odd, piece).astype(BF16)
    requests = bias_ref.shape[0]
    prompts, prompt_len = prompt_ref.shape
    own_len = lists_ref.shape[1] - 2
    group, length = lists_ref[:, own_len : own_len + 1], lists_ref[:, own_len + 1 :]
    spot = lax.broadcasted_iota(jnp.int32, (requests, rows), 1)
    page = spot // page_len + pl.program_id(0) * pages
    reach = jnp.zeros((requests, rows), jnp.int32)
    for k in range(prompt_len):
        listed = jnp.zeros((requests, 1), jnp.int32)
        for g in range(prompts):
            listed = jnp.where(group == g, prompt_ref[g, k], listed)
        reach = jnp.where(page == listed, length - page_len * k, reach)
    for k in range(own_len):
        reach = jnp.where(page == lists_ref[:, k : k + 1], length - page_len * (prompt_len + k), reach)
    bias_ref[...] = jnp.where(spot % page_len < reach, 0.0, FAR)


def split_pool(prompt_pages, lists, cache_pool, after):
    pages, page_len, _, cols = cache_pool.shape
    requests = lists.shape[0]
    block = next(b for b in (16, 8, 4, 2, 1) if pages % b == 0)
    out = jax.ShapeDtypeStruct((pages * page_len, cols), BF16)
    spec = pl.BlockSpec((block * page_len, cols), lambda b, *_: (b, 0))
    return pl.pallas_call(
        pool_kernel,
        grid_spec=pltpu.PrefetchScalarGridSpec(
            num_scalar_prefetch=1,
            grid=(pages // block,),
            in_specs=[
                block_spec(lists.shape),
                pl.BlockSpec((block, page_len, 2, cols), lambda b, *_: (b, 0, 0, 0)),
                pl.BlockSpec(memory_space=pl.ANY),
            ],
            out_specs=[spec, spec, pl.BlockSpec((requests, block * page_len), lambda b, *_: (0, b))],
        ),
        out_shape=[out, out, jax.ShapeDtypeStruct((requests, pages * page_len), F32)],
        compiler_params=params(),
        cost_estimate=pl.CostEstimate(flops=1, bytes_accessed=1, transcendentals=0),
        name="pool_split",
    )(prompt_pages, lists, cache_pool, after)


def qkv_kernel(order_ref, recv_ref, norm_ref, w_ref, _, keep_ref, send_ref, raw_ref, normed, slots):
    width = norm_ref.shape[1]
    half, row, _ = keep_ref.shape
    cols = w_ref.shape[2]
    values = recv_ref[:, :width]
    scale = recv_ref[:, width : width + 1].astype(F32)
    for piece in range(1, PIECES):
        scale = scale + recv_ref[:, width + piece : width + piece + 1].astype(F32)
    normed[...] = (values.astype(F32) * scale * norm_ref[...]).astype(BF16)
    for slot in range(2 * half):
        rows = pl.ds(pl.multiple_of(order_ref[slot] * row, row), row)
        slots[slot * row : (slot + 1) * row] = normed[rows]
        raw_ref[slot * row : (slot + 1) * row] = recv_ref[rows, :width]
    for part in range(3):
        here = slice(part * cols, (part + 1) * cols)
        result = dot_nn(slots[...], w_ref[part]).astype(BF16).reshape(2 * half, row, cols)
        keep_ref[:, :, here] = result[:half]
        send_ref[:, :, here] = result[half:]


def project_qkv(order, recv, norm_slice, weights, half, row, after):
    total, _ = recv.shape
    width, cols = weights.shape[1:]
    out = jax.ShapeDtypeStruct((half, row, 3 * cols), BF16)
    raw = jax.ShapeDtypeStruct((total, width), BF16)
    return pl.pallas_call(
        qkv_kernel,
        in_specs=[SCALARS] * 1 + [full_spec(x.shape) for x in (recv, norm_slice, weights)] + [pl.BlockSpec(memory_space=pl.ANY)],
        out_specs=[full_spec(out.shape), full_spec(out.shape), full_spec(raw.shape)],
        scratch_shapes=[pltpu.VMEM((total, width), BF16), pltpu.VMEM((total, width), BF16)],
        out_shape=[out, out, raw],
        compiler_params=params(room(total)),
        cost_estimate=pl.CostEstimate(flops=1, bytes_accessed=1, transcendentals=0),
        name="qkv",
    )(order, recv, norm_slice, weights, after)


def attention_kernel(*refs):
    parts, refs = refs[:-9], refs[-9:]
    cos_ref, sin_ref, bias_ref, key_ref, value_ref, _, out_ref, scores, probs = refs
    row, cols = out_ref.shape
    heads = cols // HD
    total = parts[0][0].astype(F32)
    for part in parts[1:]:
        total = total + part[0].astype(F32)
    lane = lax.broadcasted_iota(jnp.int32, (row, cols), 1)
    first_half = lane % HD < HD // 2

    def rotate(values):
        partner = jnp.where(
            first_half, pltpu.roll(values, cols - HD // 2, 1), pltpu.roll(values, HD // 2, 1)
        )
        return (values * cos_ref[...] + partner * sin_ref[...]).astype(BF16)

    query = rotate(total[:, :cols]).astype(F32)
    key_new = rotate(total[:, cols : 2 * cols]).astype(F32)
    value_new = total[:, 2 * cols :].astype(BF16).astype(F32)
    spread = jnp.concatenate(
        [jnp.where(lane // HD == h, query, 0.0).astype(BF16) for h in range(heads)], axis=0
    )
    scores[...] = dot_nt(spread, key_ref[...])
    own_parts = []
    for h in range(heads):
        here = slice(h * row, (h + 1) * row)
        mine = lane // HD == h
        own = jnp.sum(jnp.where(mine, query * key_new, 0.0), axis=1, keepdims=True) * HD**-0.5
        score = scores[here] * HD**-0.5 + bias_ref[...]
        highest = jnp.maximum(jnp.max(score, axis=1, keepdims=True), own)
        weight = jnp.exp(score - highest)
        weight_own = jnp.exp(own - highest)
        inverse = 1.0 / (jnp.sum(weight, axis=1, keepdims=True) + weight_own)
        probs[here] = (weight * inverse).astype(BF16)
        own_parts.append((weight_own * inverse).astype(BF16).astype(F32))
    mixture = dot_nn(probs[...], value_ref[...])
    result = jnp.zeros((row, cols), F32)
    for h in range(heads):
        mixed = mixture[h * row : (h + 1) * row] + own_parts[h] * value_new
        result = jnp.where(lane // HD == h, mixed, result)
    out_ref[...] = result.astype(BF16)


def attend(parts, cosine, sine, bias, keys, values, after):
    row, cols = cosine.shape
    stretch = keys.shape[0]
    heads = cols // HD
    operands = [*parts, cosine, sine, bias, keys, values]
    return pl.pallas_call(
        attention_kernel,
        in_specs=[full_spec(x.shape) for x in operands] + [pl.BlockSpec(memory_space=pl.ANY)],
        out_specs=full_spec((row, cols)),
        out_shape=jax.ShapeDtypeStruct((row, cols), BF16),
        scratch_shapes=[
            pltpu.VMEM((heads * row, stretch), F32),
            pltpu.VMEM((heads * row, stretch), BF16),
        ],
        compiler_params=params(ATTENTION),
        cost_estimate=pl.CostEstimate(flops=1, bytes_accessed=1, transcendentals=0),
        name="attention",
    )(*operands, after)


def out_kernel(*refs):
    parts, (other_ref, w_ref, out_ref) = refs[:-3], refs[-3:]
    half = len(parts) * parts[0].shape[0]
    mine = jnp.concatenate([part[...] for part in parts], axis=0)
    out_ref[:, :half] = dot_nt(w_ref[...], mine).astype(BF16)
    out_ref[:, half:] = dot_nt(w_ref[...], other_ref[...]).astype(BF16)


def project_heads(parts, other, weights):
    half = other.shape[0]
    operands = [*parts, other, weights]
    out = (weights.shape[0], 2 * half)
    return pl.pallas_call(
        out_kernel,
        in_specs=[full_spec(x.shape) for x in operands],
        out_specs=full_spec(out),
        out_shape=jax.ShapeDtypeStruct(out, BF16),
        compiler_params=params(room(2 * half)),
        cost_estimate=pl.CostEstimate(flops=1, bytes_accessed=1, transcendentals=0),
        name="out_projection",
    )(*operands)


def pair_block(pairs):
    return next(b for b in (256, 128, 64, 32, 16) if pairs % b == 0)


def dispatch(parts, hid_ref, norm_ref, router_ref, line_ref, resid_ref, spread_ref, aux_ref, aux_at):
    width, total = hid_ref.shape
    pairs = spread_ref.shape[1]
    resid = hid_ref[...].astype(F32)
    for part in parts:
        resid = resid + part[...].astype(F32)
    resid_ref[...] = resid
    moe = (resid * norm_ref[...]).astype(BF16)
    squares = jnp.sum(resid * resid, axis=0, keepdims=True)
    logits = dot_nn(router_ref[...], moe)
    expert = lax.broadcasted_iota(jnp.int32, logits.shape, 0)
    line = line_ref[...].astype(jnp.int32)
    sign = (expert == line[2:3]).astype(F32) - (expert == line[3:4]).astype(F32)
    gap = jnp.sum(logits * sign, axis=0, keepdims=True)
    high = lax.broadcasted_iota(jnp.int32, (LANES, total), 0)
    aux_plain = jnp.zeros((LANES, total), F32)
    aux_signed = jnp.zeros((LANES, total), F32)
    for k, piece in enumerate(split_bf16(squares)):
        aux_plain = jnp.where(high == aux_at + k, piece, aux_plain)
    for k, piece in enumerate(split_bf16(gap)):
        aux_signed = jnp.where(high == aux_at + PIECES + k, piece, aux_signed)
    aux_plain = aux_plain.astype(BF16)
    aux_signed = aux_signed.astype(BF16)
    feature = lax.broadcasted_iota(jnp.int32, (width, 2 * width), 0)
    lane = lax.broadcasted_iota(jnp.int32, (width, 2 * width), 1)
    even = (lane == 2 * feature).astype(BF16)
    odd = (lane == 2 * feature + 1).astype(BF16)
    block = pair_block(pairs)
    for start in range(0, pairs, block):
        here = slice(start, start + block)
        pair = lax.broadcasted_iota(jnp.int32, (block, total), 0) + start
        first = (pair == line[0:1]).astype(F32)
        second = (pair == line[1:2]).astype(F32)
        both = (first + second).astype(BF16)
        rows = dot_nt(both, moe).astype(BF16)
        spread_ref[0, here] = dot_nn(rows, even).astype(BF16)
        spread_ref[1, here] = dot_nn(rows, odd).astype(BF16)
        aux_ref[here] = dot_nt(both, aux_plain) + dot_nt((first - second).astype(BF16), aux_signed)


def windows(pairs, per_expert):
    return min(per_expert + 16, pairs)


def window_of(offset_ref, expert, pairs, window):
    first = offset_ref[expert]
    start = pl.multiple_of(jnp.minimum(first // 16 * 16, pairs - window), 16)
    rows = lax.broadcasted_iota(jnp.int32, (window, 1), 0) + start
    return pl.ds(start, window), (rows >= first) & (rows < offset_ref[expert + 1])


def gate_kernel(count_parts, begin, columns, tail, window, waits, offset_ref, order_ref, *refs):
    first = count_parts > 0
    refs = refs[waits:]
    if first:
        parts, refs = refs[:count_parts], refs[count_parts:]
        hid_ref, norm_ref, router_ref, line_ref, tail_ref, w_ref = refs[:6]
        keep_ref, send_ref, resid_ref, spread_ref, held, aux = refs[6:]
    else:
        spread_ref, w_ref, keep_ref, send_ref, held, w_held, w_sems = refs
    experts = w_ref.shape[0]
    pairs = spread_ref.shape[1]
    width = spread_ref.shape[2] // 2
    if first:
        tail_width, _, aux_at, size = tail
        dispatch(parts, hid_ref, norm_ref, router_ref, line_ref, resid_ref, spread_ref, aux, aux_at % LANES)
    else:
        copies = [
            pltpu.make_async_copy(w_ref.at[e, :, :, pl.ds(begin, columns)], w_held.at[e % SLOTS], w_sems.at[e % SLOTS])
            for e in range(experts)
        ]
        for copy in copies[:SLOTS]:
            copy.start()

    for expert in range(experts):
        rows, valid = window_of(offset_ref, expert, pairs, window)
        left = jnp.concatenate([spread_ref[0, rows], spread_ref[1, rows]], axis=0)
        if first:
            weights = w_ref[expert]
        else:
            copies[expert].wait()
            weights = w_held[expert % SLOTS]
        result = dot_nn(left, weights.reshape(2 * width, columns)).astype(BF16)
        if not first and expert + SLOTS < experts:
            copies[expert + SLOTS].start()
        held[rows, :columns] = jnp.where(valid, result[:window], held[rows, :columns])
        held[rows, columns : 2 * columns] = jnp.where(
            valid, result[window:], held[rows, columns : 2 * columns]
        )
        if first:
            result = dot_nn(left, tail_ref[expert])
            lane = lax.broadcasted_iota(jnp.int32, (window, LANES), 1)
            gate, up = result[:window], result[window:]
            if tail_width == LANES:
                block = jnp.where(lane < size, gate, pltpu.roll(up, size, 1))
                block = jnp.where(lane < 2 * size, block, aux[rows])
            else:
                block = jnp.concatenate([gate, up, aux[rows]], axis=1)
            here = slice(2 * columns, 2 * columns + tail_width)
            held[rows, here] = jnp.where(valid, block.astype(BF16), held[rows, here])

    half, block, _ = keep_ref.shape
    for slot in range(half):
        mine = pl.ds(pl.multiple_of(order_ref[slot] * block, block), block)
        other = pl.ds(pl.multiple_of(order_ref[half + slot] * block, block), block)
        keep_ref[slot] = held[mine]
        send_ref[slot] = held[other]


def gate_tail_kernel(size, gate_ref, _, out_ref, token_ref):
    token_ref[...] = jnp.zeros_like(token_ref)
    experts, width, _, lanes = gate_ref.shape
    lane = lax.broadcasted_iota(jnp.int32, (2 * width, lanes), 1)
    for e in range(experts):
        out_ref[e] = jnp.where(lane < size, gate_ref[e].reshape(2 * width, lanes).astype(F32), 0.0).astype(BF16)


def last_units(weights, after):
    experts, width, _, units = weights.shape
    number, size = units // LANES, units % LANES
    out = (experts, 2 * width, LANES)
    return pl.pallas_call(
        functools.partial(gate_tail_kernel, size),
        grid=(1,),
        in_specs=[
            pl.BlockSpec((experts, width, 2, LANES), lambda *_: (0, 0, 0, number)),
            pl.BlockSpec(memory_space=pl.ANY),
        ],
        out_specs=[block_spec(out), block_spec((8, LANES))],
        out_shape=[pltpu.HBM(out, BF16), jax.ShapeDtypeStruct((8, LANES), F32)],
        compiler_params=params(),
        cost_estimate=pl.CostEstimate(flops=1, bytes_accessed=1, transcendentals=0),
        name="gate_tail",
    )(weights, after)


def stage_gate_kernel(begin, columns, w_ref, tail_ref, _, out_ref, tail_out, sems):
    copies = [
        pltpu.make_async_copy(w_ref.at[:, :, :, pl.ds(begin, columns)], out_ref, sems.at[0]),
        pltpu.make_async_copy(tail_ref, tail_out, sems.at[1]),
    ]
    for copy in copies:
        copy.start()
    for copy in copies:
        copy.wait()


def stage_gate(gate_up, tail, begin, columns, after):
    anywhere = pl.BlockSpec(memory_space=pl.ANY)
    return pl.pallas_call(
        functools.partial(stage_gate_kernel, begin, columns),
        in_specs=[anywhere] * 3,
        out_specs=[anywhere] * 2,
        out_shape=[pltpu.VMEM((*gate_up.shape[:3], columns), BF16), pltpu.VMEM(tail.shape, BF16)],
        scratch_shapes=[pltpu.SemaphoreType.DMA((2,))],
        compiler_params=params(),
        cost_estimate=pl.CostEstimate(flops=1, bytes_accessed=1, transcendentals=0),
        name="stage_gate",
    )(gate_up, tail, after)


def stage_down_kernel(w_ref, _, out_ref, sem):
    copy = pltpu.make_async_copy(w_ref, out_ref, sem)
    copy.start()
    copy.wait()


def stage_down(weights, after):
    return pl.pallas_call(
        stage_down_kernel,
        in_specs=[pl.BlockSpec(memory_space=pl.ANY)] * 2,
        out_specs=pl.BlockSpec(memory_space=pl.ANY),
        out_shape=pltpu.VMEM(weights.shape, BF16),
        scratch_shapes=[pltpu.SemaphoreType.DMA],
        compiler_params=params(),
        cost_estimate=pl.CostEstimate(flops=1, bytes_accessed=1, transcendentals=0),
        name="stage_down",
    )(weights, after)


def tail_layout(units):
    size = units % LANES
    if 2 * size + 2 * PIECES <= LANES:
        return LANES, size, 2 * size, size
    return 3 * LANES, LANES, 2 * LANES, size


def sum_kernel(aux_at, groups, keep_ref, recv_ref, *outs):
    outs = outs[-len(groups) :]
    width = keep_ref.shape[2]

    def added(slot):
        total = keep_ref[slot].astype(F32) + recv_ref[slot].astype(F32)
        if aux_at is None:
            return [(slice(0, width), total)]
        base = aux_at // LANES * LANES
        tile = total[:, base : base + LANES]
        lane = lax.broadcasted_iota(jnp.int32, tile.shape, 1)
        for start in (aux_at - base, aux_at - base + PIECES):
            value = tile[:, start : start + 1]
            for k in range(1, PIECES):
                value = value + tile[:, start + k : start + k + 1]
            for k, piece in enumerate(split_bf16(value)):
                tile = jnp.where(lane == start + k, piece, tile)
        spans = [(slice(base, base + LANES), tile)]
        if base:
            spans.append((slice(0, base), total[:, :base]))
        if base + LANES < width:
            spans.append((slice(base + LANES, width), total[:, base + LANES :]))
        return spans

    for group, out in zip(groups, outs):
        for k, slot in enumerate(group):
            for span, value in added(slot):
                out[k, :, span] = value.astype(BF16)


def sum_parts(keep, recv, groups, aux_at, name, after=(), hold=None):
    _, block, width = keep.shape
    outs = [jax.ShapeDtypeStruct((len(group), block, width), BF16) for group in groups]
    in_specs = [full_spec(keep.shape)] * 2 + [pl.BlockSpec(memory_space=pl.ANY)] * len(after)
    out_specs = [full_spec(out.shape) for out in outs]
    operands = [keep, recv, *after]
    aliases = {}
    if hold is not None:
        operands.append(hold)
        in_specs.append(pl.BlockSpec(memory_space=pl.ANY))
        outs.insert(0, jax.ShapeDtypeStruct(hold.shape, hold.dtype))
        out_specs.insert(0, pl.BlockSpec(memory_space=pl.ANY))
        aliases = {len(operands) - 1: 0}
    return pl.pallas_call(
        functools.partial(sum_kernel, aux_at, groups),
        in_specs=in_specs,
        out_specs=out_specs,
        out_shape=outs,
        input_output_aliases=aliases,
        compiler_params=params(),
        cost_estimate=pl.CostEstimate(flops=1, bytes_accessed=1, transcendentals=0),
        name=name,
    )(*operands)


def halves(count):
    return [list(range(0, count, 2)), list(range(1, count, 2))] if count > 1 else [[0]]


def act_kernel(count_parts, columns, tail, features, *refs):
    parts, refs = refs[:count_parts], refs[count_parts:]
    total = parts[0][0].astype(F32)
    for part in parts[1:]:
        total = total + part[0].astype(F32)
    if tail is None:
        stat_ref, act_ref = refs[0], refs[-1]
        inverse, weight = stat_ref[:, 0:1], stat_ref[:, 1:2]
    else:
        act_ref, stat_ref = refs[-2:]
        tail_width, up_at, aux_at, size = tail
        base = 2 * columns + aux_at
        squares = total[:, base : base + 1]
        gap = total[:, base + PIECES : base + PIECES + 1]
        for k in range(1, PIECES):
            squares = squares + total[:, base + k : base + k + 1]
            gap = gap + total[:, base + PIECES + k : base + PIECES + k + 1]
        inverse = lax.rsqrt(squares / features + 1e-06)
        weight = 1.0 / (1.0 + jnp.exp(-gap * inverse))
        lane = lax.broadcasted_iota(jnp.int32, (total.shape[0], LANES), 1)
        stat_ref[...] = jnp.where(lane == 0, inverse, weight)

    def activate(gate, up):
        gate = gate * inverse
        return gate / (1.0 + jnp.exp(-gate)) * (up * inverse) * weight

    act_ref[:, :columns] = activate(total[:, :columns], total[:, columns : 2 * columns]).astype(BF16)
    if tail is not None:
        block = total[:, 2 * columns : 2 * columns + LANES]
        if tail_width == LANES:
            up = pltpu.roll(block, LANES - size, 1)
        else:
            up = total[:, 2 * columns + LANES : 2 * columns + 2 * LANES]
        last = jnp.where(lane < size, activate(block, up), 0.0)
        act_ref[:, columns:] = last.astype(BF16)


def activation(parts, stats, columns, tail, features, name, after):
    rows = parts[0].shape[1]
    out = jax.ShapeDtypeStruct((rows, columns + (LANES if tail else 0)), BF16)
    stat = jax.ShapeDtypeStruct((rows, LANES), F32)
    operands = [*parts] + ([] if tail else [stats])
    outs = [out, stat] if tail else [out]
    in_specs = [full_spec(x.shape) for x in operands] + [pl.BlockSpec(memory_space=pl.ANY)] * len(after)
    result = pl.pallas_call(
        functools.partial(act_kernel, len(parts), columns, tail, features),
        in_specs=in_specs,
        out_specs=[full_spec(x.shape) for x in outs],
        out_shape=outs,
        compiler_params=params(),
        cost_estimate=pl.CostEstimate(flops=1, bytes_accessed=1, transcendentals=0),
        name=name,
    )(*operands, *after)
    return (result[0], result[1]) if tail else (result[0], stats)


def lane_window(offset_ref, expert, pairs, window):
    first = offset_ref[expert]
    start = pl.multiple_of(jnp.minimum(first // LANES * LANES, pairs - window), LANES)
    lanes = lax.broadcasted_iota(jnp.int32, (1, window), 1) + start
    return pl.ds(start, window), (lanes >= first) & (lanes < offset_ref[expert + 1])


def down_kernel(half, chunks, tail, window, begins, ends, offset_ref, order_ref, *refs):
    gathered = []
    for _ in chunks:
        gathered.append((refs[:half], refs[half]))
        refs = refs[half + 1 :]
    w_ref, refs = refs[0], refs[1:]
    if not begins:
        before_ref, refs = refs[0], refs[1:]
    if ends:
        place_ref, resid_ref, out_ref, total_ref, *held = refs
    else:
        total_ref, *held = refs
    experts = w_ref.shape[0]
    pairs = held[0].shape[0]
    for (parts, other_ref), into in zip(gathered, held):
        block = parts[0].shape[0]
        for slot in range(half):
            mine = pl.ds(pl.multiple_of(order_ref[slot] * block, block), block)
            other = pl.ds(pl.multiple_of(order_ref[half + slot] * block, block), block)
            into[mine] = parts[slot][...]
            into[other] = other_ref[slot]
    total_ref[...] = jnp.zeros_like(total_ref) if begins else before_ref[...]
    for index, (begin, columns) in enumerate(chunks):
        for expert in range(experts):
            lanes, valid = lane_window(offset_ref, expert, pairs, window)
            result = dot_nt(w_ref[expert, :, begin : begin + columns], held[index][lanes, :columns])
            if tail and index == 0:
                units, size = w_ref.shape[2], tail[3]
                result = result + dot_nt(
                    w_ref[expert, :, units - size :], held[index][lanes, columns : columns + size]
                )
            total_ref[:, lanes] = total_ref[:, lanes] + jnp.where(valid, result, 0.0)

    if ends:
        total = out_ref.shape[0]
        pieces = [x.astype(BF16) for x in split_bf16(total_ref[...], 2)]
        resid = [x.astype(BF16) for x in split_bf16(resid_ref[...], 2)]
        step = pair_block(total)
        for start in range(0, total, step):
            here = slice(start, start + step)
            pair = lax.broadcasted_iota(jnp.int32, (step, pairs), 1)
            place = place_ref[here].astype(jnp.int32)
            pick = (pair == place[:, 0:1]) | (pair == place[:, 1:2])
            pick = pick.astype(F32).astype(BF16)
            token = lax.broadcasted_iota(jnp.int32, (step, total), 1)
            move = (token == place[:, 2:3]).astype(F32).astype(BF16)
            result = dot_nt(pick, pieces[0]) + dot_nt(pick, pieces[1])
            result = result + dot_nt(move, resid[0]) + dot_nt(move, resid[1])
            out_ref[here] = result.astype(BF16)


def stack_kernel(counts, *refs):
    outs = refs[-len(counts) :]
    for count, out in zip(counts, outs):
        parts, refs = refs[:count], refs[count:]
        for k, part in enumerate(parts):
            out[k] = part[...]


def stack_parts(lists, after):
    operands = [x for parts in lists for x in parts]
    outs = [jax.ShapeDtypeStruct((len(parts), *parts[0].shape), BF16) for parts in lists]
    return pl.pallas_call(
        functools.partial(stack_kernel, [len(parts) for parts in lists]),
        in_specs=[full_spec(x.shape) for x in operands] + [pl.BlockSpec(memory_space=pl.ANY)] * len(after),
        out_specs=[full_spec(x.shape) for x in outs],
        out_shape=outs,
        compiler_params=params(),
        cost_estimate=pl.CostEstimate(flops=1, bytes_accessed=1, transcendentals=0),
        name="stack_parts",
    )(*operands, *after)


def chunk_columns(units):
    full = units // LANES
    count = 3 if full >= 6 else 1
    ends = [-(-full * (k + 1) // count) for k in range(count)]
    return [(LANES * (e - n), LANES * n) for e, n in zip(ends, [b - a for a, b in zip([0, *ends], ends)])]


def local(
    hidden_in,
    cache_pool,
    project_in,
    project_out,
    norm_first,
    norm_second,
    router,
    gate_up,
    expert_down,
    lengths,
    prompt_pages,
    own_pages,
    groups,
    move_target,
    routes,
):
    dp = lax.axis_size("dp")
    fs = lax.axis_size("fsdp")
    half = dp // 2
    my_row = lax.axis_index("dp")
    my_column = lax.axis_index("fsdp")
    my_chip, my_core = my_row // 2, my_row % 2
    req, features = hidden_in.shape
    row = req * fs
    total = row * dp
    pairs = 2 * total
    width = project_in.shape[0]
    cols = cache_pool.shape[3]
    heads = cols // HD
    page_len = cache_pool.shape[1]
    movers = move_target.shape[1]
    staying = row - movers
    experts = router.shape[1]
    units = gate_up.shape[3]
    window = windows(pairs, CAP * dp * fs)

    hidden_in = pltpu.with_memory_space_constraint(hidden_in, pltpu.HBM)
    project_in = project_in.transpose(1, 0, 2)
    routes = pltpu.with_memory_space_constraint(routes.T, pltpu.HBM)
    gate_up = pltpu.with_memory_space_constraint(gate_up, pltpu.HBM)
    expert_down = pltpu.with_memory_space_constraint(expert_down, pltpu.HBM)

    chip = jnp.arange(half, dtype=jnp.int32)
    row_ids = jnp.arange(dp, dtype=jnp.int32)
    order = jnp.concatenate([(chip ^ my_chip) * 2 + my_core, (chip ^ my_chip) * 2 + 1 - my_core])

    def swap(x):
        return lax.ppermute(x, "dp", [(i, i ^ 1) for i in range(dp)])

    def over_chips(x, s):
        return lax.ppermute(x, "dp", [(i, i ^ (2 * s)) for i in range(dp)])

    def over_columns(x, s):
        return lax.ppermute(x, "fsdp", [(i, i ^ s) for i in range(fs)])

    payload = pack(hidden_in, routes, dp, fs)
    recv = lax.all_to_all(
        payload.reshape(dp * fs, req, payload.shape[3]), ("dp", "fsdp"), 0, 0, tiled=True
    ).reshape(total, payload.shape[3])

    row_lengths = lax.dynamic_slice_in_dim(lengths, my_row * row, row)
    lists = jnp.concatenate([own_pages, groups[:, None], row_lengths[:, None]], axis=1)
    lane = jnp.arange(cols, dtype=jnp.int32)
    channel = (lane % (HD // 2)).astype(F32)
    inverse = jnp.exp(-jnp.log(10000.0) * 2.0 * channel / HD)
    angles = row_lengths.astype(F32)[:, None] * inverse[None, :]
    cosine = jnp.cos(angles)
    sine = jnp.where((lane % HD < HD // 2)[None, :], -1.0, 1.0) * jnp.sin(angles)

    def slice_of(vector):
        return lax.dynamic_slice_in_dim(vector, my_row * width, width)

    gate_tail, token = last_units(gate_up, payload)
    keep, send, raw = project_qkv(
        order,
        recv,
        slice_of(norm_first).astype(F32)[None, :],
        project_in,
        half,
        row,
        token,
    )
    sums = sum_parts(keep, swap(send), [[s] for s in range(half)], None, "core_sum_qkv")
    slot_of = (row_ids % 2 ^ my_core) * half + (row_ids // 2 ^ my_chip)
    column = jnp.stack([my_column, jnp.int32(fs)]).astype(jnp.int32)
    offsets, place_table, line_table = pair_places(
        move_target, order, slot_of, column, recv, sums[0], experts, width
    )
    keys, values, bias = split_pool(prompt_pages, lists, cache_pool, place_table)
    parts = [sums[0]] + [over_chips(sums[s], s) for s in range(1, half)]
    heads_out = attend(parts, cosine, sine, bias, keys, values, place_table)

    parts = [heads_out] + [over_chips(heads_out, s) for s in range(1, half)]
    other = swap(jnp.concatenate(parts, axis=0))
    projected = project_heads(parts, other, project_out.T)
    parts = [projected] + [over_columns(projected, s) for s in range(1, fs)]
    chunks = chunk_columns(units)
    gate_first, gate_tail = stage_gate(gate_up, gate_tail, *chunks[0], projected)

    tail = tail_layout(units)
    block = pairs // dp
    anywhere = pl.BlockSpec(memory_space=pl.ANY)
    spread = jax.ShapeDtypeStruct((2, pairs, 2 * width), BF16)
    resid_shape = jax.ShapeDtypeStruct((width, total), F32)
    norm_column = slice_of(norm_second).astype(F32)[:, None]
    router_slice = lax.dynamic_slice_in_dim(router, my_row * width, width).T
    state = {"after": [line_table]}
    flight = []

    def waits():
        after, flight[:] = state["after"] + flight, []
        return after

    def gate(index):
        after = state["after"]
        begin, columns = chunks[index]
        first = index == 0
        out_width = 2 * columns + (tail[0] if first else 0)
        half_out = jax.ShapeDtypeStruct((half, block, out_width), BF16)
        scratch = [pltpu.VMEM((pairs, out_width), BF16)]
        weights = [pltpu.VMEM((SLOTS, width, 2, columns), BF16), pltpu.SemaphoreType.DMA((SLOTS,))]
        if first:
            operands = [*parts, raw.T, norm_column, router_slice, line_table]
            in_specs = [full_spec(x.shape) for x in operands] + [full_spec(gate_tail.shape)]
            operands.append(gate_tail)
            outs = [half_out, half_out, resid_shape, spread]
            scratch.append(pltpu.VMEM((pairs, LANES), F32))
        else:
            operands = [state["spread"]]
            in_specs = [full_spec(spread.shape)]
            outs = [half_out, half_out]
            scratch += weights
        result = pl.pallas_call(
            functools.partial(gate_kernel, len(parts) if first else 0, begin, columns, tail, window, len(after)),
            in_specs=[SCALARS] * 2 + [anywhere] * len(after) + [*in_specs, full_spec(gate_first.shape) if first else anywhere],
            out_specs=[full_spec(x.shape) for x in outs],
            scratch_shapes=scratch,
            out_shape=outs,
            compiler_params=params(room(total)),
            cost_estimate=pl.CostEstimate(flops=1, bytes_accessed=1, transcendentals=0),
            name=f"gate_up_{index}",
        )(offsets, order, *after, *operands, gate_first if first else gate_up)
        if first:
            state["resid"], state["spread"] = result[2:]
        state["after"] = [result[0]]
        return result[:2]

    def combine(index, bit, held, hold=None):
        aux_at = 2 * chunks[index][1] + tail[2] if index == 0 else None
        sums = sum_parts(
            *held, halves(held[0].shape[0]), aux_at, f"sum_{index}_{bit}", waits() if bit else state["after"], hold
        )
        kept, sent = sums[-2:]
        state["after"] = [kept]
        received = over_chips(sent, 1 << bit)
        flying.append(received)
        return [kept, received], sums[0]

    def activate(index, held):
        act, state["stats"] = activation(
            held,
            state.get("stats"),
            chunks[index][1],
            tail if index == 0 else None,
            float(features),
            f"activation_{index}",
            waits(),
        )
        state["after"] = [act]
        return act

    def spread_out(parts, fresh):
        more = {}
        for s in fresh:
            low = (s & -s).bit_length() - 1 if s else stages
            for bit in range(low):
                more[s | 1 << bit] = over_chips(parts[s], 1 << bit)
        flying.extend(more.values())
        parts.update(more)
        return list(more)

    def down(numbers, lists, after):
        first, last = numbers[0] == 0, numbers[-1] == len(chunks) - 1
        stacked = stack_parts(lists, after)
        others = [swap(x) for x in stacked]
        operands = [x for parts, other in zip(lists, others) for x in (*parts, other)]
        operands.append(down_held)
        in_specs = [full_spec(x.shape) for x in operands]
        if not first:
            operands.append(state["sum"])
            in_specs.append(full_spec(state["sum"].shape))
        sum_shape = jax.ShapeDtypeStruct((width, pairs), F32)
        scratch = [pltpu.VMEM((pairs, parts[0].shape[1]), BF16) for parts in lists]
        outs = [sum_shape]
        if last:
            operands += [place_table, state["resid"]]
            in_specs += [full_spec(place_table.shape), full_spec(state["resid"].shape)]
            outs = [jax.ShapeDtypeStruct((total, width), BF16)]
            scratch = [pltpu.VMEM(sum_shape.shape, F32)] + scratch
        result = pl.pallas_call(
            functools.partial(
                down_kernel,
                half,
                [chunks[k] for k in numbers],
                tail if first else None,
                min(-(-CAP * dp * fs // LANES) * LANES + LANES, pairs),
                first,
                last,
            ),
                    in_specs=[SCALARS] * 2 + in_specs,
            out_specs=[full_spec(x.shape) for x in outs],
            scratch_shapes=scratch,
            out_shape=outs,
            compiler_params=params(room(total)),
            cost_estimate=pl.CostEstimate(flops=1, bytes_accessed=1, transcendentals=0),
            name=f"down_{numbers[0]}",
        )(offsets, order, *operands)[0]
        state["sum"] = result
        return result

    stages = half.bit_length() - 1
    count = len(chunks)
    early = max(0, count - stages)
    held, gathered, fresh = {}, {}, {}
    flying = []
    for step in range(count + stages):
        sent = None
        if step < count:
            kept, sent = gate(step)
        if step == count - 1:
            down_held = stage_down(expert_down, state["after"][0])
        for k in range(count):
            if step - k == stages:
                if step == count - 1 + stages:
                    flight.append(down_held)
                gathered[k] = {0: activate(k, held[k])}
                if k < count - 1:
                    fresh[k] = spread_out(gathered[k], [0])
                else:
                    gathered[k].update({s: over_chips(gathered[k][0], s) for s in range(1, half)})
            elif 1 <= step - k < stages:
                held[k], through = combine(k, step - k, held[k], sent)
                sent = None if sent is None else through
        if step < count:
            held[step], _ = combine(step, 0, [kept, swap(sent)])
        for k in range(count - 1):
            if stages < step - k:
                fresh[k] = spread_out(gathered[k], fresh[k])
        flight.extend(flying)
        flying.clear()
    while any(fresh.values()):
        fresh = {k: spread_out(gathered[k], fresh[k]) for k in fresh}
    lists = [[gathered[k][s] for s in range(half)] for k in range(count)]
    last_after = state["after"]
    if early:
        last_after = [down(list(range(early)), lists[:early], state["after"])]
    result = down(list(range(early, count)), lists[early:], last_after)

    back = lax.all_to_all(result.reshape(dp * fs, req, width), ("dp", "fsdp"), 0, 0, tiled=True)
    back = back.reshape(dp, fs, req, width).astype(F32)
    return jnp.sum(back, axis=1).transpose(1, 0, 2).reshape(req, features).astype(BF16)


def solution(mesh):
    placed = (
        P(("dp", "fsdp"), None),
        P("dp", None, None, "fsdp"),
        P("dp", None, "fsdp"),
        P("fsdp", "dp"),
        P(),
        P(),
        P(),
        P(None, "dp", None, "fsdp"),
        P(None, "dp", "fsdp"),
        P(),
        P("dp", None),
        P("dp", None),
        P("dp"),
        P(),
        P(("dp", "fsdp"), None),
    )
    return jax.shard_map(
        local, mesh=mesh, in_specs=placed, out_specs=P(("dp", "fsdp"), None), check_vma=False
    )
```

```python
import functools

import jax
import jax.numpy as jnp
from jax import lax
from jax.experimental import pallas as pl
from jax.experimental.pallas import tpu as pltpu
from jax.sharding import PartitionSpec as P

HD = 64
CAP = 4
PIECES = 3
LANES = 128
BF16 = jnp.bfloat16
F32 = jnp.float32
FAR = -3.0e38
SMALL, ATTENTION, LARGE = 16, 24, 60
SLOTS = 8


def params(mib=SMALL):
    return pltpu.CompilerParams(vmem_limit_bytes=mib * 2**20)


def room(tokens):
    return SMALL if tokens <= 512 else LARGE


def dot_nn(a, b):
    return lax.dot_general(a, b, (((1,), (0,)), ((), ())), preferred_element_type=F32)


def dot_nt(a, b):
    return lax.dot_general(a, b, (((1,), (1,)), ((), ())), preferred_element_type=F32)


def split_bf16(value, count=PIECES):
    pieces = []
    for _ in range(count):
        piece = value.astype(BF16).astype(F32)
        pieces.append(piece)
        value = value - piece
    return pieces


def full_spec(shape):
    return pl.BlockSpec(memory_space=pltpu.VMEM)


def block_spec(shape):
    zeros = (0,) * len(shape)
    return pl.BlockSpec(tuple(shape), lambda *_: zeros)


SCALARS = pl.BlockSpec(memory_space=pltpu.SMEM)


def pack_kernel(hidden_hbm, routes_hbm, out_ref, hidden_ref, routes_ref, sems):
    copies = [
        pltpu.make_async_copy(hidden_hbm, hidden_ref, sems.at[0]),
        pltpu.make_async_copy(routes_hbm, routes_ref, sems.at[1]),
    ]
    for copy in copies:
        copy.start()
    for copy in copies:
        copy.wait()
    slices, copies, req, room = out_ref.shape
    features = hidden_ref.shape[1]
    width = features // slices
    values = hidden_ref[...].astype(F32)
    factor = lax.rsqrt(jnp.mean(values * values, axis=1, keepdims=True) + 1e-06)
    lane = lax.broadcasted_iota(jnp.int32, (req, room), 1)
    extra = jnp.zeros((req, room), F32)
    for k, piece in enumerate(split_bf16(factor)):
        extra = jnp.where(lane == width + k, piece, extra)
    spot = lax.broadcasted_iota(jnp.int32, (req, req), 1) == lax.broadcasted_iota(jnp.int32, (req, req), 0)
    for k in range(2):
        route = jnp.sum(jnp.where(spot, routes_ref[k : k + 1].astype(F32), 0.0), axis=1, keepdims=True)
        extra = jnp.where(lane == width + PIECES + k, route, extra)
    for index in range(slices):
        moved = pltpu.roll(values, (features - index * width) % features, 1) if index else values
        block = jnp.where(lane < width, moved[:, :room], extra).astype(BF16)
        for copy in range(copies):
            out_ref[index, copy] = block


def pack(hidden_in, routes, slices, copies):
    req, features = hidden_in.shape
    width = features // slices
    room = -(-(width + PIECES + 2) // LANES) * LANES
    out = (slices, copies, req, room)
    return pl.pallas_call(
        pack_kernel,
        in_specs=[pl.BlockSpec(memory_space=pl.ANY)] * 2,
        out_specs=full_spec(out),
        scratch_shapes=[
            pltpu.VMEM(hidden_in.shape, BF16),
            pltpu.VMEM(routes.shape, jnp.int32),
            pltpu.SemaphoreType.DMA((2,)),
        ],
        out_shape=jax.ShapeDtypeStruct(out, BF16),
        compiler_params=params(),
        cost_estimate=pl.CostEstimate(flops=1, bytes_accessed=1, transcendentals=0),
        name="pack",
    )(hidden_in, routes)


def places_kernel(
    experts, width, staying, move_ref, order_ref, slot_ref, column_ref, recv_ref, _, off_ref, place_ref, line_ref, table, slots
):
    total = recv_ref.shape[0]
    rows_count, movers = move_ref.shape
    row = total // rows_count
    block = min(total, 256)
    lane = lax.broadcasted_iota(jnp.int32, (block, LANES), 1)
    above = lax.broadcasted_iota(jnp.int32, (block, block), 0)
    beside = lax.broadcasted_iota(jnp.int32, (block, block), 1)
    before = (beside < above).astype(F32).astype(BF16)
    counts = jnp.zeros((1, LANES), F32)
    for start in range(0, total, block):
        here = slice(start, start + block)
        first = recv_ref[here, width + PIECES : width + PIECES + 1].astype(F32).astype(jnp.int32)
        second = recv_ref[here, width + PIECES + 1 : width + PIECES + 2].astype(F32).astype(jnp.int32)
        member = (lane == first).astype(F32) + (lane == second).astype(F32)
        rank = dot_nn(before, member.astype(BF16)) + counts
        counts = counts + jnp.sum(member, axis=0, keepdims=True)
        mine = jnp.sum(jnp.where(lane == first, rank, 0.0), axis=1, keepdims=True)
        other = jnp.sum(jnp.where(lane == second, rank, 0.0), axis=1, keepdims=True)
        block_table = jnp.where(lane == 0, mine, jnp.where(lane == 1, other, 0.0))
        block_table = jnp.where(lane == 2, first.astype(F32), block_table)
        table[here] = jnp.where(lane == 3, second.astype(F32), block_table)
    single = lax.broadcasted_iota(jnp.int32, (1, LANES), 1)
    sums = [jnp.sum(jnp.where(single == e, counts, 0.0)) for e in range(experts)]
    off_ref[0] = 0
    running = jnp.float32(0.0)
    begins = jnp.zeros((1, LANES), F32)
    for e in range(experts):
        begins = jnp.where(single == e, running, begins)
        running = running + sums[e]
        off_ref[e + 1] = running.astype(jnp.int32)
    for start in range(0, total, block):
        here = slice(start, start + block)
        values = table[here]
        first = values[:, 2:3].astype(jnp.int32)
        second = values[:, 3:4].astype(jnp.int32)
        begin_first = jnp.sum(jnp.where(lane == first, begins, 0.0), axis=1, keepdims=True)
        begin_second = jnp.sum(jnp.where(lane == second, begins, 0.0), axis=1, keepdims=True)
        values = values + jnp.where(lane == 0, begin_first, jnp.where(lane == 1, begin_second, 0.0))
        table[here] = values
        place_ref[here] = values
    within = lax.broadcasted_iota(jnp.int32, (row, LANES), 0)
    wide = lax.broadcasted_iota(jnp.int32, (row, LANES), 1)
    req = row // column_ref[1]
    mine = (within >= column_ref[0] * req) & (within < (column_ref[0] + 1) * req)
    for r in range(rows_count):
        here = slice(r * row, (r + 1) * row)
        lies = jnp.where(mine, (within + slot_ref[r] * row).astype(F32), -1.0)
        place_ref[here] = jnp.where(wide == 2, lies, place_ref[here])
    for r in range(rows_count):
        for j in range(movers):
            at = staying + j
            target = pl.ds(move_ref[r, j] * row + at, 1)
            held = (at >= column_ref[0] * req) & (at < (column_ref[0] + 1) * req)
            lies = jnp.where(held, slot_ref[r] * row + at, -1).astype(F32)
            place_ref[target] = jnp.where(single == 2, lies, place_ref[target])
    for b in range(rows_count):
        slots[b * row : (b + 1) * row] = table[pl.ds(pl.multiple_of(order_ref[b] * row, row), row)]
        for j in range(movers):
            at = staying + j
            source = pl.ds(move_ref[order_ref[b], j] * row + at, 1)
            slots[b * row + at : b * row + at + 1] = table[source]
    line_ref[...] = slots[...].T[:8]


def pair_places(move_target, order, slot_of, column, recv, after, experts, width):
    total = recv.shape[0]
    rows_count, movers = move_target.shape
    staying = total // rows_count - movers
    outs = [
        jax.ShapeDtypeStruct((experts + 1,), jnp.int32),
        jax.ShapeDtypeStruct((total, LANES), F32),
        jax.ShapeDtypeStruct((8, total), F32),
    ]
    return pl.pallas_call(
        functools.partial(places_kernel, experts, width, staying),
        in_specs=[SCALARS] * 4 + [full_spec(recv.shape), pl.BlockSpec(memory_space=pl.ANY)],
        out_specs=[
            pl.BlockSpec(memory_space=pltpu.SMEM),
            full_spec(outs[1].shape),
            full_spec(outs[2].shape),
        ],
        scratch_shapes=[pltpu.VMEM((total, LANES), F32), pltpu.VMEM((total, LANES), F32)],
        out_shape=outs,
        compiler_params=params(room(total)),
        cost_estimate=pl.CostEstimate(flops=1, bytes_accessed=1, transcendentals=0),
        name="pair_places",
    )(move_target, order, slot_of, column, recv, after)


def pool_kernel(prompt_ref, lists_ref, pool_ref, _, key_ref, value_ref, bias_ref):
    pages, page_len, _, cols = pool_ref.shape
    rows = pages * page_len
    both = pool_ref[...].reshape(2 * rows, cols)
    part = min(rows, LANES)
    wide = lax.broadcasted_iota(jnp.int32, (part, 2 * part), 1)
    high = lax.broadcasted_iota(jnp.int32, (part, 2 * part), 0)
    even = (wide == 2 * high).astype(F32).astype(BF16)
    odd = (wide == 2 * high + 1).astype(F32).astype(BF16)
    for start in range(0, rows, part):
        piece = both[2 * start : 2 * (start + part)]
        key_ref[start : start + part] = dot_nn(even, piece).astype(BF16)
        value_ref[start : start + part] = dot_nn(odd, piece).astype(BF16)
    requests = bias_ref.shape[0]
    prompts, prompt_len = prompt_ref.shape
    own_len = lists_ref.shape[1] - 2
    group, length = lists_ref[:, own_len : own_len + 1], lists_ref[:, own_len + 1 :]
    spot = lax.broadcasted_iota(jnp.int32, (requests, rows), 1)
    page = spot // page_len + pl.program_id(0) * pages
    reach = jnp.zeros((requests, rows), jnp.int32)
    for k in range(prompt_len):
        listed = jnp.zeros((requests, 1), jnp.int32)
        for g in range(prompts):
            listed = jnp.where(group == g, prompt_ref[g, k], listed)
        reach = jnp.where(page == listed, length - page_len * k, reach)
    for k in range(own_len):
        reach = jnp.where(page == lists_ref[:, k : k + 1], length - page_len * (prompt_len + k), reach)
    bias_ref[...] = jnp.where(spot % page_len < reach, 0.0, FAR)


def split_pool(prompt_pages, lists, cache_pool, after):
    pages, page_len, _, cols = cache_pool.shape
    requests = lists.shape[0]
    block = next(b for b in (16, 8, 4, 2, 1) if pages % b == 0)
    out = jax.ShapeDtypeStruct((pages * page_len, cols), BF16)
    spec = pl.BlockSpec((block * page_len, cols), lambda b, *_: (b, 0))
    return pl.pallas_call(
        pool_kernel,
        grid_spec=pltpu.PrefetchScalarGridSpec(
            num_scalar_prefetch=1,
            grid=(pages // block,),
            in_specs=[
                block_spec(lists.shape),
                pl.BlockSpec((block, page_len, 2, cols), lambda b, *_: (b, 0, 0, 0)),
                pl.BlockSpec(memory_space=pl.ANY),
            ],
            out_specs=[spec, spec, pl.BlockSpec((requests, block * page_len), lambda b, *_: (0, b))],
        ),
        out_shape=[out, out, jax.ShapeDtypeStruct((requests, pages * page_len), F32)],
        compiler_params=params(),
        cost_estimate=pl.CostEstimate(flops=1, bytes_accessed=1, transcendentals=0),
        name="pool_split",
    )(prompt_pages, lists, cache_pool, after)


def qkv_kernel(order_ref, recv_ref, norm_ref, w_ref, _, keep_ref, send_ref, raw_ref, normed, slots):
    width = norm_ref.shape[1]
    half, row, _ = keep_ref.shape
    cols = w_ref.shape[2]
    values = recv_ref[:, :width]
    scale = recv_ref[:, width : width + 1].astype(F32)
    for piece in range(1, PIECES):
        scale = scale + recv_ref[:, width + piece : width + piece + 1].astype(F32)
    normed[...] = (values.astype(F32) * scale * norm_ref[...]).astype(BF16)
    for slot in range(2 * half):
        rows = pl.ds(pl.multiple_of(order_ref[slot] * row, row), row)
        slots[slot * row : (slot + 1) * row] = normed[rows]
        raw_ref[slot * row : (slot + 1) * row] = recv_ref[rows, :width]
    for part in range(3):
        here = slice(part * cols, (part + 1) * cols)
        result = dot_nn(slots[...], w_ref[part]).astype(BF16).reshape(2 * half, row, cols)
        keep_ref[:, :, here] = result[:half]
        send_ref[:, :, here] = result[half:]


def project_qkv(order, recv, norm_slice, weights, half, row, after):
    total, _ = recv.shape
    width, cols = weights.shape[1:]
    out = jax.ShapeDtypeStruct((half, row, 3 * cols), BF16)
    raw = jax.ShapeDtypeStruct((total, width), BF16)
    return pl.pallas_call(
        qkv_kernel,
        in_specs=[SCALARS] * 1 + [full_spec(x.shape) for x in (recv, norm_slice, weights)] + [pl.BlockSpec(memory_space=pl.ANY)],
        out_specs=[full_spec(out.shape), full_spec(out.shape), full_spec(raw.shape)],
        scratch_shapes=[pltpu.VMEM((total, width), BF16), pltpu.VMEM((total, width), BF16)],
        out_shape=[out, out, raw],
        compiler_params=params(room(total)),
        cost_estimate=pl.CostEstimate(flops=1, bytes_accessed=1, transcendentals=0),
        name="qkv",
    )(order, recv, norm_slice, weights, after)


def attention_kernel(*refs):
    parts, refs = refs[:-9], refs[-9:]
    cos_ref, sin_ref, bias_ref, key_ref, value_ref, _, out_ref, scores, probs = refs
    row, cols = out_ref.shape
    heads = cols // HD
    total = parts[0][0].astype(F32)
    for part in parts[1:]:
        total = total + part[0].astype(F32)
    lane = lax.broadcasted_iota(jnp.int32, (row, cols), 1)
    first_half = lane % HD < HD // 2

    def rotate(values):
        partner = jnp.where(
            first_half, pltpu.roll(values, cols - HD // 2, 1), pltpu.roll(values, HD // 2, 1)
        )
        return (values * cos_ref[...] + partner * sin_ref[...]).astype(BF16)

    query = rotate(total[:, :cols]).astype(F32)
    key_new = rotate(total[:, cols : 2 * cols]).astype(F32)
    value_new = total[:, 2 * cols :].astype(BF16).astype(F32)
    spread = jnp.concatenate(
        [jnp.where(lane // HD == h, query, 0.0).astype(BF16) for h in range(heads)], axis=0
    )
    scores[...] = dot_nt(spread, key_ref[...])
    own_parts = []
    for h in range(heads):
        here = slice(h * row, (h + 1) * row)
        mine = lane // HD == h
        own = jnp.sum(jnp.where(mine, query * key_new, 0.0), axis=1, keepdims=True) * HD**-0.5
        score = scores[here] * HD**-0.5 + bias_ref[...]
        highest = jnp.maximum(jnp.max(score, axis=1, keepdims=True), own)
        weight = jnp.exp(score - highest)
        weight_own = jnp.exp(own - highest)
        inverse = 1.0 / (jnp.sum(weight, axis=1, keepdims=True) + weight_own)
        probs[here] = (weight * inverse).astype(BF16)
        own_parts.append((weight_own * inverse).astype(BF16).astype(F32))
    mixture = dot_nn(probs[...], value_ref[...])
    result = jnp.zeros((row, cols), F32)
    for h in range(heads):
        mixed = mixture[h * row : (h + 1) * row] + own_parts[h] * value_new
        result = jnp.where(lane // HD == h, mixed, result)
    out_ref[...] = result.astype(BF16)


def attend(parts, cosine, sine, bias, keys, values, after):
    row, cols = cosine.shape
    stretch = keys.shape[0]
    heads = cols // HD
    operands = [*parts, cosine, sine, bias, keys, values]
    return pl.pallas_call(
        attention_kernel,
        in_specs=[full_spec(x.shape) for x in operands] + [pl.BlockSpec(memory_space=pl.ANY)],
        out_specs=full_spec((row, cols)),
        out_shape=jax.ShapeDtypeStruct((row, cols), BF16),
        scratch_shapes=[
            pltpu.VMEM((heads * row, stretch), F32),
            pltpu.VMEM((heads * row, stretch), BF16),
        ],
        compiler_params=params(ATTENTION),
        cost_estimate=pl.CostEstimate(flops=1, bytes_accessed=1, transcendentals=0),
        name="attention",
    )(*operands, after)


def out_kernel(*refs):
    parts, (other_ref, w_ref, out_ref) = refs[:-3], refs[-3:]
    half = len(parts) * parts[0].shape[0]
    mine = jnp.concatenate([part[...] for part in parts], axis=0)
    out_ref[:, :half] = dot_nt(w_ref[...], mine).astype(BF16)
    out_ref[:, half:] = dot_nt(w_ref[...], other_ref[...]).astype(BF16)


def project_heads(parts, other, weights):
    half = other.shape[0]
    operands = [*parts, other, weights]
    out = (weights.shape[0], 2 * half)
    return pl.pallas_call(
        out_kernel,
        in_specs=[full_spec(x.shape) for x in operands],
        out_specs=full_spec(out),
        out_shape=jax.ShapeDtypeStruct(out, BF16),
        compiler_params=params(room(2 * half)),
        cost_estimate=pl.CostEstimate(flops=1, bytes_accessed=1, transcendentals=0),
        name="out_projection",
    )(*operands)


def pair_block(pairs):
    return next(b for b in (256, 128, 64, 32, 16) if pairs % b == 0)


def dispatch(parts, hid_ref, norm_ref, router_ref, line_ref, resid_ref, spread_ref, aux_ref, aux_at):
    width, total = hid_ref.shape
    pairs = spread_ref.shape[1]
    resid = hid_ref[...].astype(F32)
    for part in parts:
        resid = resid + part[...].astype(F32)
    resid_ref[...] = resid
    moe = (resid * norm_ref[...]).astype(BF16)
    squares = jnp.sum(resid * resid, axis=0, keepdims=True)
    logits = dot_nn(router_ref[...], moe)
    expert = lax.broadcasted_iota(jnp.int32, logits.shape, 0)
    line = line_ref[...].astype(jnp.int32)
    sign = (expert == line[2:3]).astype(F32) - (expert == line[3:4]).astype(F32)
    gap = jnp.sum(logits * sign, axis=0, keepdims=True)
    high = lax.broadcasted_iota(jnp.int32, (LANES, total), 0)
    aux_plain = jnp.zeros((LANES, total), F32)
    aux_signed = jnp.zeros((LANES, total), F32)
    for k, piece in enumerate(split_bf16(squares)):
        aux_plain = jnp.where(high == aux_at + k, piece, aux_plain)
    for k, piece in enumerate(split_bf16(gap)):
        aux_signed = jnp.where(high == aux_at + PIECES + k, piece, aux_signed)
    aux_plain = aux_plain.astype(BF16)
    aux_signed = aux_signed.astype(BF16)
    feature = lax.broadcasted_iota(jnp.int32, (width, 2 * width), 0)
    lane = lax.broadcasted_iota(jnp.int32, (width, 2 * width), 1)
    even = (lane == 2 * feature).astype(BF16)
    odd = (lane == 2 * feature + 1).astype(BF16)
    block = pair_block(pairs)
    for start in range(0, pairs, block):
        here = slice(start, start + block)
        pair = lax.broadcasted_iota(jnp.int32, (block, total), 0) + start
        first = (pair == line[0:1]).astype(F32)
        second = (pair == line[1:2]).astype(F32)
        both = (first + second).astype(BF16)
        rows = dot_nt(both, moe).astype(BF16)
        spread_ref[0, here] = dot_nn(rows, even).astype(BF16)
        spread_ref[1, here] = dot_nn(rows, odd).astype(BF16)
        aux_ref[here] = dot_nt(both, aux_plain) + dot_nt((first - second).astype(BF16), aux_signed)


def windows(pairs, per_expert):
    return min(per_expert + 16, pairs)


def window_of(offset_ref, expert, pairs, window):
    first = offset_ref[expert]
    start = pl.multiple_of(jnp.minimum(first // 16 * 16, pairs - window), 16)
    rows = lax.broadcasted_iota(jnp.int32, (window, 1), 0) + start
    return pl.ds(start, window), (rows >= first) & (rows < offset_ref[expert + 1])


def gate_kernel(count_parts, begin, columns, tail, window, waits, offset_ref, order_ref, *refs):
    first = count_parts > 0
    refs = refs[waits:]
    if first:
        parts, refs = refs[:count_parts], refs[count_parts:]
        hid_ref, norm_ref, router_ref, line_ref, tail_ref, w_ref = refs[:6]
        keep_ref, send_ref, resid_ref, spread_ref, held, aux = refs[6:]
    else:
        spread_ref, w_ref, keep_ref, send_ref, held, w_held, w_sems = refs
    experts = w_ref.shape[0]
    pairs = spread_ref.shape[1]
    width = spread_ref.shape[2] // 2
    if first:
        tail_width, _, aux_at, size = tail
        dispatch(parts, hid_ref, norm_ref, router_ref, line_ref, resid_ref, spread_ref, aux, aux_at % LANES)
    else:
        copies = [
            pltpu.make_async_copy(w_ref.at[e, :, :, pl.ds(begin, columns)], w_held.at[e % SLOTS], w_sems.at[e % SLOTS])
            for e in range(experts)
        ]
        for copy in copies[:SLOTS]:
            copy.start()

    for expert in range(experts):
        rows, valid = window_of(offset_ref, expert, pairs, window)
        left = jnp.concatenate([spread_ref[0, rows], spread_ref[1, rows]], axis=0)
        if first:
            weights = w_ref[expert]
        else:
            copies[expert].wait()
            weights = w_held[expert % SLOTS]
        result = dot_nn(left, weights.reshape(2 * width, columns)).astype(BF16)
        if not first and expert + SLOTS < experts:
            copies[expert + SLOTS].start()
        held[rows, :columns] = jnp.where(valid, result[:window], held[rows, :columns])
        held[rows, columns : 2 * columns] = jnp.where(
            valid, result[window:], held[rows, columns : 2 * columns]
        )
        if first:
            result = dot_nn(left, tail_ref[expert])
            lane = lax.broadcasted_iota(jnp.int32, (window, LANES), 1)
            gate, up = result[:window], result[window:]
            if tail_width == LANES:
                block = jnp.where(lane < size, gate, pltpu.roll(up, size, 1))
                block = jnp.where(lane < 2 * size, block, aux[rows])
            else:
                block = jnp.concatenate([gate, up, aux[rows]], axis=1)
            here = slice(2 * columns, 2 * columns + tail_width)
            held[rows, here] = jnp.where(valid, block.astype(BF16), held[rows, here])

    half, block, _ = keep_ref.shape
    for slot in range(half):
        mine = pl.ds(pl.multiple_of(order_ref[slot] * block, block), block)
        other = pl.ds(pl.multiple_of(order_ref[half + slot] * block, block), block)
        keep_ref[slot] = held[mine]
        send_ref[slot] = held[other]


def gate_tail_kernel(size, gate_ref, _, out_ref, token_ref):
    token_ref[...] = jnp.zeros_like(token_ref)
    experts, width, _, lanes = gate_ref.shape
    lane = lax.broadcasted_iota(jnp.int32, (2 * width, lanes), 1)
    for e in range(experts):
        out_ref[e] = jnp.where(lane < size, gate_ref[e].reshape(2 * width, lanes).astype(F32), 0.0).astype(BF16)


def last_units(weights, after):
    experts, width, _, units = weights.shape
    number, size = units // LANES, units % LANES
    out = (experts, 2 * width, LANES)
    return pl.pallas_call(
        functools.partial(gate_tail_kernel, size),
        grid=(1,),
        in_specs=[
            pl.BlockSpec((experts, width, 2, LANES), lambda *_: (0, 0, 0, number)),
            pl.BlockSpec(memory_space=pl.ANY),
        ],
        out_specs=[block_spec(out), block_spec((8, LANES))],
        out_shape=[pltpu.HBM(out, BF16), jax.ShapeDtypeStruct((8, LANES), F32)],
        compiler_params=params(),
        cost_estimate=pl.CostEstimate(flops=1, bytes_accessed=1, transcendentals=0),
        name="gate_tail",
    )(weights, after)


def stage_gate_kernel(begin, columns, w_ref, tail_ref, _, out_ref, tail_out, sems):
    copies = [
        pltpu.make_async_copy(w_ref.at[:, :, :, pl.ds(begin, columns)], out_ref, sems.at[0]),
        pltpu.make_async_copy(tail_ref, tail_out, sems.at[1]),
    ]
    for copy in copies:
        copy.start()
    for copy in copies:
        copy.wait()


def stage_gate(gate_up, tail, begin, columns, after):
    anywhere = pl.BlockSpec(memory_space=pl.ANY)
    return pl.pallas_call(
        functools.partial(stage_gate_kernel, begin, columns),
        in_specs=[anywhere] * 3,
        out_specs=[anywhere] * 2,
        out_shape=[pltpu.VMEM((*gate_up.shape[:3], columns), BF16), pltpu.VMEM(tail.shape, BF16)],
        scratch_shapes=[pltpu.SemaphoreType.DMA((2,))],
        compiler_params=params(),
        cost_estimate=pl.CostEstimate(flops=1, bytes_accessed=1, transcendentals=0),
        name="stage_gate",
    )(gate_up, tail, after)


def stage_down_kernel(w_ref, _, out_ref, sem):
    copy = pltpu.make_async_copy(w_ref, out_ref, sem)
    copy.start()
    copy.wait()


def stage_down(weights, after):
    return pl.pallas_call(
        stage_down_kernel,
        in_specs=[pl.BlockSpec(memory_space=pl.ANY)] * 2,
        out_specs=pl.BlockSpec(memory_space=pl.ANY),
        out_shape=pltpu.VMEM(weights.shape, BF16),
        scratch_shapes=[pltpu.SemaphoreType.DMA],
        compiler_params=params(),
        cost_estimate=pl.CostEstimate(flops=1, bytes_accessed=1, transcendentals=0),
        name="stage_down",
    )(weights, after)


def tail_layout(units):
    size = units % LANES
    if 2 * size + 2 * PIECES <= LANES:
        return LANES, size, 2 * size, size
    return 3 * LANES, LANES, 2 * LANES, size


def sum_kernel(aux_at, groups, keep_ref, recv_ref, *outs):
    outs = outs[-len(groups) :]
    width = keep_ref.shape[2]

    def added(slot):
        total = keep_ref[slot].astype(F32) + recv_ref[slot].astype(F32)
        if aux_at is None:
            return [(slice(0, width), total)]
        base = aux_at // LANES * LANES
        tile = total[:, base : base + LANES]
        lane = lax.broadcasted_iota(jnp.int32, tile.shape, 1)
        for start in (aux_at - base, aux_at - base + PIECES):
            value = tile[:, start : start + 1]
            for k in range(1, PIECES):
                value = value + tile[:, start + k : start + k + 1]
            for k, piece in enumerate(split_bf16(value)):
                tile = jnp.where(lane == start + k, piece, tile)
        spans = [(slice(base, base + LANES), tile)]
        if base:
            spans.append((slice(0, base), total[:, :base]))
        if base + LANES < width:
            spans.append((slice(base + LANES, width), total[:, base + LANES :]))
        return spans

    for group, out in zip(groups, outs):
        for k, slot in enumerate(group):
            for span, value in added(slot):
                out[k, :, span] = value.astype(BF16)


def sum_parts(keep, recv, groups, aux_at, name, after=(), hold=None):
    _, block, width = keep.shape
    outs = [jax.ShapeDtypeStruct((len(group), block, width), BF16) for group in groups]
    in_specs = [full_spec(keep.shape)] * 2 + [pl.BlockSpec(memory_space=pl.ANY)] * len(after)
    out_specs = [full_spec(out.shape) for out in outs]
    operands = [keep, recv, *after]
    aliases = {}
    if hold is not None:
        operands.append(hold)
        in_specs.append(pl.BlockSpec(memory_space=pl.ANY))
        outs.insert(0, jax.ShapeDtypeStruct(hold.shape, hold.dtype))
        out_specs.insert(0, pl.BlockSpec(memory_space=pl.ANY))
        aliases = {len(operands) - 1: 0}
    return pl.pallas_call(
        functools.partial(sum_kernel, aux_at, groups),
        in_specs=in_specs,
        out_specs=out_specs,
        out_shape=outs,
        input_output_aliases=aliases,
        compiler_params=params(),
        cost_estimate=pl.CostEstimate(flops=1, bytes_accessed=1, transcendentals=0),
        name=name,
    )(*operands)


def halves(count):
    return [list(range(0, count, 2)), list(range(1, count, 2))] if count > 1 else [[0]]


def act_kernel(count_parts, columns, tail, features, *refs):
    parts, refs = refs[:count_parts], refs[count_parts:]
    total = parts[0][0].astype(F32)
    for part in parts[1:]:
        total = total + part[0].astype(F32)
    if tail is None:
        stat_ref, act_ref = refs[0], refs[-1]
        inverse, weight = stat_ref[:, 0:1], stat_ref[:, 1:2]
    else:
        act_ref, stat_ref = refs[-2:]
        tail_width, up_at, aux_at, size = tail
        base = 2 * columns + aux_at
        squares = total[:, base : base + 1]
        gap = total[:, base + PIECES : base + PIECES + 1]
        for k in range(1, PIECES):
            squares = squares + total[:, base + k : base + k + 1]
            gap = gap + total[:, base + PIECES + k : base + PIECES + k + 1]
        inverse = lax.rsqrt(squares / features + 1e-06)
        weight = 1.0 / (1.0 + jnp.exp(-gap * inverse))
        lane = lax.broadcasted_iota(jnp.int32, (total.shape[0], LANES), 1)
        stat_ref[...] = jnp.where(lane == 0, inverse, weight)

    def activate(gate, up):
        gate = gate * inverse
        return gate / (1.0 + jnp.exp(-gate)) * (up * inverse) * weight

    act_ref[:, :columns] = activate(total[:, :columns], total[:, columns : 2 * columns]).astype(BF16)
    if tail is not None:
        block = total[:, 2 * columns : 2 * columns + LANES]
        if tail_width == LANES:
            up = pltpu.roll(block, LANES - size, 1)
        else:
            up = total[:, 2 * columns + LANES : 2 * columns + 2 * LANES]
        last = jnp.where(lane < size, activate(block, up), 0.0)
        act_ref[:, columns:] = last.astype(BF16)


def activation(parts, stats, columns, tail, features, name, after):
    rows = parts[0].shape[1]
    out = jax.ShapeDtypeStruct((rows, columns + (LANES if tail else 0)), BF16)
    stat = jax.ShapeDtypeStruct((rows, LANES), F32)
    operands = [*parts] + ([] if tail else [stats])
    outs = [out, stat] if tail else [out]
    in_specs = [full_spec(x.shape) for x in operands] + [pl.BlockSpec(memory_space=pl.ANY)] * len(after)
    result = pl.pallas_call(
        functools.partial(act_kernel, len(parts), columns, tail, features),
        in_specs=in_specs,
        out_specs=[full_spec(x.shape) for x in outs],
        out_shape=outs,
        compiler_params=params(),
        cost_estimate=pl.CostEstimate(flops=1, bytes_accessed=1, transcendentals=0),
        name=name,
    )(*operands, *after)
    return (result[0], result[1]) if tail else (result[0], stats)


def lane_window(offset_ref, expert, pairs, window):
    first = offset_ref[expert]
    start = pl.multiple_of(jnp.minimum(first // LANES * LANES, pairs - window), LANES)
    lanes = lax.broadcasted_iota(jnp.int32, (1, window), 1) + start
    return pl.ds(start, window), (lanes >= first) & (lanes < offset_ref[expert + 1])


def down_kernel(half, chunks, tail, window, begins, ends, offset_ref, order_ref, *refs):
    gathered = []
    for _ in chunks:
        gathered.append((refs[:half], refs[half]))
        refs = refs[half + 1 :]
    w_ref, refs = refs[0], refs[1:]
    if not begins:
        before_ref, refs = refs[0], refs[1:]
    if ends:
        place_ref, resid_ref, out_ref, total_ref, *held = refs
    else:
        total_ref, *held = refs
    experts = w_ref.shape[0]
    pairs = held[0].shape[0]
    for (parts, other_ref), into in zip(gathered, held):
        block = parts[0].shape[0]
        for slot in range(half):
            mine = pl.ds(pl.multiple_of(order_ref[slot] * block, block), block)
            other = pl.ds(pl.multiple_of(order_ref[half + slot] * block, block), block)
            into[mine] = parts[slot][...]
            into[other] = other_ref[slot]
    total_ref[...] = jnp.zeros_like(total_ref) if begins else before_ref[...]
    for index, (begin, columns) in enumerate(chunks):
        for expert in range(experts):
            lanes, valid = lane_window(offset_ref, expert, pairs, window)
            result = dot_nt(w_ref[expert, :, begin : begin + columns], held[index][lanes, :columns])
            if tail and index == 0:
                units, size = w_ref.shape[2], tail[3]
                result = result + dot_nt(
                    w_ref[expert, :, units - size :], held[index][lanes, columns : columns + size]
                )
            total_ref[:, lanes] = total_ref[:, lanes] + jnp.where(valid, result, 0.0)

    if ends:
        total = out_ref.shape[0]
        pieces = [x.astype(BF16) for x in split_bf16(total_ref[...], 2)]
        resid = [x.astype(BF16) for x in split_bf16(resid_ref[...], 2)]
        step = pair_block(total)
        for start in range(0, total, step):
            here = slice(start, start + step)
            pair = lax.broadcasted_iota(jnp.int32, (step, pairs), 1)
            place = place_ref[here].astype(jnp.int32)
            pick = (pair == place[:, 0:1]) | (pair == place[:, 1:2])
            pick = pick.astype(F32).astype(BF16)
            token = lax.broadcasted_iota(jnp.int32, (step, total), 1)
            move = (token == place[:, 2:3]).astype(F32).astype(BF16)
            result = dot_nt(pick, pieces[0]) + dot_nt(pick, pieces[1])
            result = result + dot_nt(move, resid[0]) + dot_nt(move, resid[1])
            out_ref[here] = result.astype(BF16)


def stack_kernel(counts, *refs):
    outs = refs[-len(counts) :]
    for count, out in zip(counts, outs):
        parts, refs = refs[:count], refs[count:]
        for k, part in enumerate(parts):
            out[k] = part[...]


def stack_parts(lists, after):
    operands = [x for parts in lists for x in parts]
    outs = [jax.ShapeDtypeStruct((len(parts), *parts[0].shape), BF16) for parts in lists]
    return pl.pallas_call(
        functools.partial(stack_kernel, [len(parts) for parts in lists]),
        in_specs=[full_spec(x.shape) for x in operands] + [pl.BlockSpec(memory_space=pl.ANY)] * len(after),
        out_specs=[full_spec(x.shape) for x in outs],
        out_shape=outs,
        compiler_params=params(),
        cost_estimate=pl.CostEstimate(flops=1, bytes_accessed=1, transcendentals=0),
        name="stack_parts",
    )(*operands, *after)


def chunk_columns(units):
    full = units // LANES
    count = 3 if full >= 6 else 1
    ends = [full * 4 // 11, full * 9 // 11, full] if count == 3 else [full]
    return [(LANES * (e - n), LANES * n) for e, n in zip(ends, [b - a for a, b in zip([0, *ends], ends)])]


def local(
    hidden_in,
    cache_pool,
    project_in,
    project_out,
    norm_first,
    norm_second,
    router,
    gate_up,
    expert_down,
    lengths,
    prompt_pages,
    own_pages,
    groups,
    move_target,
    routes,
):
    dp = lax.axis_size("dp")
    fs = lax.axis_size("fsdp")
    half = dp // 2
    my_row = lax.axis_index("dp")
    my_column = lax.axis_index("fsdp")
    my_chip, my_core = my_row // 2, my_row % 2
    req, features = hidden_in.shape
    row = req * fs
    total = row * dp
    pairs = 2 * total
    width = project_in.shape[0]
    cols = cache_pool.shape[3]
    heads = cols // HD
    page_len = cache_pool.shape[1]
    movers = move_target.shape[1]
    staying = row - movers
    experts = router.shape[1]
    units = gate_up.shape[3]
    window = windows(pairs, CAP * dp * fs)

    hidden_in = pltpu.with_memory_space_constraint(hidden_in, pltpu.HBM)
    project_in = project_in.transpose(1, 0, 2)
    routes = pltpu.with_memory_space_constraint(routes.T, pltpu.HBM)
    gate_up = pltpu.with_memory_space_constraint(gate_up, pltpu.HBM)
    expert_down = pltpu.with_memory_space_constraint(expert_down, pltpu.HBM)

    chip = jnp.arange(half, dtype=jnp.int32)
    row_ids = jnp.arange(dp, dtype=jnp.int32)
    order = jnp.concatenate([(chip ^ my_chip) * 2 + my_core, (chip ^ my_chip) * 2 + 1 - my_core])

    def swap(x):
        return lax.ppermute(x, "dp", [(i, i ^ 1) for i in range(dp)])

    def over_chips(x, s):
        return lax.ppermute(x, "dp", [(i, i ^ (2 * s)) for i in range(dp)])

    def over_columns(x, s):
        return lax.ppermute(x, "fsdp", [(i, i ^ s) for i in range(fs)])

    payload = pack(hidden_in, routes, dp, fs)
    recv = lax.all_to_all(
        payload.reshape(dp * fs, req, payload.shape[3]), ("dp", "fsdp"), 0, 0, tiled=True
    ).reshape(total, payload.shape[3])

    row_lengths = lax.dynamic_slice_in_dim(lengths, my_row * row, row)
    lists = jnp.concatenate([own_pages, groups[:, None], row_lengths[:, None]], axis=1)
    lane = jnp.arange(cols, dtype=jnp.int32)
    channel = (lane % (HD // 2)).astype(F32)
    inverse = jnp.exp(-jnp.log(10000.0) * 2.0 * channel / HD)
    angles = row_lengths.astype(F32)[:, None] * inverse[None, :]
    cosine = jnp.cos(angles)
    sine = jnp.where((lane % HD < HD // 2)[None, :], -1.0, 1.0) * jnp.sin(angles)

    def slice_of(vector):
        return lax.dynamic_slice_in_dim(vector, my_row * width, width)

    gate_tail, token = last_units(gate_up, payload)
    keep, send, raw = project_qkv(
        order,
        recv,
        slice_of(norm_first).astype(F32)[None, :],
        project_in,
        half,
        row,
        token,
    )
    sums = sum_parts(keep, swap(send), [[s] for s in range(half)], None, "core_sum_qkv")
    slot_of = (row_ids % 2 ^ my_core) * half + (row_ids // 2 ^ my_chip)
    column = jnp.stack([my_column, jnp.int32(fs)]).astype(jnp.int32)
    offsets, place_table, line_table = pair_places(
        move_target, order, slot_of, column, recv, sums[0], experts, width
    )
    keys, values, bias = split_pool(prompt_pages, lists, cache_pool, place_table)
    parts = [sums[0]] + [over_chips(sums[s], s) for s in range(1, half)]
    heads_out = attend(parts, cosine, sine, bias, keys, values, place_table)

    parts = [heads_out] + [over_chips(heads_out, s) for s in range(1, half)]
    other = swap(jnp.concatenate(parts, axis=0))
    projected = project_heads(parts, other, project_out.T)
    parts = [projected] + [over_columns(projected, s) for s in range(1, fs)]
    chunks = chunk_columns(units)
    gate_first, gate_tail = stage_gate(gate_up, gate_tail, *chunks[0], projected)

    tail = tail_layout(units)
    block = pairs // dp
    anywhere = pl.BlockSpec(memory_space=pl.ANY)
    spread = jax.ShapeDtypeStruct((2, pairs, 2 * width), BF16)
    resid_shape = jax.ShapeDtypeStruct((width, total), F32)
    norm_column = slice_of(norm_second).astype(F32)[:, None]
    router_slice = lax.dynamic_slice_in_dim(router, my_row * width, width).T
    state = {"after": [line_table]}
    flight = []

    def waits():
        after, flight[:] = state["after"] + flight, []
        return after

    def gate(index):
        after = state["after"]
        begin, columns = chunks[index]
        first = index == 0
        out_width = 2 * columns + (tail[0] if first else 0)
        half_out = jax.ShapeDtypeStruct((half, block, out_width), BF16)
        scratch = [pltpu.VMEM((pairs, out_width), BF16)]
        weights = [pltpu.VMEM((SLOTS, width, 2, columns), BF16), pltpu.SemaphoreType.DMA((SLOTS,))]
        if first:
            operands = [*parts, raw.T, norm_column, router_slice, line_table]
            in_specs = [full_spec(x.shape) for x in operands] + [full_spec(gate_tail.shape)]
            operands.append(gate_tail)
            outs = [half_out, half_out, resid_shape, spread]
            scratch.append(pltpu.VMEM((pairs, LANES), F32))
        else:
            operands = [state["spread"]]
            in_specs = [full_spec(spread.shape)]
            outs = [half_out, half_out]
            scratch += weights
        result = pl.pallas_call(
            functools.partial(gate_kernel, len(parts) if first else 0, begin, columns, tail, window, len(after)),
            in_specs=[SCALARS] * 2 + [anywhere] * len(after) + [*in_specs, full_spec(gate_first.shape) if first else anywhere],
            out_specs=[full_spec(x.shape) for x in outs],
            scratch_shapes=scratch,
            out_shape=outs,
            compiler_params=params(room(total)),
            cost_estimate=pl.CostEstimate(flops=1, bytes_accessed=1, transcendentals=0),
            name=f"gate_up_{index}",
        )(offsets, order, *after, *operands, gate_first if first else gate_up)
        if first:
            state["resid"], state["spread"] = result[2:]
        state["after"] = [result[0]]
        return result[:2]

    def combine(index, bit, held, hold=None):
        aux_at = 2 * chunks[index][1] + tail[2] if index == 0 else None
        sums = sum_parts(
            *held, halves(held[0].shape[0]), aux_at, f"sum_{index}_{bit}", waits() if bit else state["after"], hold
        )
        kept, sent = sums[-2:]
        state["after"] = [kept]
        received = over_chips(sent, 1 << bit)
        flying.append(received)
        return [kept, received], sums[0]

    def activate(index, held):
        act, state["stats"] = activation(
            held,
            state.get("stats"),
            chunks[index][1],
            tail if index == 0 else None,
            float(features),
            f"activation_{index}",
            waits(),
        )
        state["after"] = [act]
        return act

    def spread_out(parts, fresh):
        more = {}
        for s in fresh:
            low = (s & -s).bit_length() - 1 if s else stages
            for bit in range(low):
                more[s | 1 << bit] = over_chips(parts[s], 1 << bit)
        flying.extend(more.values())
        parts.update(more)
        return list(more)

    def down(numbers, lists, after):
        first, last = numbers[0] == 0, numbers[-1] == len(chunks) - 1
        stacked = stack_parts(lists, after)
        others = [swap(x) for x in stacked]
        operands = [x for parts, other in zip(lists, others) for x in (*parts, other)]
        operands.append(down_held)
        in_specs = [full_spec(x.shape) for x in operands]
        if not first:
            operands.append(state["sum"])
            in_specs.append(full_spec(state["sum"].shape))
        sum_shape = jax.ShapeDtypeStruct((width, pairs), F32)
        scratch = [pltpu.VMEM((pairs, parts[0].shape[1]), BF16) for parts in lists]
        outs = [sum_shape]
        if last:
            operands += [place_table, state["resid"]]
            in_specs += [full_spec(place_table.shape), full_spec(state["resid"].shape)]
            outs = [jax.ShapeDtypeStruct((total, width), BF16)]
            scratch = [pltpu.VMEM(sum_shape.shape, F32)] + scratch
        result = pl.pallas_call(
            functools.partial(
                down_kernel,
                half,
                [chunks[k] for k in numbers],
                tail if first else None,
                min(-(-CAP * dp * fs // LANES) * LANES + LANES, pairs),
                first,
                last,
            ),
                    in_specs=[SCALARS] * 2 + in_specs,
            out_specs=[full_spec(x.shape) for x in outs],
            scratch_shapes=scratch,
            out_shape=outs,
            compiler_params=params(room(total)),
            cost_estimate=pl.CostEstimate(flops=1, bytes_accessed=1, transcendentals=0),
            name=f"down_{numbers[0]}",
        )(offsets, order, *operands)[0]
        state["sum"] = result
        return result

    stages = half.bit_length() - 1
    count = len(chunks)
    early = max(0, count - stages)
    held, gathered, fresh = {}, {}, {}
    flying = []
    for step in range(count + stages):
        sent = None
        if step < count:
            kept, sent = gate(step)
        if step == count - 1:
            down_held = stage_down(expert_down, state["after"][0])
        for k in range(count):
            if step - k == stages:
                if step == count - 1 + stages:
                    flight.append(down_held)
                gathered[k] = {0: activate(k, held[k])}
                if k < count - 1:
                    fresh[k] = spread_out(gathered[k], [0])
                else:
                    gathered[k].update({s: over_chips(gathered[k][0], s) for s in range(1, half)})
            elif 1 <= step - k < stages:
                held[k], through = combine(k, step - k, held[k], sent)
                sent = None if sent is None else through
        if step < count:
            held[step], _ = combine(step, 0, [kept, swap(sent)])
        for k in range(count - 1):
            if stages < step - k:
                fresh[k] = spread_out(gathered[k], fresh[k])
        flight.extend(flying)
        flying.clear()
    while any(fresh.values()):
        fresh = {k: spread_out(gathered[k], fresh[k]) for k in fresh}
    lists = [[gathered[k][s] for s in range(half)] for k in range(count)]
    last_after = state["after"]
    if early:
        last_after = [down(list(range(early)), lists[:early], state["after"])]
    result = down(list(range(early, count)), lists[early:], last_after)

    back = lax.all_to_all(result.reshape(dp * fs, req, width), ("dp", "fsdp"), 0, 0, tiled=True)
    back = back.reshape(dp, fs, req, width).astype(F32)
    return jnp.sum(back, axis=1).transpose(1, 0, 2).reshape(req, features).astype(BF16)


def solution(mesh):
    placed = (
        P(("dp", "fsdp"), None),
        P("dp", None, None, "fsdp"),
        P("dp", None, "fsdp"),
        P("fsdp", "dp"),
        P(),
        P(),
        P(),
        P(None, "dp", None, "fsdp"),
        P(None, "dp", "fsdp"),
        P(),
        P("dp", None),
        P("dp", None),
        P("dp"),
        P(),
        P(("dp", "fsdp"), None),
    )
    return jax.shard_map(
        local, mesh=mesh, in_specs=placed, out_specs=P(("dp", "fsdp"), None), check_vma=False
    )
```
